32 devices in a mesh: seq: 4 (over z), fsdp: 8 (over y, x, core).
Axes of the slice: x: 2, y: 2, z: 4, core: 2. Of those that a mesh axis runs over, the one named last changes fastest.
Arguments:
- tokens: bfloat16 [8, 1024, 1024], P('fsdp', 'seq'), may hold values from -6 to 6
- routes: int32 [8, 1024, 8], P('fsdp', 'seq'), may hold values from 0 to 31, all different within a row; in each aligned block of 256 rows (0 to 255, 256 to 511, ..., all dimensions but the last counted through in order) at most 96 rows name the same one
- cotangent: bfloat16 [8, 1024, 1024], P('fsdp', 'seq'), may hold values from -6 to 6
- norm_gains: float32 [2, 1024], P(None, 'fsdp'), may hold values from 0.5 to 1.5
- qkv_weight: float32 [1024, 2048], P('fsdp'), may hold values from -4 to 4
- out_weight: float32 [1024, 1024], P('fsdp'), may hold values from -3 to 3
- router_weight: float32 [1024, 32], P('fsdp'), may hold values from -1 to 1
- expert_up: float32 [32, 1024, 1024], P('seq', 'fsdp'), may hold values from -0.1875 to 0.1875
- expert_down: float32 [32, 512, 1024], P('seq', 'fsdp'), may hold values from -1 to 1
- mean_gains: float32 [2, 1024], P(None, 'fsdp')
- square_gains: float32 [2, 1024], P(None, 'fsdp'), as said below
- mean_qkv: float32 [1024, 2048], P('fsdp')
- square_qkv: float32 [1024, 2048], P('fsdp'), as said below
- mean_out: float32 [1024, 1024], P('fsdp')
- square_out: float32 [1024, 1024], P('fsdp'), as said below
- mean_router: float32 [1024, 32], P('fsdp')
- square_router: float32 [1024, 32], P('fsdp'), as said below
- mean_up: float32 [32, 1024, 1024], P('seq', 'fsdp')
- square_up: float32 [32, 1024, 1024], P('seq', 'fsdp'), as said below
- mean_down: float32 [32, 512, 1024], P('seq', 'fsdp')
- square_down: float32 [32, 512, 1024], P('seq', 'fsdp'), as said below
Outputs:
- output: bfloat16 [8, 1024, 1024], P('fsdp', 'seq')
- tokens_grad: float32 [8, 1024, 1024], P('fsdp', 'seq')
- grad_gains: float32 [2, 1024], P(None, 'fsdp')
- grad_qkv: float32 [1024, 2048], P('fsdp')
- grad_out: float32 [1024, 1024], P('fsdp')
- grad_router: float32 [1024, 32], P('fsdp')
- grad_up: float32 [32, 1024, 1024], P('seq', 'fsdp')
- grad_down: float32 [32, 512, 1024], P('seq', 'fsdp')
- fresh_gains: float32 [2, 1024], P(None, 'fsdp')
- fresh_qkv: float32 [1024, 2048], P('fsdp')
- fresh_out: float32 [1024, 1024], P('fsdp')
- fresh_router: float32 [1024, 32], P('fsdp')
- fresh_up: float32 [32, 1024, 1024], P('seq', 'fsdp')
- fresh_down: float32 [32, 512, 1024], P('seq', 'fsdp')
- momentum_gains: float32 [2, 1024], P(None, 'fsdp')
- momentum_qkv: float32 [1024, 2048], P('fsdp')
- momentum_out: float32 [1024, 1024], P('fsdp')
- momentum_router: float32 [1024, 32], P('fsdp')
- momentum_up: float32 [32, 1024, 1024], P('seq', 'fsdp')
- momentum_down: float32 [32, 512, 1024], P('seq', 'fsdp')
- variance_gains: float32 [2, 1024], P(None, 'fsdp')
- variance_qkv: float32 [1024, 2048], P('fsdp')
- variance_out: float32 [1024, 1024], P('fsdp')
- variance_router: float32 [1024, 32], P('fsdp')
- variance_up: float32 [32, 1024, 1024], P('seq', 'fsdp')
- variance_down: float32 [32, 512, 1024], P('seq', 'fsdp')
The draws below stay inside these ranges and needn't reach their ends.
Inputs may be any that keep to these rules, and one draw needn't show every extreme that they name: `routes`: each token names 8 different experts; among the 256 tokens of one device no expert is named more than 96 times. `square_gains`: positive. `square_qkv`: positive. `square_out`: positive. `square_router`: positive. `square_up`: positive. `square_down`: positive.
All inputs are finite; a program needn't handle non-finite values.
Results may differ from the reference program's by a relative error of at most 0.02.
Values may be sent and summed in bfloat16 or wider, within the bound.
No kernel may reach another device: no remote copies, remote signals or barrier semaphores. Data moves between devices by JAX's collectives and lax.ppermute only.
A program may use at most 256 MiB of HBM per device.

```python
import math
import jax
import jax.numpy as jnp
import numpy as np
from jax import lax

MODEL_WIDTH = 1024
QUERY_HEADS = 16
KEY_VALUE_HEADS = 8
HEAD_SIZE = 64
EXPERTS = 32
FF = 512
TOP = 8
TOK_DEV = 256
STEP = 3
SEQS = 8
SEQUENCE_TOKENS = 1024
QKVW = 2048
CAP = 96


def gradient_size(which):
    token_total = SEQS * SEQUENCE_TOKENS
    expert_pairs = token_total * TOP / EXPERTS
    hidden_grad = math.sqrt(MODEL_WIDTH) * (0.22 / TOP) * 4.0 / math.sqrt(FF)
    if which == 0:
        return math.sqrt(token_total)
    if which == 1:
        return 0.05 * math.sqrt(token_total * MODEL_WIDTH)
    if which == 2:
        return 0.09 * math.sqrt(token_total)
    if which == 3:
        return 0.44 * math.sqrt(MODEL_WIDTH) / TOP * math.sqrt(expert_pairs)
    if which == 4:
        return 0.6 * hidden_grad * math.sqrt(expert_pairs)
    return 0.11 * math.sqrt(expert_pairs) / TOP


def first_moment(key, shape, which):
    noise = jnp.clip(jax.random.normal(key, shape, jnp.float32), -4.0, 4.0)
    return noise * (0.15 * gradient_size(which))


def second_moment(key, shape, which):
    size = gradient_size(which)
    factor = jnp.exp(jax.random.uniform(key, shape, jnp.float32, math.log(0.5), math.log(8.0)))
    return factor * (0.0526 * size * size)


def draw_qkv_weight(key, part):
    key = jax.random.fold_in(key, 11)
    column_list = (QUERY_HEADS + 2 * KEY_VALUE_HEADS) * HEAD_SIZE
    sampled_values = jnp.clip(jax.random.normal(key, (MODEL_WIDTH, column_list), jnp.float32), -6.0, 6.0) / math.sqrt(MODEL_WIDTH)
    score_gain = math.sqrt(1.5 / (0.015625 * math.sqrt(HEAD_SIZE)))
    query_factor = jnp.full((QUERY_HEADS * HEAD_SIZE,), score_gain, jnp.float32)
    pair_factor = jnp.concatenate([jnp.full((HEAD_SIZE,), score_gain, jnp.float32), jnp.ones((HEAD_SIZE,), jnp.float32)])
    column_factor = jnp.concatenate([query_factor, jnp.tile(pair_factor, KEY_VALUE_HEADS)])
    return sampled_values * column_factor[None, :]


def draw_router_weight(key, part):
    noise = jnp.clip(jax.random.normal(jax.random.fold_in(key, 23), (MODEL_WIDTH, EXPERTS), jnp.float32), -6.0, 6.0)
    return noise * (0.5 / math.sqrt(MODEL_WIDTH))


def draw_mean_gains(key, part):
    return first_moment(jax.random.fold_in(key, 31), (2, MODEL_WIDTH), 0)


def draw_square_gains(key, part):
    return second_moment(jax.random.fold_in(key, 32), (2, MODEL_WIDTH), 0)


def draw_mean_qkv(key, part):
    return first_moment(jax.random.fold_in(key, 33), (MODEL_WIDTH, (QUERY_HEADS + 2 * KEY_VALUE_HEADS) * HEAD_SIZE), 1)


def draw_square_qkv(key, part):
    return second_moment(jax.random.fold_in(key, 34), (MODEL_WIDTH, (QUERY_HEADS + 2 * KEY_VALUE_HEADS) * HEAD_SIZE), 1)


def draw_mean_out(key, part):
    return first_moment(jax.random.fold_in(key, 35), (QUERY_HEADS * HEAD_SIZE, MODEL_WIDTH), 2)


def draw_square_out(key, part):
    return second_moment(jax.random.fold_in(key, 36), (QUERY_HEADS * HEAD_SIZE, MODEL_WIDTH), 2)


def draw_mean_router(key, part):
    return first_moment(jax.random.fold_in(key, 37), (MODEL_WIDTH, EXPERTS), 3)


def draw_square_router(key, part):
    return second_moment(jax.random.fold_in(key, 38), (MODEL_WIDTH, EXPERTS), 3)


def draw_mean_up(key, part):
    return first_moment(jax.random.fold_in(key, 39), (EXPERTS, MODEL_WIDTH, 2 * FF), 4)


def draw_square_up(key, part):
    return second_moment(jax.random.fold_in(key, 40), (EXPERTS, MODEL_WIDTH, 2 * FF), 4)


def draw_mean_down(key, part):
    return first_moment(jax.random.fold_in(key, 41), (EXPERTS, FF, MODEL_WIDTH), 5)


def draw_square_down(key, part):
    return second_moment(jax.random.fold_in(key, 42), (EXPERTS, FF, MODEL_WIDTH), 5)


def block_levels(key, extent, pieces, smallest, top_value):
    def one(dim, shards_of):
        steps = jax.random.uniform(jax.random.fold_in(jax.random.fold_in(key, 6), dim), (shards_of,), jnp.float32, smallest / len(pieces), top_value / len(pieces))
        return jnp.repeat(jnp.exp(steps), extent[dim] // shards_of).reshape((-1,) + (1,) * (len(extent) - dim - 1))

    gain = one(*pieces[0])
    for cut in pieces[1:]:
        gain = gain * one(*cut)
    return gain


def routed_block(stream_key, own, number, rows, amount, top, most, skew):
    order = jax.random.permutation(stream_key, amount)
    heavy_load, usual = portions_of(amount, rows * top, most, skew, True), portions_of(amount, rows * top, most, skew, False)
    places = jnp.arange(amount)

    def named(sizes, rotation):
        used = int((sizes > 0).sum())
        fixed = max(1, used // 4)
        shifted = fixed + (places - fixed + rotation * (used - fixed)) % max(1, amount - fixed)
        return jnp.zeros((amount,), jnp.int32).at[order[jnp.where(places < fixed, places, shifted)]].set(jnp.asarray(sizes, jnp.int32))

    sizes = jnp.where(number % 4 == 0, named(heavy_load, number // 4), named(usual, number - number // 4 - 1))
    mixed = jax.random.permutation(jax.random.fold_in(own, 3), amount)
    source_of, taker = mixed[0:amount // 2 * 2:2], mixed[1:amount // 2 * 2:2]
    room = jnp.minimum(sizes[source_of] - 1, most - sizes[taker]) // 2
    room = jnp.where((source_of == order[0]) | (taker == order[0]) | (sizes[taker] == 0), 0, jnp.maximum(room, 0))
    shifted = jax.random.randint(jax.random.fold_in(own, 4), (amount // 2,), 0, 1 << 20) % (room + 1)
    sizes = sizes.at[source_of].add(-shifted).at[taker].add(shifted)
    items = jnp.searchsorted(jnp.cumsum(sizes), jnp.arange(rows * top), side="right").astype(jnp.int32)
    listing = items.reshape(top, rows).T
    listing = listing[jax.random.permutation(jax.random.fold_in(own, 1), rows)]
    rotation = jax.random.randint(jax.random.fold_in(own, 2), (rows, 1), 0, top)
    return jnp.take_along_axis(listing, (jnp.arange(top)[None, :] + rotation) % top, axis=1)


def portions_of(count, total, reach, lean, full):
    portions = [(1 << 20) // math.isqrt(rank ** lean) + 1 for rank in range(1, count + 1)]
    largest = reach if full else min(reach, max(-(-total // count), total * portions[0] // sum(portions)))
    least = 1 if total - largest >= count - 1 else 0
    counts, rest = [largest] + [least] * (count - 1), total - largest - least * (count - 1)
    while rest > 0:
        candidates = [i for i in range(1, count) if counts[i] < largest] or [i for i in range(1, count) if counts[i] < reach]
        whole, left = sum([portions[i] for i in candidates]), rest
        for i in candidates:
            addition = min(reach - counts[i], max(1, left * portions[i] // whole), rest)
            counts[i] = counts[i] + addition
            rest = rest - addition
    return np.array(counts)


def centred(own_key, extent, spread, reach, cuts=(), kind=jnp.bfloat16):
    values = jax.random.normal(own_key, extent, jnp.float32) * spread
    if len(cuts) > 0:
        values = block_levels(own_key, extent, cuts, -0.22, 0.18) * values
    return jnp.clip(values, min=-reach, max=reach).astype(kind)


def setup_inputs(seed: int = 0) -> dict:
    splits = jax.random.split(jax.random.key(seed), 22)
    tokens = centred(splits[0], (SEQS, SEQUENCE_TOKENS, MODEL_WIDTH), 1.0, 6.0, ((0, 8), (1, 4)))
    routes_keys = jax.random.split(jax.random.fold_in(splits[1], 1), SEQS * SEQUENCE_TOKENS // TOK_DEV)
    routes_turns = jax.random.permutation(jax.random.fold_in(splits[1], 3), SEQS * SEQUENCE_TOKENS // TOK_DEV)
    routes = jax.vmap(lambda own, number: routed_block(jax.random.fold_in(splits[1], 2), own, number, TOK_DEV, EXPERTS, TOP, CAP, 1))(routes_keys, routes_turns).reshape((SEQS, SEQUENCE_TOKENS, TOP))
    cotangent = centred(splits[2], (SEQS, SEQUENCE_TOKENS, MODEL_WIDTH), 1.0, 6.0, ((0, 8), (1, 4)))
    norm_gains = jnp.clip(1.0 + 0.1 * jax.random.normal(splits[3], (2, MODEL_WIDTH), jnp.float32), 0.5, 1.5)
    qkv_weight = draw_qkv_weight(jax.random.fold_in(splits[21], 71), 0)
    out_weight = centred(splits[5], (QUERY_HEADS * HEAD_SIZE, MODEL_WIDTH), 0.5, 3.0, ((0, 8),), jnp.float32)
    router_weight = draw_router_weight(jax.random.fold_in(splits[21], 71), 0)
    expert_up = centred(splits[7], (EXPERTS, MODEL_WIDTH, 2 * FF), MODEL_WIDTH ** -0.5, 0.1875, ((0, 4), (1, 8)), jnp.float32)
    expert_down = centred(splits[8], (EXPERTS, FF, MODEL_WIDTH), (FF // 16) ** -0.5, 1.0, ((0, 4), (1, 8)), jnp.float32)
    mean_gains = draw_mean_gains(jax.random.fold_in(splits[21], 71), 0)
    square_gains = draw_square_gains(jax.random.fold_in(splits[21], 71), 0)
    mean_qkv = draw_mean_qkv(jax.random.fold_in(splits[21], 71), 0)
    square_qkv = draw_square_qkv(jax.random.fold_in(splits[21], 71), 0)
    mean_out = draw_mean_out(jax.random.fold_in(splits[21], 71), 0)
    square_out = draw_square_out(jax.random.fold_in(splits[21], 71), 0)
    mean_router = draw_mean_router(jax.random.fold_in(splits[21], 71), 0)
    square_router = draw_square_router(jax.random.fold_in(splits[21], 71), 0)
    mean_up = draw_mean_up(jax.random.fold_in(splits[21], 71), 0)
    square_up = draw_square_up(jax.random.fold_in(splits[21], 71), 0)
    mean_down = draw_mean_down(jax.random.fold_in(splits[21], 71), 0)
    square_down = draw_square_down(jax.random.fold_in(splits[21], 71), 0)
    return {"tokens": tokens, "routes": routes, "cotangent": cotangent, "norm_gains": norm_gains, "qkv_weight": qkv_weight, "out_weight": out_weight, "router_weight": router_weight, "expert_up": expert_up, "expert_down": expert_down, "mean_gains": mean_gains, "square_gains": square_gains, "mean_qkv": mean_qkv, "square_qkv": square_qkv, "mean_out": mean_out, "square_out": square_out, "mean_router": mean_router, "square_router": square_router, "mean_up": mean_up, "square_up": square_up, "mean_down": mean_down, "square_down": square_down}


epsilon = 1e-06
res_scale = 0.22
att_scale = 0.015625
beta_one = 0.9
beta_two = 0.95
adam_eps = 1e-08
weight_decay = 0.1
learn_rates = (0.4, 0.04, 0.2, 0.01, 0.01, 0.05)

def rounded(values):
    return lax.optimization_barrier(values.astype(jnp.bfloat16)).astype(jnp.float32)

def rope_tables(length_total, offset):
    position = (offset + jnp.arange(length_total)).astype(jnp.float32)
    frequency = 10000.0 ** (-(jnp.arange(HEAD_SIZE // 2).astype(jnp.float32) * 2.0 / HEAD_SIZE))
    angles = position[:, None] * frequency[None, :]
    angles = jnp.concatenate([angles, angles], axis=1)
    return (jnp.cos(angles)[:, None, :], jnp.sin(angles)[:, None, :])

def rotate(values, cosine_table, sine_table):
    middle = values.shape[-1] // 2
    turned = jnp.concatenate([-values[..., middle:], values[..., :middle]], axis=-1)
    return values * cosine_table + turned * sine_table

def rotate_back(gradient, cosine_table, sine_table):
    middle = gradient.shape[-1] // 2
    scaled = gradient * sine_table
    turned = jnp.concatenate([scaled[..., middle:], -scaled[..., :middle]], axis=-1)
    return gradient * cosine_table + turned

def split_heads(projected_input, cosine_table, sine_table):
    length_total = projected_input.shape[0]
    query_rows_all = rotate(projected_input[:, :QUERY_HEADS * HEAD_SIZE].reshape(length_total, QUERY_HEADS, HEAD_SIZE), cosine_table, sine_table)
    paired_values = projected_input[:, QUERY_HEADS * HEAD_SIZE:].reshape(length_total, KEY_VALUE_HEADS, 2, HEAD_SIZE)
    rotated_keys = rotate(paired_values[:, :, 0], cosine_table, sine_table)
    paired_values = jnp.stack([rotated_keys, paired_values[:, :, 1]], axis=2)
    return (query_rows_all.reshape(length_total, QUERY_HEADS * HEAD_SIZE), paired_values.reshape(length_total, KEY_VALUE_HEADS * 2 * HEAD_SIZE))

def norm_forward(values, gain_row):
    scale_inv = lax.rsqrt(lax.optimization_barrier(jnp.mean(values * values, axis=-1, keepdims=True)) + epsilon)
    return (values * scale_inv * gain_row, scale_inv)

def norm_backward(upstream, values, scale_inv, gain_row):
    normed = values * scale_inv
    scaled = upstream * gain_row
    inner_mean = lax.optimization_barrier(jnp.mean(scaled * normed, axis=-1, keepdims=True))
    return (scale_inv * (scaled - normed * inner_mean), lax.optimization_barrier(jnp.sum(upstream * normed, axis=0)))

def masked_scores(query_rows_all, key_rows):
    length_total = query_rows_all.shape[0]
    scores = jnp.einsum('qgd,kd->gqk', query_rows_all.astype(jnp.float32), key_rows.astype(jnp.float32)) * att_scale
    causal = jnp.arange(length_total)[:, None] >= jnp.arange(length_total)[None, :]
    return jnp.where(causal[None], scores, -jnp.inf)

def head_forward(query_rows_all, key_rows, value_rows):
    scores = masked_scores(query_rows_all, key_rows)
    top_score = lax.optimization_barrier(jnp.max(scores, axis=-1, keepdims=True))
    logsum = top_score + jnp.log(lax.optimization_barrier(jnp.sum(jnp.exp(scores - top_score), axis=-1, keepdims=True)))
    weights = jnp.exp(scores - logsum)
    outputs = jnp.einsum('gqk,kd->qgd', rounded(weights), value_rows.astype(jnp.float32))
    return (outputs.astype(jnp.bfloat16), logsum[..., 0])

def head_backward(query_rows_all, key_rows, value_rows, outputs, logsum, upstream):
    scores = masked_scores(query_rows_all, key_rows)
    weights = jnp.exp(scores - logsum[..., None])
    upstream_f = upstream.astype(jnp.float32)
    prob_grad = jnp.einsum('qgd,kd->gqk', upstream_f, value_rows.astype(jnp.float32))
    row_inner = lax.optimization_barrier(jnp.sum(upstream_f * outputs.astype(jnp.float32), axis=-1)).T
    score_grad = rounded(weights * (prob_grad - row_inner[..., None]))
    query_grad = att_scale * jnp.einsum('gqk,kd->qgd', score_grad, key_rows.astype(jnp.float32))
    key_grad = att_scale * jnp.einsum('gqk,qgd->kd', score_grad, query_rows_all.astype(jnp.float32))
    value_grad = jnp.einsum('gqk,qgd->kd', rounded(weights), upstream_f)
    return (query_grad.astype(jnp.bfloat16), key_grad.astype(jnp.bfloat16), value_grad.astype(jnp.bfloat16))

def adam_update(weight, gradient, first, second, rate):
    first_new = beta_one * first + (1.0 - beta_one) * gradient
    second_new = beta_two * second + (1.0 - beta_two) * gradient * gradient
    first_hat = first_new / (1.0 - beta_one ** STEP)
    second_hat = second_new / (1.0 - beta_two ** STEP)
    fresh = weight - rate * (first_hat / (jnp.sqrt(second_hat) + adam_eps) + weight_decay * weight)
    return (fresh, first_new, second_new)

def reference(tokens, routes, cotangent, norm_gains, qkv_weight, out_weight, router_weight, expert_up, expert_down, mean_gains, square_gains, mean_qkv, square_qkv, mean_out, square_out, mean_router, square_router, mean_up, square_up, mean_down, square_down):
    gain_vals = rounded(norm_gains)
    qkv_half = qkv_weight.astype(jnp.bfloat16)
    out_half = out_weight.astype(jnp.bfloat16)
    router_half = router_weight.astype(jnp.bfloat16)
    up_half = expert_up.astype(jnp.bfloat16)
    down_half = expert_down.astype(jnp.bfloat16)
    head_grouping = QUERY_HEADS // KEY_VALUE_HEADS
    cosine_table, sine_table = rope_tables(SEQUENCE_TOKENS, 0)

    def heads_of(query_rows_all, paired_values):
        query_per_head = query_rows_all.reshape(SEQUENCE_TOKENS, KEY_VALUE_HEADS, head_grouping, HEAD_SIZE).transpose(1, 0, 2, 3)
        paired_heads = paired_values.reshape(SEQUENCE_TOKENS, KEY_VALUE_HEADS, 2, HEAD_SIZE).transpose(1, 2, 0, 3)
        return (query_per_head, paired_heads[:, 0], paired_heads[:, 1])

    def attention_inputs(seq_tokens):
        source = seq_tokens.astype(jnp.float32)
        normed_one, inv_one = norm_forward(source, gain_vals[0])
        normed_first = normed_one.astype(jnp.bfloat16)
        projected_input = jnp.dot(normed_first, qkv_half, preferred_element_type=jnp.float32)
        query_rows_all, paired_values = split_heads(projected_input, cosine_table, sine_table)
        return (source, inv_one, normed_first, heads_of(query_rows_all.astype(jnp.bfloat16), paired_values.astype(jnp.bfloat16)))

    def forward_sequence(seq_tokens):
        source, inv_one, normed_first, heads = attention_inputs(seq_tokens)
        outputs, logsum = lax.map(lambda inputs: head_forward(inputs[0], inputs[1], inputs[2]), heads)
        attended = outputs.transpose(1, 0, 2, 3).reshape(SEQUENCE_TOKENS, QUERY_HEADS * HEAD_SIZE)
        resid = source + res_scale * jnp.dot(attended, out_half, preferred_element_type=jnp.float32)
        normed_two, inv_two = norm_forward(resid, gain_vals[1])
        normed_second = normed_two.astype(jnp.bfloat16)
        logits = jnp.dot(normed_second, router_half, preferred_element_type=jnp.float32)
        return (resid, normed_second, logits, attended, logsum)
    resid, normed_second, logits, attended, logsums = lax.map(forward_sequence, tokens)
    all_rows = SEQS * SEQUENCE_TOKENS
    flat_normed = normed_second.reshape(all_rows, MODEL_WIDTH)
    flat_logits = logits.reshape(all_rows, EXPERTS)
    flat_routes = routes.reshape(all_rows, TOP).astype(jnp.int32)
    expert_ids = jnp.arange(EXPERTS, dtype=jnp.int32)
    choose = (flat_routes[:, :, None] == expert_ids[None, None, :]).astype(jnp.float32)
    picked = lax.optimization_barrier(jnp.sum(choose * flat_logits[:, None, :], axis=-1))
    gate_probs = jax.nn.softmax(picked, axis=-1)
    block_count = all_rows // TOK_DEV
    block_routes = flat_routes.reshape(block_count, TOK_DEV * TOP)
    expert_hits = (block_routes[:, :, None] == expert_ids[None, None, :]).astype(jnp.int32)
    before = (jnp.cumsum(expert_hits, axis=1) - expert_hits).astype(jnp.int32)
    slot_rank = lax.optimization_barrier(jnp.sum(before * expert_hits, axis=-1)).astype(jnp.int32)
    block_base = (jnp.arange(block_count, dtype=jnp.int32) * CAP)[:, None]
    pair_ids = jnp.arange(all_rows * TOP, dtype=jnp.int32).reshape(block_count, TOK_DEV * TOP)
    slot_owner = jnp.full((EXPERTS, block_count * CAP), all_rows * TOP, jnp.int32)
    slot_owner = slot_owner.at[block_routes, (block_base + slot_rank).astype(jnp.int32)].set(pair_ids)
    padded_normed = jnp.concatenate([flat_normed, jnp.zeros((1, MODEL_WIDTH), jnp.bfloat16)], axis=0)
    upstream_all = cotangent.reshape(all_rows, MODEL_WIDTH).astype(jnp.float32)
    branch_pad = jnp.concatenate([res_scale * upstream_all, jnp.zeros((1, MODEL_WIDTH), jnp.float32)], axis=0)
    gate_pad = jnp.concatenate([gate_probs.reshape(-1), jnp.zeros((1,), jnp.float32)])

    def expert_step(running, inputs):
        mixture, normed_grad, gate_grad = running
        owner_pairs, up_one, down_one = inputs
        owner_rows = (owner_pairs // TOP).astype(jnp.int32)
        arrived = padded_normed[owner_rows]
        upgate = jnp.dot(arrived, up_one, preferred_element_type=jnp.float32)
        gate_part = upgate[:, :FF]
        up_part = upgate[:, FF:]
        sigmoid_gate = jax.nn.sigmoid(gate_part)
        swish_gate = gate_part * sigmoid_gate
        hidden = (swish_gate * up_part).astype(jnp.bfloat16)
        produced = rounded(jnp.dot(hidden, down_one, preferred_element_type=jnp.float32))
        gate_rows = gate_pad[owner_pairs]
        branch_rows = branch_pad[owner_rows]
        mixture = mixture.at[owner_rows].add(gate_rows[:, None] * produced, mode='drop')
        gate_grad = gate_grad.at[owner_pairs].set(lax.optimization_barrier(jnp.sum(branch_rows * produced, axis=-1)), mode='drop')
        incoming = (gate_rows[:, None] * branch_rows).astype(jnp.bfloat16)
        hidden_grad = jnp.dot(incoming, down_one.T, preferred_element_type=jnp.float32)
        grad_down_one = jnp.dot(hidden.T, incoming, preferred_element_type=jnp.float32)
        swish_grad = sigmoid_gate * (1.0 + gate_part * (1.0 - sigmoid_gate))
        upgate_grad = jnp.concatenate([hidden_grad * up_part * swish_grad, hidden_grad * swish_gate], axis=1).astype(jnp.bfloat16)
        grad_up_one = jnp.dot(arrived.T, upgate_grad, preferred_element_type=jnp.float32)
        slot_input = rounded(jnp.dot(upgate_grad, up_one.T, preferred_element_type=jnp.float32))
        normed_grad = normed_grad.at[owner_rows].add(slot_input, mode='drop')
        return ((mixture, normed_grad, gate_grad), (grad_up_one, grad_down_one))
    start_state = (jnp.zeros((all_rows, MODEL_WIDTH), jnp.float32), jnp.zeros((all_rows, MODEL_WIDTH), jnp.float32), jnp.zeros((all_rows * TOP,), jnp.float32))
    (mixture, normed_grad, gate_grad), (grad_up, grad_down) = lax.scan(expert_step, start_state, (slot_owner, up_half, down_half))
    gate_grad = gate_grad.reshape(all_rows, TOP)
    picked_grad = gate_probs * (gate_grad - lax.optimization_barrier(jnp.sum(gate_probs * gate_grad, axis=-1, keepdims=True)))
    logit_grad = lax.optimization_barrier(jnp.sum(picked_grad[:, :, None] * choose, axis=1)).astype(jnp.bfloat16)
    grad_router = jnp.dot(flat_normed.T, logit_grad, preferred_element_type=jnp.float32)
    normed_grad = normed_grad + jnp.dot(logit_grad, router_half.T, preferred_element_type=jnp.float32)
    output = (resid.reshape(all_rows, MODEL_WIDTH) + res_scale * mixture).astype(jnp.bfloat16).reshape(SEQS, SEQUENCE_TOKENS, MODEL_WIDTH)

    def backward_sequence(running, inputs):
        grad_gains, grad_qkv, grad_out = running
        seq_tokens, seq_resid, seq_normed_grad, seq_cot, sequence_attended, seq_logsum = inputs
        source, inv_one, normed_first, heads = attention_inputs(seq_tokens)
        normed_two, inv_two = norm_forward(seq_resid, gain_vals[1])
        part_two, gain_grad_two = norm_backward(seq_normed_grad, seq_resid, inv_two, gain_vals[1])
        resid_grad = seq_cot.astype(jnp.float32) + part_two
        attn_grad = (res_scale * resid_grad).astype(jnp.bfloat16)
        grad_out = grad_out + jnp.dot(sequence_attended.T, attn_grad, preferred_element_type=jnp.float32)
        returned_gradient = jnp.dot(attn_grad, out_half.T, preferred_element_type=jnp.float32).astype(jnp.bfloat16)
        head_output = sequence_attended.reshape(SEQUENCE_TOKENS, KEY_VALUE_HEADS, head_grouping, HEAD_SIZE).transpose(1, 0, 2, 3)
        head_upward = returned_gradient.reshape(SEQUENCE_TOKENS, KEY_VALUE_HEADS, head_grouping, HEAD_SIZE).transpose(1, 0, 2, 3)
        query_grad, key_grad, value_grad = lax.map(lambda inputs: head_backward(inputs[0], inputs[1], inputs[2], inputs[3], inputs[4], inputs[5]), (heads[0], heads[1], heads[2], head_output, seq_logsum, head_upward))
        query_tok = rotate_back(query_grad.transpose(1, 0, 2, 3).reshape(SEQUENCE_TOKENS, QUERY_HEADS, HEAD_SIZE).astype(jnp.float32), cosine_table, sine_table)
        key_token = rotate_back(key_grad.transpose(1, 0, 2).astype(jnp.float32), cosine_table, sine_table)
        value_token = value_grad.transpose(1, 0, 2).astype(jnp.float32)
        key_value_token = jnp.stack([key_token, value_token], axis=2).reshape(SEQUENCE_TOKENS, KEY_VALUE_HEADS * 2 * HEAD_SIZE)
        projected_grad = jnp.concatenate([query_tok.reshape(SEQUENCE_TOKENS, QUERY_HEADS * HEAD_SIZE), key_value_token], axis=1).astype(jnp.bfloat16)
        grad_qkv = grad_qkv + jnp.dot(normed_first.T, projected_grad, preferred_element_type=jnp.float32)
        normed_one_grad = jnp.dot(projected_grad, qkv_half.T, preferred_element_type=jnp.float32)
        part_one, gain_grad_one = norm_backward(normed_one_grad, source, inv_one, gain_vals[0])
        grad_gains = grad_gains + jnp.stack([gain_grad_one, gain_grad_two])
        return ((grad_gains, grad_qkv, grad_out), resid_grad + part_one)
    zero_grads = (jnp.zeros((2, MODEL_WIDTH), jnp.float32), jnp.zeros((MODEL_WIDTH, QKVW), jnp.float32), jnp.zeros((QUERY_HEADS * HEAD_SIZE, MODEL_WIDTH), jnp.float32))
    (grad_gains, grad_qkv, grad_out), tokens_grad = lax.scan(backward_sequence, zero_grads, (tokens, resid, normed_grad.reshape(SEQS, SEQUENCE_TOKENS, MODEL_WIDTH), cotangent, attended, logsums))
    fresh_gains, momentum_gains, variance_gains = adam_update(norm_gains, grad_gains, mean_gains, square_gains, learn_rates[0])
    fresh_qkv, momentum_qkv, variance_qkv = adam_update(qkv_weight, grad_qkv, mean_qkv, square_qkv, learn_rates[1])
    fresh_out, momentum_out, variance_out = adam_update(out_weight, grad_out, mean_out, square_out, learn_rates[2])
    fresh_router, momentum_router, variance_router = adam_update(router_weight, grad_router, mean_router, square_router, learn_rates[3])
    fresh_up, momentum_up, variance_up = adam_update(expert_up, grad_up, mean_up, square_up, learn_rates[4])
    fresh_down, momentum_down, variance_down = adam_update(expert_down, grad_down, mean_down, square_down, learn_rates[5])
    return (output, tokens_grad, grad_gains, grad_qkv, grad_out, grad_router, grad_up, grad_down, fresh_gains, fresh_qkv, fresh_out, fresh_router, fresh_up, fresh_down, momentum_gains, momentum_qkv, momentum_out, momentum_router, momentum_up, momentum_down, variance_gains, variance_qkv, variance_out, variance_router, variance_up, variance_down)
```

```python
import functools

import jax
import jax.numpy as jnp
from jax import lax
from jax.experimental import pallas as pl
from jax.experimental.pallas import tpu as pltpu
from jax.sharding import PartitionSpec as P

MODEL_WIDTH = 1024
QUERY_HEADS = 16
KEY_VALUE_HEADS = 8
HEAD_SIZE = 64
EXPERTS = 32
FF = 512
TOP = 8
STEP = 3
CAP = 96
LANES = 128
TILE = 256
CHUNKS = 2

epsilon = 1e-06
res_scale = 0.22
att_scale = 0.015625
beta_one = 0.9
beta_two = 0.95
adam_eps = 1e-08
weight_decay = 0.1
learn_rates = (0.4, 0.04, 0.2, 0.01, 0.01, 0.05)

bf16 = jnp.bfloat16
f32 = jnp.float32
WIDE = MODEL_WIDTH + LANES


def adam_update(weight, gradient, first, second, rate):
    first_new = beta_one * first + (1.0 - beta_one) * gradient
    second_new = beta_two * second + (1.0 - beta_two) * gradient * gradient
    first_hat = first_new / (1.0 - beta_one**STEP)
    second_hat = second_new / (1.0 - beta_two**STEP)
    fresh = weight - rate * (first_hat / (jnp.sqrt(second_hat) + adam_eps) + weight_decay * weight)
    return (fresh, first_new, second_new)


def dot_nn(a, b):
    return lax.dot_general(a, b, (((1,), (0,)), ((), ())), preferred_element_type=f32)


def dot_nt(a, b):
    return lax.dot_general(a, b, (((1,), (1,)), ((), ())), preferred_element_type=f32)


def dot_tn(a, b):
    return lax.dot_general(a, b, (((0,), (0,)), ((), ())), preferred_element_type=f32)


def lanes_of(shape):
    return lax.broadcasted_iota(jnp.int32, shape, len(shape) - 1)


def aligned(index, size):
    return pl.ds(pl.multiple_of(index, size), size)


def kernel_call(body, outs, ins, scalars, scratch=(), grid=None, in_specs=None, out_specs=None, flops=0, limit=48):
    in_specs = in_specs or [pl.BlockSpec(memory_space=pltpu.VMEM)] * len(ins)
    out_specs = out_specs or [pl.BlockSpec(memory_space=pltpu.VMEM)] * len(outs)
    moved = sum(a.size * a.dtype.itemsize for a in list(ins) + list(outs))
    return pl.pallas_call(
        body,
        out_shape=outs,
        grid_spec=pltpu.PrefetchScalarGridSpec(
            num_scalar_prefetch=1,
            grid=grid or (1,),
            in_specs=in_specs,
            out_specs=out_specs,
            scratch_shapes=list(scratch),
        ),
        compiler_params=pltpu.CompilerParams(vmem_limit_bytes=limit * 1024 * 1024),
        cost_estimate=pl.CostEstimate(flops=flops, bytes_accessed=moved, transcendentals=0),
    )(scalars, *ins)


def shape_of(shape, kind=bf16):
    return jax.ShapeDtypeStruct(shape, kind)


def xor_permute(value, axis, mask):
    return lax.ppermute(value, axis, [(i, i ^ mask) for i in range(lax.axis_size(axis))])


def shift_permute(value, axis, step):
    size = lax.axis_size(axis)
    return lax.ppermute(value, axis, [(i, (i + step) % size) for i in range(size)])


def gather_shards(value):
    count = lax.axis_size("fsdp")
    if count != 8:
        whole = lax.all_gather(value, "fsdp", axis=0)
        order = lax.axis_index("fsdp") ^ jnp.arange(count)
        whole = jnp.take(whole, order, axis=0)
        return [(r, 0, whole[r]) for r in range(count)]
    half = value.shape[-2] // 2
    over_x = xor_permute(value, "fsdp", 2)
    over_y = xor_permute(value, "fsdp", 4)
    far_a = xor_permute(over_x[..., :half, :], "fsdp", 4)
    far_b = xor_permute(over_y[..., half:, :], "fsdp", 2)
    pieces = [(0, 0, value), (2, 0, over_x), (4, 0, over_y), (6, 0, far_a), (6, half, far_b)]
    return pieces + [(r + 1, row, xor_permute(a, "fsdp", 1)) for r, row, a in pieces]


def scatter_sets(send, keep):
    count = lax.axis_size("fsdp")
    rows = keep.shape[-2]
    half = rows // 2
    if count != 8:
        both = jnp.stack([keep, send], axis=1).reshape((count,) + keep.shape[1:])
        both = jnp.take(both, lax.axis_index("fsdp") ^ jnp.arange(count), axis=0)
        total = lax.psum_scatter(both, "fsdp", scatter_dimension=0).astype(f32)
        return (total[..., :half, :], total[..., half:, :])
    got = xor_permute(send, "fsdp", 1)

    def pair(i, part):
        piece = slice(0, half) if part == 0 else slice(half, rows)
        return keep[i, ..., piece, :].astype(f32) + got[i, ..., piece, :].astype(f32)

    over_x = xor_permute(jnp.stack([pair(3, 0), pair(1, 0)]).astype(bf16), "fsdp", 2)
    over_y = xor_permute(jnp.stack([pair(3, 1), pair(2, 1)]).astype(bf16), "fsdp", 4)
    then_x = xor_permute((pair(1, 1) + over_y[0].astype(f32)).astype(bf16), "fsdp", 2)
    then_y = xor_permute((pair(2, 0) + over_x[0].astype(f32)).astype(bf16), "fsdp", 4)
    first = pair(0, 0) + over_x[1].astype(f32) + then_y.astype(f32)
    second = pair(0, 1) + over_y[1].astype(f32) + then_x.astype(f32)
    return (first, second)


def ring_gather(block):
    count = lax.axis_size("seq")
    if count != 4:
        whole = lax.all_gather(block, "seq", axis=0)
        whole = jnp.take(whole, (lax.axis_index("seq") - jnp.arange(count)) % count, axis=0)
        return [(k, 0, whole[k]) for k in range(count)]
    half = block.shape[0] // 2
    below = shift_permute(block, "seq", 1)
    above = shift_permute(block, "seq", -1)
    far_a = shift_permute(below[:half], "seq", 1)
    far_b = shift_permute(above[half:], "seq", -1)
    return [(0, 0, block), (1, 0, below), (3, 0, above), (2, 0, far_a), (2, half, far_b)]


def ring_shapes(count, rows, columns):
    if count != 4:
        return [shape_of((count, rows, columns))]
    half = rows // 2
    return [shape_of((r, columns)) for r in (rows, rows, rows, half, half)]


def ring_put(count, refs, k, rows, value):
    half = rows // 2
    width = value.shape[1]
    value = value.astype(bf16)
    if count != 4:
        refs[0][k, :, :width] = value
        return
    own, down, up, keep_down, keep_up = refs
    places = {
        0: ((own, 0), (own, half)),
        1: ((keep_down, 0), (down, half)),
        2: ((down, 0), (up, 0)),
        3: ((up, half), (keep_up, 0)),
    }
    for part, (ref, row) in enumerate(places[k]):
        ref[row : row + half, :width] = value[part * half : (part + 1) * half]


def ring_put_tail(count, refs, k, rows, value):
    half = rows // 2
    value = value.astype(bf16)
    if count != 4:
        refs[0][k, :, MODEL_WIDTH:] = value
        return
    own, down, up, keep_down, keep_up = refs
    places = {
        0: ((own, 0), (own, half)),
        1: ((keep_down, 0), (down, half)),
        2: ((down, 0), (up, 0)),
        3: ((up, half), (keep_up, 0)),
    }
    for part, (ref, row) in enumerate(places[k]):
        ref[row : row + half, MODEL_WIDTH:] = value[part * half : (part + 1) * half]


def ring_reduce(arrays):
    count = lax.axis_size("seq")
    if count != 4:
        whole = jnp.take(arrays[0], (lax.axis_index("seq") - jnp.arange(count)) % count, axis=0)
        return [lax.psum_scatter(whole, "seq", scatter_dimension=0)]
    own, down, up, keep_down, keep_up = arrays
    half = keep_down.shape[0]
    from_above = shift_permute(down, "seq", -1)
    from_below = shift_permute(up, "seq", 1)
    then_down = (keep_down.astype(f32) + from_above[:half].astype(f32)).astype(bf16)
    then_up = (keep_up.astype(f32) + from_below[:half].astype(f32)).astype(bf16)
    last_above = shift_permute(then_down, "seq", -1)
    last_below = shift_permute(then_up, "seq", 1)
    return [own, from_above, from_below, last_above, last_below]


def ring_total(refs):
    if len(refs) == 1:
        return refs[0][...].astype(f32)
    own, above, below, last_above, last_below = [r[...].astype(f32) for r in refs]
    half = own.shape[0] // 2
    first = own[:half] + below[half:] + last_above
    second = own[half:] + above[half:] + last_below
    return jnp.concatenate([first, second], axis=0)


def block_value(pieces, refs, k):
    found = sorted((row, ref) for (kk, row, _), ref in zip(pieces, refs) if kk == k)
    if len(found) == 1:
        return found[0][1][...]
    return jnp.concatenate([ref[...] for _, ref in found], axis=0)


def block_lanes(pieces, refs, k, lanes):
    found = [(row, ref) for (kk, row, _), ref in zip(pieces, refs) if kk == k]
    found.sort(key=lambda entry: entry[0])
    if len(found) == 1:
        return found[0][1][:, lanes]
    return jnp.concatenate([ref[:, lanes] for _, ref in found], axis=0)


def rotate_tile(tile, cosine, sine):
    first = lanes_of(tile.shape) % HEAD_SIZE < HEAD_SIZE // 2
    turned = jnp.where(first, pltpu.roll(tile, LANES - HEAD_SIZE // 2, 1), pltpu.roll(tile, HEAD_SIZE // 2, 1))
    return tile * cosine + turned * sine


def rotate_tile_back(tile, cosine, sine):
    return rotate_tile(tile, cosine, -sine)


def qkv_body(pieces, meta, x_ref, cos_ref, sin_ref, *refs):
    shards = refs[: len(pieces)]
    wq_ref, wkv_ref, wo_ref, extra_ref, normed_ref, q_ref, kv_ref, columns = refs[len(pieces) :]
    shard_rows = MODEL_WIDTH // max(r + 1 for r, _, _ in pieces)
    for (r, row, value), ref in zip(pieces, shards):
        rows = value.shape[0]
        place = pl.ds(pl.multiple_of(meta[r] * shard_rows + row, rows), rows)
        wq_ref[place, :] = ref[:, :MODEL_WIDTH]
        wkv_ref[place, :] = ref[:, MODEL_WIDTH : 2 * MODEL_WIDTH]
        wo_ref[place, :] = ref[:, 2 * MODEL_WIDTH : 3 * MODEL_WIDTH]
        columns[place, :] = ref[:, 3 * MODEL_WIDTH :].astype(f32)
    extra_ref[...] = columns[...].T
    source = x_ref[...].astype(f32)
    scale_inv = lax.rsqrt(jnp.mean(source * source, axis=-1, keepdims=True) + epsilon)
    normed = (source * scale_inv * extra_ref[EXPERTS : EXPERTS + 1, :]).astype(bf16)
    normed_ref[...] = normed
    cosine, sine = cos_ref[...], sin_ref[...]
    low = lanes_of(cosine.shape) < HEAD_SIZE
    for j in range(MODEL_WIDTH // TILE):
        block = dot_nn(normed, wq_ref[:, j * TILE : (j + 1) * TILE])
        for i in range(TILE // LANES):
            at = j * TILE + i * LANES
            tile = block[:, i * LANES : (i + 1) * LANES]
            q_ref[:, at : at + LANES] = rotate_tile(tile, cosine, sine).astype(bf16)
    for j in range(MODEL_WIDTH // TILE):
        block = dot_nn(normed, wkv_ref[:, j * TILE : (j + 1) * TILE])
        for i in range(TILE // LANES):
            at = j * TILE + i * LANES
            tile = block[:, i * LANES : (i + 1) * LANES]
            kv_ref[:, at : at + LANES] = jnp.where(low, rotate_tile(tile, cosine, sine), tile).astype(bf16)


def causal_scores(pair, keys, k):
    scores = dot_nt(pair, keys)
    if k == 0:
        rows = keys.shape[0]
        place = lax.broadcasted_iota(jnp.int32, scores.shape, 0) % rows
        scores = jnp.where(place >= lanes_of(scores.shape), scores, -jnp.inf)
    return scores


def query_pair(tile):
    low = lanes_of(tile.shape) < HEAD_SIZE
    tile = tile.astype(f32) * att_scale
    even = jnp.where(low, tile, 0.0)
    odd = jnp.where(low, pltpu.roll(tile, HEAD_SIZE, 1), 0.0)
    return jnp.concatenate([even, odd], axis=0).astype(bf16)


def attend_body(count, pieces, meta, q_ref, x_ref, wo_ref, extra_ref, *refs):
    blocks = refs[: len(pieces)]
    a_ref, lse_ref, h_ref, normed_ref = refs[len(pieces) :]
    rows = q_ref.shape[0]
    place = meta[0]

    def variant(seen):
        def group(g, carry):
            lanes = aligned(g * LANES, LANES)
            pair = query_pair(q_ref[:, lanes])
            keys = [block_lanes(pieces, blocks, k, lanes) for k in range(seen)]
            scores = [causal_scores(pair, keys[k], k) for k in range(seen)]
            top = functools.reduce(jnp.maximum, [jnp.max(s, axis=-1, keepdims=True) for s in scores])
            weights = [jnp.exp(s - top) for s in scores]
            total = functools.reduce(jnp.add, [jnp.sum(w, axis=-1, keepdims=True) for w in weights])
            summed = functools.reduce(jnp.add, [dot_nn(w.astype(bf16), t) for w, t in zip(weights, keys)])
            summed = summed * (1.0 / total)
            logsum = top + jnp.log(total)
            low = lanes_of((rows, LANES)) < HEAD_SIZE
            a_ref[:, lanes] = jnp.where(low, pltpu.roll(summed[:rows], HEAD_SIZE, 1), summed[rows:]).astype(bf16)
            lse_ref[:, lanes] = jnp.where(low, logsum[:rows], logsum[rows:])
            return carry

        lax.fori_loop(0, KEY_VALUE_HEADS, group, 0)

    for seen in range(1, count + 1):
        pl.when(place == seen - 1)(functools.partial(variant, seen))
    resid = x_ref[...].astype(f32) + res_scale * dot_nn(a_ref[...], wo_ref[...])
    h_ref[...] = resid
    scale_inv = lax.rsqrt(jnp.mean(resid * resid, axis=-1, keepdims=True) + epsilon)
    normed_ref[...] = (resid * scale_inv * extra_ref[EXPERTS + 1 : EXPERTS + 2, :]).astype(bf16)


def softmax_over(picked, logits, axis):
    top = jnp.max(jnp.where(picked, logits, -jnp.inf), axis=axis, keepdims=True)
    raised = jnp.where(picked, jnp.exp(jnp.minimum(logits - top, 0.0)), 0.0)
    return raised / jnp.sum(raised, axis=axis, keepdims=True)


def experts_body(count, shards, pieces, chunk, last, meta, routes_ref, c_ref, extra_ref, *refs):
    refs = list(refs)

    def take(number):
        taken = refs[:number]
        del refs[:number]
        return taken

    weights, blocks = take(len(pieces[0])), take(len(pieces[1]))
    if chunk > 0:
        (part_g, part_m) = take(2)
    send_ref, keep_ref = take(2)
    (mix_ref,) = take(1)
    ring_refs = take(len(ring_shapes(count, TILE, WIDE)) if last else 1)
    up_s, down_s, x_s, c_s, ge_s, a_s, gu_s, d_s, eg_s, gs_s, gup_s, gdown_s, gate_s, rank_s, gg_s = refs
    step = pl.program_id(0)
    local = EXPERTS // count
    members = local // CHUNKS
    up_rows, down_rows = MODEL_WIDTH // shards, FF // shards
    slots = count * CAP
    place = meta[shards]
    expert = place * local + chunk * members + step

    def absolute(k):
        return lax.rem(place - k + count, count)

    @pl.when(step == 0)
    def routing():
        router = extra_ref[:EXPERTS, :].astype(bf16)
        later = (
            lax.broadcasted_iota(jnp.int32, (TILE, TILE), 0) < lax.broadcasted_iota(jnp.int32, (TILE, TILE), 1)
        )
        later = jnp.where(later, 1.0, 0.0).astype(bf16)
        names = lax.broadcasted_iota(jnp.int32, (EXPERTS, TILE), 0)
        for k in range(count):
            named = routes_ref[absolute(k)]
            picked = names == named[0:1, :]
            for j in range(1, TOP):
                picked = jnp.logical_or(picked, names == named[j : j + 1, :])
            logits = dot_nt(router, block_value(pieces[1], blocks, k))
            gate_s[k] = softmax_over(picked, logits, 0)
            before = dot_nn(jnp.where(picked, 1.0, 0.0).astype(bf16), later)
            rank_s[k] = jnp.where(picked, before, -1.0)
        gg_s[...] = jnp.zeros_like(gg_s)

    for (r, row, value), ref in zip(pieces[0], weights):
        rows = value.shape[1]
        low, high = row, min(row + rows, up_rows)
        if high > low:
            to = pl.ds(pl.multiple_of(meta[r] * up_rows + low, 32), high - low)
            up_s[to, :] = ref[0, low - row : high - row, :]
        low, high = max(row, up_rows), row + rows
        if high > low:
            to = pl.ds(pl.multiple_of(meta[r] * down_rows + low - up_rows, 32), high - low)
            down_s[to, :] = ref[0, low - row : high - row, :]

    wanted = lax.broadcasted_iota(jnp.int32, (CAP, TILE), 0).astype(f32)
    held = aligned(step * CAP, CAP)
    gates = []
    for k in range(count):
        rank = rank_s[k, pl.ds(expert, 1), :]
        gate = gate_s[k, pl.ds(expert, 1), :]
        hit = wanted == rank
        chosen = jnp.where(hit, 1.0, 0.0).astype(bf16)
        d_s[k, held, :] = chosen
        here = slice(k * CAP, (k + 1) * CAP)
        x_s[here, :] = dot_nn(chosen, block_value(pieces[1], blocks, k)).astype(bf16)
        upstream = dot_nn(chosen, c_ref[aligned(absolute(k) * TILE, TILE), :])
        own_gate = jnp.sum(jnp.where(hit, gate, 0.0), axis=1, keepdims=True)
        gates.append(own_gate)
        c_s[here, :] = upstream.astype(bf16)
        ge_s[here, :] = (own_gate * (res_scale * upstream)).astype(bf16)

    for j in range(FF // TILE):
        left, right = slice(j * TILE, (j + 1) * TILE), slice(FF + j * TILE, FF + (j + 1) * TILE)
        gate_part = dot_nn(x_s[...], up_s[:, left])
        up_part = dot_nn(x_s[...], up_s[:, right])
        hidden_grad = dot_nt(ge_s[...], down_s[left, :])
        sigmoid_gate = jax.nn.sigmoid(gate_part)
        swish = gate_part * sigmoid_gate
        a_s[:, left] = (swish * up_part).astype(bf16)
        slope = sigmoid_gate * (1.0 + gate_part * (1.0 - sigmoid_gate))
        gu_s[:, left] = (hidden_grad * up_part * slope).astype(bf16)
        gu_s[:, right] = (hidden_grad * swish).astype(bf16)

    gate_grad = jnp.zeros((slots, 1), f32)
    for j in range(MODEL_WIDTH // TILE):
        columns = slice(j * TILE, (j + 1) * TILE)
        produced = dot_nn(a_s[...], down_s[:, columns]).astype(bf16).astype(f32)
        gate_grad += jnp.sum(res_scale * c_s[:, columns].astype(f32) * produced, axis=1, keepdims=True)
        input_grad = dot_nt(gu_s[...], up_s[columns, :]).astype(bf16)
        for k in range(count):
            here = slice(k * CAP, (k + 1) * CAP)
            eg_s[k, held, columns] = (gates[k] * produced[here]).astype(bf16)
            gs_s[k, held, columns] = input_grad[here]
    for k in range(count):
        hit = wanted == rank_s[k, pl.ds(expert, 1), :]
        spread = jnp.where(hit, gate_grad[k * CAP : (k + 1) * CAP], 0.0)
        gg_s[k, pl.ds(expert, 1), :] = jnp.sum(spread, axis=0, keepdims=True)

    for j in range(FF // TILE):
        rows = slice(j * TILE, (j + 1) * TILE)
        gdown_s[rows, :] = dot_tn(a_s[:, rows], ge_s[...]).astype(bf16)
    for j in range(MODEL_WIDTH // TILE):
        rows = slice(j * TILE, (j + 1) * TILE)
        gup_s[rows, :] = dot_tn(x_s[:, rows], gu_s[...]).astype(bf16)
    for r in range(shards):
        ref = send_ref if r % 2 else keep_ref
        ref[r // 2, 0, :up_rows, :] = gup_s[aligned(meta[r] * up_rows, up_rows), :]
        ref[r // 2, 0, up_rows:, :] = gdown_s[aligned(meta[r] * down_rows, down_rows), :]

    @pl.when(step == members - 1)
    def combine():
        for k in range(count):
            spread = d_s[k]
            mixed = dot_tn(spread, eg_s[k])
            summed = dot_tn(spread, gs_s[k])
            exact = gg_s[k]
            rounded = exact.astype(bf16).astype(f32)
            rest = jnp.zeros((LANES - 2 * EXPERTS, TILE), f32)
            tail = jnp.concatenate([rounded, exact - rounded, rest], axis=0).T
            at = absolute(k)
            if chunk > 0:
                mixed += part_m[at].astype(f32)
                summed += part_g[k, :, :MODEL_WIDTH].astype(f32)
                tail += part_g[k, :, MODEL_WIDTH:].astype(f32)
            mix_ref[at] = mixed.astype(bf16)
            if last:
                ring_put(count, ring_refs, k, TILE, summed)
                ring_put_tail(count, ring_refs, k, TILE, tail)
            else:
                ring_refs[0][k, :, :MODEL_WIDTH] = summed.astype(bf16)
                ring_refs[0][k, :, MODEL_WIDTH:] = tail.astype(bf16)


def backward_body(count, pieces, summed, meta, routes_ref, normed_ref, extra_ref, h_ref, c_ref, a_ref, wo_ref, q_ref, lse_ref, cos_ref, sin_ref, *refs):
    sums = refs[:summed]
    blocks = refs[summed : summed + len(pieces)]
    outs = refs[summed + len(pieces) :]
    gh_ref, go_ref, gpq_ref, gex_ref, gain_ref = outs[:5]
    ring_refs, ga_s = outs[5:-1], outs[-1]
    rows = q_ref.shape[0]
    place = meta[0]
    total = ring_total(sums)
    normed_grad, tail = total[:, :MODEL_WIDTH], total[:, MODEL_WIDTH:]
    names = lanes_of((rows, LANES))
    named = routes_ref[...]
    picked = names == named[:, 0:1]
    for j in range(1, TOP):
        picked = jnp.logical_or(picked, names == named[:, j : j + 1])
    row_names = lax.broadcasted_iota(jnp.int32, (LANES, MODEL_WIDTH), 0)
    router = jnp.where(row_names < EXPERTS, extra_ref[...], 0.0).astype(bf16)
    gate = softmax_over(picked, dot_nt(normed_ref[...], router), 1)
    gate_grad = jnp.where(picked, tail + pltpu.roll(tail, LANES - EXPERTS, 1), 0.0)
    inner = jnp.sum(gate * gate_grad, axis=1, keepdims=True)
    logit_grad = (gate * (gate_grad - inner)).astype(bf16)
    gex_ref[...] = dot_tn(normed_ref[...], logit_grad)
    normed_grad += dot_nn(logit_grad, router)
    resid = h_ref[...]
    scale_inv = lax.rsqrt(jnp.mean(resid * resid, axis=-1, keepdims=True) + epsilon)
    hat = resid * scale_inv
    gain_ref[...] = jnp.broadcast_to(jnp.sum(normed_grad * hat, axis=0, keepdims=True), gain_ref.shape)
    scaled = normed_grad * extra_ref[EXPERTS + 1 : EXPERTS + 2, :]
    part = scale_inv * (scaled - hat * jnp.mean(scaled * hat, axis=-1, keepdims=True))
    resid_grad = c_ref[...].astype(f32) + part
    gh_ref[...] = resid_grad
    go = (res_scale * resid_grad).astype(bf16)
    go_ref[...] = go
    ga_s[...] = dot_nt(go, wo_ref[...]).astype(bf16)
    cosine, sine = cos_ref[...], sin_ref[...]
    low = lanes_of((rows, LANES)) < HEAD_SIZE

    def variant(seen):
        def group(g, carry):
            lanes = aligned(g * LANES, LANES)
            pair = query_pair(q_ref[:, lanes])
            upstream = ga_s[:, lanes].astype(f32)
            product = upstream * a_ref[:, lanes].astype(f32)
            inner_low = jnp.sum(jnp.where(low, product, 0.0), axis=1, keepdims=True)
            inner_high = jnp.sum(jnp.where(low, 0.0, product), axis=1, keepdims=True)
            delta = jnp.concatenate([inner_low, inner_high], axis=0)
            logs = lse_ref[:, lanes]
            logsum = jnp.concatenate([logs[:, 0:1], logs[:, HEAD_SIZE : HEAD_SIZE + 1]], axis=0)
            high_pair = jnp.concatenate(
                [jnp.where(low, 0.0, pltpu.roll(upstream, HEAD_SIZE, 1)), jnp.where(low, 0.0, upstream)], axis=0
            ).astype(bf16)
            query_grad = jnp.zeros((2 * rows, LANES), f32)
            for k in range(seen):
                keys = block_lanes(pieces, blocks, k, lanes)
                weights = jnp.exp(causal_scores(pair, keys, k) - logsum)
                score_grad = (weights * (dot_nt(high_pair, keys) - delta)).astype(bf16)
                query_grad += dot_nn(score_grad, keys)
                back = dot_tn(score_grad, pair) + dot_tn(weights.astype(bf16), high_pair)
                put_lanes(k, lanes, back)
            query_grad = query_grad * att_scale
            tile = jnp.where(low, query_grad[:rows], pltpu.roll(query_grad[rows:], HEAD_SIZE, 1))
            tile = tile.astype(bf16).astype(f32)
            gpq_ref[:, lanes] = rotate_tile_back(tile, cosine, sine).astype(bf16)
            return carry

        lax.fori_loop(0, KEY_VALUE_HEADS, group, 0)
        for k in range(seen, count):
            ring_put(count, ring_refs, k, rows, jnp.zeros((rows, MODEL_WIDTH), f32))

    def put_lanes(k, lanes, value):
        views = [r.at[..., lanes] for r in ring_refs]
        ring_put(count, views, k, rows, value)

    for seen in range(1, count + 1):
        pl.when(place == seen - 1)(functools.partial(variant, seen))


def store_sets(shards, meta, source, send_ref, keep_ref, columns):
    rows = MODEL_WIDTH // shards
    for r in range(shards):
        ref = send_ref if r % 2 else keep_ref
        ref[r // 2, :, columns] = source[aligned(meta[r] * rows, rows), :].astype(bf16)


def query_weights_body(shards, meta, a_ref, go_ref, normed_ref, gpq_ref, wq_ref, send_ref, keep_ref, part_ref, full_s):
    full_s[...] = dot_tn(normed_ref[...], gpq_ref[...]).astype(bf16)
    store_sets(shards, meta, full_s, send_ref, keep_ref, slice(0, MODEL_WIDTH))
    full_s[...] = dot_tn(a_ref[...], go_ref[...]).astype(bf16)
    store_sets(shards, meta, full_s, send_ref, keep_ref, slice(MODEL_WIDTH, 2 * MODEL_WIDTH))
    part_ref[...] = dot_nt(gpq_ref[...], wq_ref[...])


def final_body(shards, summed, meta, x_ref, normed_ref, wkv_ref, extra_ref, part_ref, gh_ref, gex_ref, gain_ref, cos_ref, sin_ref, *refs):
    sums = refs[:summed]
    grad_ref, send_ref, keep_ref, gpkv_s, full_s, extra_s = refs[summed:]
    total = ring_total(sums).astype(bf16).astype(f32)
    cosine, sine = cos_ref[...], sin_ref[...]
    low = lanes_of(cosine.shape) < HEAD_SIZE
    for j in range(MODEL_WIDTH // LANES):
        lanes = slice(j * LANES, (j + 1) * LANES)
        tile = total[:, lanes]
        gpkv_s[:, lanes] = jnp.where(low, rotate_tile_back(tile, cosine, sine), tile).astype(bf16)
    normed_grad = part_ref[...] + dot_nt(gpkv_s[...], wkv_ref[...])
    source = x_ref[...].astype(f32)
    scale_inv = lax.rsqrt(jnp.mean(source * source, axis=-1, keepdims=True) + epsilon)
    hat = source * scale_inv
    gain_grad = jnp.sum(normed_grad * hat, axis=0, keepdims=True)
    scaled = normed_grad * extra_ref[EXPERTS : EXPERTS + 1, :]
    part = scale_inv * (scaled - hat * jnp.mean(scaled * hat, axis=-1, keepdims=True))
    grad_ref[...] = gh_ref[...] + part
    full_s[...] = dot_tn(normed_ref[...], gpkv_s[...]).astype(bf16)
    store_sets(shards, meta, full_s, send_ref, keep_ref, slice(0, MODEL_WIDTH))
    row_names = lax.broadcasted_iota(jnp.int32, (LANES, MODEL_WIDTH), 0)
    gains = jnp.where(row_names == EXPERTS, gain_grad, jnp.where(row_names == EXPERTS + 1, gain_ref[0:1, :], 0.0))
    extra_s[...] = gex_ref[...] + gains.T
    store_sets(shards, meta, extra_s, send_ref, keep_ref, slice(MODEL_WIDTH, WIDE))


def angle_tables(rows, offset):
    position = (offset + jnp.arange(rows)).astype(f32)
    frequency = 10000.0 ** (-(jnp.arange(HEAD_SIZE // 2).astype(f32) * 2.0 / HEAD_SIZE))
    angles = position[:, None] * frequency[None, :]
    cosine, sine = jnp.cos(angles), jnp.sin(angles)
    return (jnp.concatenate([cosine] * 4, axis=1), jnp.concatenate([-sine, sine] * 2, axis=1))


def shards_step(
    tokens,
    routes,
    cotangent,
    norm_gains,
    qkv_weight,
    out_weight,
    router_weight,
    expert_up,
    expert_down,
    mean_gains,
    square_gains,
    mean_qkv,
    square_qkv,
    mean_out,
    square_out,
    mean_router,
    square_router,
    mean_up,
    square_up,
    mean_down,
    square_down,
):
    rows = tokens.shape[1]
    count = lax.axis_size("seq")
    shards = lax.axis_size("fsdp")
    shard_rows = MODEL_WIDTH // shards
    local = EXPERTS // count
    members = local // CHUNKS
    place = lax.axis_index("seq").astype(jnp.int32)
    owners = (lax.axis_index("fsdp") ^ jnp.arange(shards)).astype(jnp.int32)
    owner_meta = jnp.concatenate([owners, place[None]])
    place_meta = place[None]
    x, c, own_routes = tokens[0], cotangent[0], routes[0]

    blank = jnp.zeros((shard_rows, LANES - EXPERTS - 2), f32)
    dense = jnp.concatenate([qkv_weight, out_weight, router_weight, norm_gains.T, blank], axis=1).astype(bf16)
    dense_pieces = gather_shards(dense)
    expert_pieces = []
    for i in range(CHUNKS):
        mine = slice(i * members, (i + 1) * members)
        packed = jnp.concatenate([expert_up[mine], expert_down[mine]], axis=1).astype(bf16)
        expert_pieces.append(gather_shards(packed))
    all_c = lax.all_gather(c, "seq", axis=0, tiled=True)
    all_routes = lax.all_gather(own_routes.T, "seq", axis=0)
    cosine, sine = angle_tables(rows, place * rows)

    square = shape_of((MODEL_WIDTH, MODEL_WIDTH))
    wide = shape_of((rows, MODEL_WIDTH))
    wide_f = shape_of((rows, MODEL_WIDTH), f32)
    extra_shape = shape_of((LANES, MODEL_WIDTH), f32)
    unit = 2 * rows * MODEL_WIDTH * MODEL_WIDTH
    wq, wkv, wo, extra, normed_one, q, kv = kernel_call(
        functools.partial(qkv_body, dense_pieces),
        [square, square, square, extra_shape, wide, wide, wide],
        [x, cosine, sine] + [a for _, _, a in dense_pieces],
        owner_meta,
        scratch=[pltpu.VMEM((MODEL_WIDTH, LANES), f32)],
        flops=2 * unit,
    )
    kv_pieces = ring_gather(kv)
    attended, logsum, resid, normed_two = kernel_call(
        functools.partial(attend_body, count, kv_pieces),
        [wide, wide_f, wide_f, wide],
        [q, x, wo, extra] + [a for _, _, a in kv_pieces],
        place_meta,
        flops=4 * unit,
    )
    two_pieces = ring_gather(normed_two)

    slots = count * CAP
    packed_rows = (MODEL_WIDTH + FF) // shards
    part_g = part_m = None
    sets = []
    for i in range(CHUNKS):
        last = i == CHUNKS - 1
        pieces = (expert_pieces[i], two_pieces)
        ins = [all_routes, all_c, extra] + [a for _, _, a in pieces[0]] + [a for _, _, a in pieces[1]]

        def still(a):
            return pl.BlockSpec(a.shape, functools.partial(lambda n, e, m: (0,) * n, a.ndim), pipeline_mode=pl.Buffered(1))

        in_specs = [still(a) for a in ins[:3]]
        in_specs += [pl.BlockSpec((1,) + a.shape[1:], lambda e, m: (e, 0, 0)) for _, _, a in pieces[0]]
        in_specs += [still(a) for _, _, a in pieces[1]]
        if i > 0:
            ins += [part_g, part_m]
            in_specs += [still(part_g), still(part_m)]
        set_shape = shape_of((shards // 2, members, packed_rows, MODEL_WIDTH))
        set_spec = pl.BlockSpec((shards // 2, 1, packed_rows, MODEL_WIDTH), lambda e, m: (0, e, 0, 0))
        ring = ring_shapes(count, rows, WIDE) if last else [shape_of((count, rows, WIDE))]
        outs = [set_shape, set_shape, shape_of((count, rows, MODEL_WIDTH))] + ring
        out_specs = [set_spec, set_spec] + [still(a) for a in outs[2:]]
        scratch = [
            pltpu.VMEM((MODEL_WIDTH, 2 * FF), bf16),
            pltpu.VMEM((FF, MODEL_WIDTH), bf16),
            pltpu.VMEM((slots, MODEL_WIDTH), bf16),
            pltpu.VMEM((slots, MODEL_WIDTH), bf16),
            pltpu.VMEM((slots, MODEL_WIDTH), bf16),
            pltpu.VMEM((slots, FF), bf16),
            pltpu.VMEM((slots, 2 * FF), bf16),
            pltpu.VMEM((count, members * CAP, rows), bf16),
            pltpu.VMEM((count, members * CAP, MODEL_WIDTH), bf16),
            pltpu.VMEM((count, members * CAP, MODEL_WIDTH), bf16),
            pltpu.VMEM((MODEL_WIDTH, 2 * FF), bf16),
            pltpu.VMEM((FF, MODEL_WIDTH), bf16),
            pltpu.VMEM((count, EXPERTS, rows), f32),
            pltpu.VMEM((count, EXPERTS, rows), f32),
            pltpu.VMEM((count, EXPERTS, rows), f32),
        ]
        results = kernel_call(
            functools.partial(experts_body, count, shards, pieces, i, last),
            outs,
            ins,
            owner_meta,
            scratch=scratch,
            grid=(members,),
            in_specs=in_specs,
            out_specs=out_specs,
            flops=members * slots * MODEL_WIDTH * FF * 18,
            limit=60,
        )
        sets.append(scatter_sets(results[0], results[1]))
        part_m = results[2]
        part_g = results[3]
        ring_parts = results[3:]

    mixture = lax.psum_scatter(part_m, "seq", scatter_dimension=0).astype(f32)
    output = (resid + res_scale * mixture).astype(bf16)[None]

    two_sums = ring_reduce(ring_parts)
    ring = ring_shapes(count, rows, MODEL_WIDTH)
    results = kernel_call(
        functools.partial(backward_body, count, kv_pieces, len(two_sums)),
        [wide_f, wide, wide, shape_of((MODEL_WIDTH, LANES), f32), shape_of((8, MODEL_WIDTH), f32)] + ring,
        [own_routes, normed_two, extra, resid, c, attended, wo, q, logsum, cosine, sine]
        + list(two_sums)
        + [a for _, _, a in kv_pieces],
        place_meta,
        scratch=[pltpu.VMEM((rows, MODEL_WIDTH), bf16)],
        flops=8 * unit,
    )
    resid_grad, go, gpq, router_grad, gain_grad = results[:5]
    kv_sums = ring_reduce(results[5:])
    dense_sets = shape_of((shards // 2, shard_rows, 2 * MODEL_WIDTH))
    send_q, keep_q, normed_part = kernel_call(
        functools.partial(query_weights_body, shards),
        [dense_sets, dense_sets, wide_f],
        [attended, go, normed_one, gpq, wq],
        owner_meta,
        scratch=[pltpu.VMEM((MODEL_WIDTH, MODEL_WIDTH), bf16)],
        flops=3 * unit,
    )
    rest_sets = shape_of((shards // 2, shard_rows, WIDE))
    tokens_grad, send_kv, keep_kv = kernel_call(
        functools.partial(final_body, shards, len(kv_sums)),
        [wide_f, rest_sets, rest_sets],
        [x, normed_one, wkv, extra, normed_part, resid_grad, router_grad, gain_grad, cosine, sine] + list(kv_sums),
        owner_meta,
        scratch=[
            pltpu.VMEM((rows, MODEL_WIDTH), bf16),
            pltpu.VMEM((MODEL_WIDTH, MODEL_WIDTH), bf16),
            pltpu.VMEM((MODEL_WIDTH, LANES), f32),
        ],
        flops=2 * unit,
    )
    tokens_grad = tokens_grad[None]

    def dense_total(send, keep):
        whole = jnp.concatenate(scatter_sets(send, keep), axis=0)
        return lax.psum(whole.astype(bf16), "seq").astype(f32)

    first = dense_total(send_q, keep_q)
    second = dense_total(send_kv, keep_kv)
    shard_qkv = jnp.concatenate([first[:, :MODEL_WIDTH], second[:, :MODEL_WIDTH]], axis=1)
    shard_out = first[:, MODEL_WIDTH:]
    shard_router = second[:, MODEL_WIDTH : MODEL_WIDTH + EXPERTS]
    shard_gains = second[:, MODEL_WIDTH + EXPERTS : MODEL_WIDTH + EXPERTS + 2].T
    packed_grad = jnp.concatenate([jnp.concatenate(s, axis=1) for s in sets], axis=0)
    shard_up = packed_grad[:, :shard_rows]
    shard_down = packed_grad[:, shard_rows:]
    fresh_gains, momentum_gains, variance_gains = adam_update(
        norm_gains, shard_gains, mean_gains, square_gains, learn_rates[0]
    )
    fresh_qkv, momentum_qkv, variance_qkv = adam_update(
        qkv_weight, shard_qkv, mean_qkv, square_qkv, learn_rates[1]
    )
    fresh_out, momentum_out, variance_out = adam_update(
        out_weight, shard_out, mean_out, square_out, learn_rates[2]
    )
    fresh_router, momentum_router, variance_router = adam_update(
        router_weight, shard_router, mean_router, square_router, learn_rates[3]
    )
    fresh_up, momentum_up, variance_up = adam_update(
        expert_up, shard_up, mean_up, square_up, learn_rates[4]
    )
    fresh_down, momentum_down, variance_down = adam_update(
        expert_down, shard_down, mean_down, square_down, learn_rates[5]
    )
    return (
        output,
        tokens_grad,
        shard_gains,
        shard_qkv,
        shard_out,
        shard_router,
        shard_up,
        shard_down,
        fresh_gains,
        fresh_qkv,
        fresh_out,
        fresh_router,
        fresh_up,
        fresh_down,
        momentum_gains,
        momentum_qkv,
        momentum_out,
        momentum_router,
        momentum_up,
        momentum_down,
        variance_gains,
        variance_qkv,
        variance_out,
        variance_router,
        variance_up,
        variance_down,
    )


def solution(mesh):
    block = P("fsdp", "seq", None)
    gains, dense, experts = P(None, "fsdp"), P("fsdp", None), P("seq", "fsdp", None)
    weights = (gains, dense, dense, dense, experts, experts)
    moments = tuple(s for spec in weights for s in (spec, spec))
    return jax.shard_map(
        shards_step,
        mesh=mesh,
        in_specs=(block, block, block) + weights + moments,
        out_specs=(block, block) + weights * 4,
        check_vma=False,
    )
```

```python
import functools

import jax
import jax.numpy as jnp
from jax import lax
from jax.experimental import pallas as pl
from jax.experimental.pallas import tpu as pltpu
from jax.sharding import PartitionSpec as P

MODEL_WIDTH = 1024
QUERY_HEADS = 16
KEY_VALUE_HEADS = 8
HEAD_SIZE = 64
EXPERTS = 32
FF = 512
TOP = 8
STEP = 3
CAP = 96
LANES = 128
TILE = 256

epsilon = 1e-06
res_scale = 0.22
att_scale = 0.015625
beta_one = 0.9
beta_two = 0.95
adam_eps = 1e-08
weight_decay = 0.1
learn_rates = (0.4, 0.04, 0.2, 0.01, 0.01, 0.05)

bf16 = jnp.bfloat16
f32 = jnp.float32
WIDE = MODEL_WIDTH + LANES


def adam_update(weight, gradient, first, second, rate):
    first_new = beta_one * first + (1.0 - beta_one) * gradient
    second_new = beta_two * second + (1.0 - beta_two) * gradient * gradient
    first_hat = first_new / (1.0 - beta_one**STEP)
    second_hat = second_new / (1.0 - beta_two**STEP)
    fresh = weight - rate * (first_hat / (jnp.sqrt(second_hat) + adam_eps) + weight_decay * weight)
    return (fresh, first_new, second_new)


def dot_nn(a, b):
    return lax.dot_general(a, b, (((1,), (0,)), ((), ())), preferred_element_type=f32)


def dot_nt(a, b):
    return lax.dot_general(a, b, (((1,), (1,)), ((), ())), preferred_element_type=f32)


def dot_tn(a, b):
    return lax.dot_general(a, b, (((0,), (0,)), ((), ())), preferred_element_type=f32)


def lanes_of(shape):
    return lax.broadcasted_iota(jnp.int32, shape, len(shape) - 1)


def aligned(index, size):
    if isinstance(index, int):
        return slice(index, index + size)
    return pl.ds(pl.multiple_of(index, size), size)


def kernel_call(body, outs, ins, scalars, scratch=(), grid=None, in_specs=None, out_specs=None, limit=60, after=(), micros=10, aliases=None):
    in_specs = in_specs or [pl.BlockSpec(memory_space=pltpu.VMEM)] * len(ins)
    out_specs = out_specs or [pl.BlockSpec(memory_space=pltpu.VMEM)] * len(outs)
    in_specs = [pl.BlockSpec(memory_space=pl.ANY)] * len(after) + in_specs

    def ordered_body(meta, *refs):
        body(meta, *refs[len(after) :])

    return pl.pallas_call(
        ordered_body,
        out_shape=outs,
        grid_spec=pltpu.PrefetchScalarGridSpec(
            num_scalar_prefetch=1,
            grid=grid or (1,),
            in_specs=in_specs,
            out_specs=out_specs,
            scratch_shapes=list(scratch),
        ),
        compiler_params=pltpu.CompilerParams(vmem_limit_bytes=limit * 1024 * 1024),
        input_output_aliases=aliases or {},
        cost_estimate=pl.CostEstimate(flops=micros * 10**9, bytes_accessed=micros * 10**6, transcendentals=0),
    )(scalars, *after, *ins)


def tie(value, *earlier):
    anywhere = pl.BlockSpec(memory_space=pl.ANY)
    return pl.pallas_call(
        lambda *refs: None,
        out_shape=shape_of(value.shape, value.dtype),
        in_specs=[anywhere] * (1 + len(earlier)),
        out_specs=anywhere,
        input_output_aliases={0: 0},
    )(value, *earlier)


def shape_of(shape, kind=bf16):
    return jax.ShapeDtypeStruct(shape, kind)


def xor_permute(value, axis, mask):
    return lax.ppermute(value, axis, [(i, i ^ mask) for i in range(lax.axis_size(axis))])


def shift_permute(value, axis, step):
    size = lax.axis_size(axis)
    return lax.ppermute(value, axis, [(i, (i + step) % size) for i in range(size)])


class Gathered:
    def __init__(self, value):
        self.plain = lax.axis_size("fsdp") != 8
        self.value = value
        self.half = value.shape[0] // 2
        if not self.plain:
            self.over_x = xor_permute(value, "fsdp", 2)
            self.over_y = xor_permute(value, "fsdp", 4)
            self.core = xor_permute(value, "fsdp", 1)

    def forward(self, *earlier):
        if self.plain:
            return
        self.over_x = tie(self.over_x, self.core, *earlier)
        self.over_y = tie(self.over_y, self.core, *earlier)
        self.far_first = xor_permute(self.over_x[: self.half], "fsdp", 4)
        self.far_second = xor_permute(self.over_y[self.half :], "fsdp", 2)

    def arrived(self):
        return () if self.plain else (self.far_first, self.far_second)

    def pieces(self, *earlier):
        count, half = lax.axis_size("fsdp"), self.half
        if self.plain:
            whole = lax.all_gather(self.value, "fsdp", axis=0)
            whole = jnp.take(whole, lax.axis_index("fsdp") ^ jnp.arange(count), axis=0)
            return [(r, 0, whole[r]) for r in range(count)]
        if earlier:
            self.far_first = tie(self.far_first, *earlier)
            self.far_second = tie(self.far_second, *earlier)
        mine = [(2, 0, self.over_x), (4, 0, self.over_y), (6, 0, self.far_first), (6, half, self.far_second)]
        pieces = [(0, 0, self.value), (1, 0, self.core)] + mine
        return pieces + [(r + 1, row, xor_permute(a, "fsdp", 1)) for r, row, a in mine]


def pairs_body(groups, meta, *refs):
    sent_x, sent_y, rest = refs[2 * groups :]
    left = 0
    for keep, got in zip(refs[:groups], refs[groups : 2 * groups]):
        half, columns = keep.shape[1] // 2, keep.shape[2]
        lanes = slice(left, left + columns)
        left += columns

        def pair(i, part):
            piece = slice(part * half, (part + 1) * half)
            return (keep[i, piece, :].astype(f32) + got[i, piece, :].astype(f32)).astype(bf16)

        for ref, place, value in (
            (sent_x, 0, pair(3, 0)),
            (sent_x, 1, pair(1, 0)),
            (sent_y, 0, pair(3, 1)),
            (sent_y, 1, pair(2, 1)),
            (rest, 0, pair(0, 0)),
            (rest, 1, pair(0, 1)),
            (rest, 2, pair(1, 1)),
            (rest, 3, pair(2, 0)),
        ):
            ref[place, :, lanes] = value


def passed_body(meta, rest, over_x, over_y, then_x, then_y):
    then_x[...] = (rest[2].astype(f32) + over_y[0].astype(f32)).astype(bf16)
    then_y[...] = (rest[3].astype(f32) + over_x[0].astype(f32)).astype(bf16)


def summed_body(meta, rest, over_x, over_y, then_x, then_y, total):
    half = rest.shape[1]
    total[:half, :] = (rest[0].astype(f32) + over_x[1].astype(f32) + then_y[...].astype(f32)).astype(bf16)
    total[half:, :] = (rest[1].astype(f32) + over_y[1].astype(f32) + then_x[...].astype(f32)).astype(bf16)


class Scattered:
    def __init__(self, scalars):
        self.plain = lax.axis_size("fsdp") != 8
        self.scalars = scalars
        self.send, self.keep, self.got = [], [], []

    def add(self, send, keep, *earlier):
        self.send.append(send)
        self.keep.append(keep)
        if not self.plain:
            self.got.append(xor_permute(tie(send, *earlier) if earlier else send, "fsdp", 1))

    def first(self, *earlier):
        if self.plain:
            return ()
        rows, columns = self.keep[0].shape[1], sum(a.shape[2] for a in self.keep)
        two, four = shape_of((2, rows // 2, columns)), shape_of((4, rows // 2, columns))
        body = functools.partial(pairs_body, len(self.keep))
        sent_x, sent_y, self.rest = kernel_call(
            body, [two, two, four], self.keep + self.got, self.scalars, after=earlier, micros=3
        )
        self.over_x = xor_permute(sent_x, "fsdp", 2)
        self.over_y = xor_permute(sent_y, "fsdp", 4)
        return (sent_x, sent_y)

    def second(self, *earlier):
        if self.plain:
            return ()
        one = shape_of(self.rest.shape[1:])
        ins = [self.rest, self.over_x, self.over_y]
        sent_x, sent_y = kernel_call(passed_body, [one, one], ins, self.scalars, after=earlier, micros=2)
        self.then_x = xor_permute(sent_x, "fsdp", 2)
        self.then_y = xor_permute(sent_y, "fsdp", 4)
        return (sent_x, sent_y)

    def total(self, *earlier):
        if self.plain:
            count = lax.axis_size("fsdp")
            keep, send = jnp.concatenate(self.keep, axis=2), jnp.concatenate(self.send, axis=2)
            both = jnp.stack([keep, send], axis=1).reshape((count,) + keep.shape[1:])
            both = jnp.take(both, lax.axis_index("fsdp") ^ jnp.arange(count), axis=0)
            return lax.psum_scatter(both, "fsdp", scatter_dimension=0)
        ins = [self.rest, self.over_x, self.over_y, self.then_x, self.then_y]
        outs = [shape_of((2 * self.rest.shape[1], self.rest.shape[2]))]
        return kernel_call(summed_body, outs, ins, self.scalars, after=earlier, micros=2)[0]


def expert_pairs_body(meta, keep, got, sent_x, sent_y, rest):
    half = keep.shape[2] // 2

    def pair(i, part):
        piece = slice(part * half, (part + 1) * half)
        return (keep[i, 0, piece, :].astype(f32) + got[i, 0, piece, :].astype(f32)).astype(bf16)

    sent_x[0, 0], sent_x[1, 0] = pair(3, 0), pair(1, 0)
    sent_y[0, 0], sent_y[1, 0] = pair(3, 1), pair(2, 1)
    rest[0, 0], rest[1, 0], rest[2, 0], rest[3, 0] = pair(0, 0), pair(0, 1), pair(1, 1), pair(2, 0)


def expert_passed_body(meta, rest, over_x, over_y, then_x, then_y):
    then_x[0] = (rest[0, 0].astype(f32) + over_y[0, 0].astype(f32)).astype(bf16)
    then_y[0] = (rest[1, 0].astype(f32) + over_x[0, 0].astype(f32)).astype(bf16)


class ScatteredExperts:
    def __init__(self, send, keep, scalars):
        self.plain = lax.axis_size("fsdp") != 8
        self.send, self.keep, self.scalars = send, keep, scalars
        if not self.plain:
            self.got = xor_permute(send, "fsdp", 1)

    def first(self, *earlier):
        if self.plain:
            return ()
        sets, self.members, rows, columns = self.keep.shape
        half = rows // 2

        def group(n, start=0):
            return pl.BlockSpec((n, 1, half, columns), lambda e, m: (start, e, 0, 0))

        self.group = group
        self.single = pl.BlockSpec((1, half, columns), lambda e, m: (e, 0, 0))
        whole = pl.BlockSpec((sets, 1, rows, columns), lambda e, m: (0, e, 0, 0))
        shapes = [shape_of((n, self.members, half, columns)) for n in (2, 2, 4)]
        sent_x, sent_y, self.rest = kernel_call(
            expert_pairs_body,
            shapes,
            [self.keep, self.got],
            self.scalars,
            grid=(self.members,),
            in_specs=[whole, whole],
            out_specs=[group(2), group(2), group(4)],
            after=earlier,
            micros=6,
        )
        self.over_x = xor_permute(sent_x, "fsdp", 2)
        self.over_y = xor_permute(sent_y, "fsdp", 4)
        return (sent_x, sent_y)

    def arrived(self):
        return () if self.plain else (self.over_x, self.over_y)

    def second(self, *earlier):
        if self.plain:
            return ()
        one = shape_of(self.rest.shape[1:])
        sent_x, sent_y = kernel_call(
            expert_passed_body,
            [one, one],
            [self.rest, self.over_x, self.over_y],
            self.scalars,
            grid=(self.members,),
            in_specs=[self.group(2, 1), self.group(1), self.group(1)],
            out_specs=[self.single, self.single],
            after=earlier,
            micros=4,
        )
        self.then_x = xor_permute(sent_x, "fsdp", 2)
        self.then_y = xor_permute(sent_y, "fsdp", 4)
        return (sent_x, sent_y)

    def total(self):
        if self.plain:
            count = lax.axis_size("fsdp")
            both = jnp.stack([self.keep, self.send], axis=1).reshape((count,) + self.keep.shape[1:])
            both = jnp.take(both, lax.axis_index("fsdp") ^ jnp.arange(count), axis=0)
            share = lax.psum_scatter(both, "fsdp", scatter_dimension=0)
            spec = pl.BlockSpec((1,) + share.shape[1:], lambda e, m: (e, 0, 0))
            return ([share], [spec], lambda refs: refs[0][0].astype(f32))
        arrays = [self.rest, self.over_x, self.over_y, self.then_x, self.then_y]
        specs = [self.group(2), self.group(1, 1), self.group(1, 1), self.single, self.single]

        def rows_of(refs):
            rest, over_x, over_y, then_x, then_y = refs
            first = rest[0, 0].astype(f32) + over_x[0, 0].astype(f32) + then_y[0].astype(f32)
            second = rest[1, 0].astype(f32) + over_y[0, 0].astype(f32) + then_x[0].astype(f32)
            return jnp.concatenate([first, second], axis=0)

        return (arrays, specs, rows_of)


class Ringed:
    def __init__(self, block):
        self.plain = lax.axis_size("seq") != 4
        self.block = block
        self.half = block.shape[0] // 2
        if not self.plain:
            self.below = shift_permute(block, "seq", 1)
            self.above = shift_permute(block, "seq", -1)

    def near(self):
        return () if self.plain else (self.below, self.above)

    def forward(self):
        if self.plain:
            return ()
        self.far_first = shift_permute(self.below[: self.half], "seq", 1)
        self.far_second = shift_permute(self.above[self.half :], "seq", -1)
        return (self.far_first, self.far_second)

    def pieces(self):
        count = lax.axis_size("seq")
        if self.plain:
            whole = lax.all_gather(self.block, "seq", axis=0)
            whole = jnp.take(whole, (lax.axis_index("seq") - jnp.arange(count)) % count, axis=0)
            return [(k, 0, whole[k]) for k in range(count)]
        pieces = [(0, 0, self.block), (1, 0, self.below), (3, 0, self.above)]
        return pieces + [(2, 0, self.far_first), (2, self.half, self.far_second)]


def ring_gather(block):
    ring = Ringed(block)
    ring.forward()
    return ring.pieces()


def ring_shapes(count, rows, columns):
    if count != 4:
        return [shape_of((count, rows, columns))]
    half = rows // 2
    return [shape_of((r, columns)) for r in (rows, rows, rows, half, half)]


def ring_put(count, refs, k, rows, value):
    half = rows // 2
    width = value.shape[1]
    value = value.astype(bf16)
    if count != 4:
        refs[0][k, :, :width] = value
        return
    own, down, up, keep_down, keep_up = refs
    places = {
        0: ((own, 0), (own, half)),
        1: ((keep_down, 0), (down, half)),
        2: ((down, 0), (up, 0)),
        3: ((up, half), (keep_up, 0)),
    }
    for part, (ref, row) in enumerate(places[k]):
        ref[row : row + half, :width] = value[part * half : (part + 1) * half]


def ring_put_tail(count, refs, k, rows, value):
    half = rows // 2
    value = value.astype(bf16)
    if count != 4:
        refs[0][k, :, MODEL_WIDTH:] = value
        return
    own, down, up, keep_down, keep_up = refs
    places = {
        0: ((own, 0), (own, half)),
        1: ((keep_down, 0), (down, half)),
        2: ((down, 0), (up, 0)),
        3: ((up, half), (keep_up, 0)),
    }
    for part, (ref, row) in enumerate(places[k]):
        ref[row : row + half, MODEL_WIDTH:] = value[part * half : (part + 1) * half]


def ring_get(count, refs, k, rows):
    if count != 4:
        return refs[0][k]
    half = rows // 2
    own, down, up, keep_down, keep_up = refs
    if k == 0:
        return own[...]
    first, second = {
        1: ((keep_down, 0), (down, half)),
        2: ((down, 0), (up, 0)),
        3: ((up, half), (keep_up, 0)),
    }[k]
    return jnp.concatenate([ref[row : row + half, :] for ref, row in (first, second)], axis=0)


class RingSum:
    def __init__(self, arrays, *earlier):
        self.plain = lax.axis_size("seq") != 4
        self.arrays = list(arrays)
        self.sent = ()
        if not self.plain:
            own, down, up, keep_down, keep_up = self.arrays
            if earlier:
                down, up = tie(down, *earlier), tie(up, *earlier)
            self.from_above = shift_permute(down, "seq", -1)
            self.from_below = shift_permute(up, "seq", 1)

    def near(self):
        return () if self.plain else (self.from_above, self.from_below)

    def parts(self, *earlier):
        if self.plain:
            count = lax.axis_size("seq")
            whole = jnp.take(self.arrays[0], (lax.axis_index("seq") - jnp.arange(count)) % count, axis=0)
            return [lax.psum_scatter(whole, "seq", scatter_dimension=0)]
        own, down, up, keep_down, keep_up = self.arrays
        half = keep_down.shape[0]
        if earlier:
            self.from_above = tie(self.from_above, *earlier)
            self.from_below = tie(self.from_below, *earlier)
        then_down = (keep_down.astype(f32) + self.from_above[:half].astype(f32)).astype(bf16)
        then_up = (keep_up.astype(f32) + self.from_below[:half].astype(f32)).astype(bf16)
        self.sent = (then_down, then_up)
        last_above = shift_permute(then_down, "seq", -1)
        last_below = shift_permute(then_up, "seq", 1)
        return [own, self.from_above, self.from_below, last_above, last_below]


def ring_total(refs):
    if len(refs) == 1:
        return refs[0][...].astype(f32)
    own, above, below, last_above, last_below = [r[...].astype(f32) for r in refs]
    half = own.shape[0] // 2
    first = own[:half] + below[half:] + last_above
    second = own[half:] + above[half:] + last_below
    return jnp.concatenate([first, second], axis=0)


def block_value(pieces, refs, k):
    found = [(row, ref) for (kk, row, _), ref in zip(pieces, refs) if kk == k]
    found.sort(key=lambda entry: entry[0])
    if len(found) == 1:
        return found[0][1][...]
    return jnp.concatenate([ref[...] for _, ref in found], axis=0)


def block_lanes(pieces, refs, k, lanes):
    found = [(row, ref) for (kk, row, _), ref in zip(pieces, refs) if kk == k]
    found.sort(key=lambda entry: entry[0])
    if len(found) == 1:
        return found[0][1][:, lanes]
    return jnp.concatenate([ref[:, lanes] for _, ref in found], axis=0)


def rotate_tile(tile, cosine, sine):
    first = lanes_of(tile.shape) % HEAD_SIZE < HEAD_SIZE // 2
    turned = jnp.where(first, pltpu.roll(tile, LANES - HEAD_SIZE // 2, 1), pltpu.roll(tile, HEAD_SIZE // 2, 1))
    return tile * cosine + turned * sine


def rotate_tile_back(tile, cosine, sine):
    return rotate_tile(tile, cosine, -sine)


def qkv_body(pieces, meta, x_ref, cos_ref, sin_ref, *refs):
    shards = refs[: len(pieces)]
    wq_ref, wkv_ref, wo_ref, extra_ref, normed_ref, q_ref, kv_ref, columns = refs[len(pieces) :]
    shard_rows = MODEL_WIDTH // max(r + 1 for r, _, _ in pieces)
    for (r, row, value), ref in zip(pieces, shards):
        rows = value.shape[0]
        place = pl.ds(pl.multiple_of(meta[r] * shard_rows + row, rows), rows)
        wq_ref[place, :] = ref[:, :MODEL_WIDTH]
        wkv_ref[place, :] = ref[:, MODEL_WIDTH : 2 * MODEL_WIDTH]
        wo_ref[place, :] = ref[:, 2 * MODEL_WIDTH : 3 * MODEL_WIDTH]
        columns[place, :] = ref[:, 3 * MODEL_WIDTH :].astype(f32)
    extra_ref[...] = columns[...].T
    source = x_ref[...].astype(f32)
    scale_inv = lax.rsqrt(jnp.mean(source * source, axis=-1, keepdims=True) + epsilon)
    normed = (source * scale_inv * extra_ref[EXPERTS : EXPERTS + 1, :]).astype(bf16)
    normed_ref[...] = normed
    cosine, sine = cos_ref[...], sin_ref[...]
    low = lanes_of(cosine.shape) < HEAD_SIZE
    for j in range(MODEL_WIDTH // TILE):
        block = dot_nn(normed, wq_ref[:, j * TILE : (j + 1) * TILE])
        for i in range(TILE // LANES):
            at = j * TILE + i * LANES
            tile = block[:, i * LANES : (i + 1) * LANES]
            q_ref[:, at : at + LANES] = rotate_tile(tile, cosine, sine).astype(bf16)
    for j in range(MODEL_WIDTH // TILE):
        block = dot_nn(normed, wkv_ref[:, j * TILE : (j + 1) * TILE])
        for i in range(TILE // LANES):
            at = j * TILE + i * LANES
            tile = block[:, i * LANES : (i + 1) * LANES]
            tile = jnp.where(low, rotate_tile(tile, cosine, sine), tile).astype(bf16)
            kv_ref[:, at : at + LANES] = tile


def causal_scores(keys, pair, k):
    scores = dot_nt(keys, pair)
    if k == 0:
        rows = keys.shape[0]
        query = lanes_of(scores.shape) % rows
        scores = jnp.where(query >= lax.broadcasted_iota(jnp.int32, scores.shape, 0), scores, -jnp.inf)
    return scores


def query_pair(tile):
    low = lanes_of(tile.shape) < HEAD_SIZE
    tile = tile.astype(f32) * att_scale
    even = jnp.where(low, tile, 0.0)
    odd = jnp.where(low, pltpu.roll(tile, HEAD_SIZE, 1), 0.0)
    return jnp.concatenate([even, odd], axis=0).astype(bf16)


def attend_body(count, pieces, meta, q_ref, x_ref, wo_ref, extra_ref, *refs):
    blocks = refs[: len(pieces)]
    a_ref, lse_ref, h_ref, normed_ref = refs[len(pieces) :]
    rows = q_ref.shape[0]
    place = meta[0]

    def variant(seen):
        def group(g, carry):
            lanes = aligned(g * LANES, LANES)
            pair = query_pair(q_ref[:, lanes])
            keys = [block_lanes(pieces, blocks, k, lanes) for k in range(seen)]
            scores = [causal_scores(keys[k], pair, k) for k in range(seen)]
            top = functools.reduce(jnp.maximum, [jnp.max(s, axis=0, keepdims=True) for s in scores])
            weights = [jnp.exp(s - top) for s in scores]
            total = functools.reduce(jnp.add, [jnp.sum(w, axis=0, keepdims=True) for w in weights])
            summed = functools.reduce(jnp.add, [dot_tn(t, w.astype(bf16)) for w, t in zip(weights, keys)])
            summed = summed[HEAD_SIZE:] * (1.0 / total)
            both = jnp.concatenate([summed[:, :rows], summed[:, rows:]], axis=0)
            a_ref[:, lanes] = both.T.astype(bf16)
            lse_ref[pl.ds(g, 1), :] = top + jnp.log(total)
            return carry

        lax.fori_loop(0, KEY_VALUE_HEADS, group, 0)

    for seen in range(1, count + 1):
        pl.when(place == seen - 1)(functools.partial(variant, seen))
    resid = x_ref[...].astype(f32) + res_scale * dot_nn(a_ref[...], wo_ref[...])
    h_ref[...] = resid
    scale_inv = lax.rsqrt(jnp.mean(resid * resid, axis=-1, keepdims=True) + epsilon)
    normed_ref[...] = (resid * scale_inv * extra_ref[EXPERTS + 1 : EXPERTS + 2, :]).astype(bf16)


def softmax_over(picked, logits, axis):
    top = jnp.max(jnp.where(picked, logits, -jnp.inf), axis=axis, keepdims=True)
    raised = jnp.where(picked, jnp.exp(jnp.minimum(logits - top, 0.0)), 0.0)
    return raised / jnp.sum(raised, axis=axis, keepdims=True)


def experts_body(count, shards, pieces, start, members, last, meta, extra_ref, *refs):
    refs = list(refs)

    def take(number):
        taken = refs[:number]
        del refs[:number]
        return taken

    (weights,) = take(1)
    blocks, (told,) = take(len(pieces)), take(1)
    if start > 0:
        (part_g, part_m) = take(2)
    keep_ref, send_ref = take(2) if last else (take(1) + [None])
    ring_count = len(ring_shapes(count, TILE, WIDE)) if last else 1
    mix_refs, ring_refs = take(ring_count), take(ring_count)
    up_s, down_s, x_s, c_s, ge_s, a_s, gu_s, d_s, eg_s, gs_s, gup_s, gdown_s, gate_s, rank_s, gg_s = refs
    step = pl.program_id(0)
    local = EXPERTS // count
    up_rows, down_rows = MODEL_WIDTH // shards, FF // shards
    slots = count * CAP
    place = meta[shards]
    expert = place * local + start + step

    def absolute(k):
        return lax.rem(place - k + count, count)

    @pl.when(step == 0)
    def routing():
        router = extra_ref[:EXPERTS, :].astype(bf16)
        later = (
            lax.broadcasted_iota(jnp.int32, (TILE, TILE), 0) < lax.broadcasted_iota(jnp.int32, (TILE, TILE), 1)
        )
        later = jnp.where(later, 1.0, 0.0).astype(bf16)
        names = lax.broadcasted_iota(jnp.int32, (EXPERTS, TILE), 0).astype(f32)
        for k in range(count):
            named = told[absolute(k), :, MODEL_WIDTH:].astype(f32).T
            picked = names == named[0:1, :]
            for j in range(1, TOP):
                picked = jnp.logical_or(picked, names == named[j : j + 1, :])
            logits = dot_nt(router, block_value(pieces, blocks, k))
            gate_s[k] = softmax_over(picked, logits, 0)
            before = dot_nn(jnp.where(picked, 1.0, 0.0).astype(bf16), later)
            rank_s[k] = jnp.where(picked, before, -1.0)
        gg_s[...] = jnp.zeros_like(gg_s)

    for r in range(shards):
        up_s[r * up_rows : (r + 1) * up_rows, :] = weights[r, 0, :up_rows, :]
        down_s[r * down_rows : (r + 1) * down_rows, :] = weights[r, 0, up_rows:, :]

    wanted = lax.broadcasted_iota(jnp.int32, (CAP, TILE), 0).astype(f32)
    held = aligned(step * CAP, CAP)
    gates = []
    for k in range(count):
        rank = rank_s[k, pl.ds(expert, 1), :]
        gate = gate_s[k, pl.ds(expert, 1), :]
        hit = wanted == rank
        chosen = jnp.where(hit, 1.0, 0.0).astype(bf16)
        d_s[k, held, :] = chosen
        here = slice(k * CAP, (k + 1) * CAP)
        x_s[here, :] = dot_nn(chosen, block_value(pieces, blocks, k)).astype(bf16)
        upstream = dot_nn(chosen, told[absolute(k), :, :MODEL_WIDTH])
        own_gate = jnp.sum(jnp.where(hit, gate, 0.0), axis=1, keepdims=True)
        gates.append(own_gate)
        c_s[here, :] = upstream.astype(bf16)
        ge_s[here, :] = (own_gate * (res_scale * upstream)).astype(bf16)

    for j in range(FF // TILE):
        left, right = slice(j * TILE, (j + 1) * TILE), slice(FF + j * TILE, FF + (j + 1) * TILE)
        gate_part = dot_nn(x_s[...], up_s[:, left])
        up_part = dot_nn(x_s[...], up_s[:, right])
        hidden_grad = dot_nt(ge_s[...], down_s[left, :])
        sigmoid_gate = jax.nn.sigmoid(gate_part)
        swish = gate_part * sigmoid_gate
        a_s[:, left] = (swish * up_part).astype(bf16)
        slope = sigmoid_gate * (1.0 + gate_part * (1.0 - sigmoid_gate))
        gu_s[:, left] = (hidden_grad * up_part * slope).astype(bf16)
        gu_s[:, right] = (hidden_grad * swish).astype(bf16)

    gate_grad = jnp.zeros((slots, 1), f32)
    for j in range(MODEL_WIDTH // TILE):
        columns = slice(j * TILE, (j + 1) * TILE)
        produced = dot_nn(a_s[...], down_s[:, columns]).astype(bf16).astype(f32)
        gate_grad += jnp.sum(res_scale * c_s[:, columns].astype(f32) * produced, axis=1, keepdims=True)
        input_grad = dot_nt(gu_s[...], up_s[columns, :]).astype(bf16)
        for k in range(count):
            here = slice(k * CAP, (k + 1) * CAP)
            eg_s[k, held, columns] = (gates[k] * produced[here]).astype(bf16)
            gs_s[k, held, columns] = input_grad[here]
    for k in range(count):
        hit = wanted == rank_s[k, pl.ds(expert, 1), :]
        spread = jnp.where(hit, gate_grad[k * CAP : (k + 1) * CAP], 0.0)
        gg_s[k, pl.ds(expert, 1), :] = jnp.sum(spread, axis=0, keepdims=True)

    for j in range(FF // TILE):
        rows = slice(j * TILE, (j + 1) * TILE)
        gdown_s[rows, :] = dot_tn(a_s[:, rows], ge_s[...]).astype(bf16)
    for j in range(MODEL_WIDTH // TILE):
        rows = slice(j * TILE, (j + 1) * TILE)
        gup_s[rows, :] = dot_tn(x_s[:, rows], gu_s[...]).astype(bf16)
    for r in range(shards):
        if last:
            ref, at, owner = (send_ref if r % 2 else keep_ref), r // 2, meta[r]
        else:
            ref, at, owner = keep_ref, r, r
        ref[at, 0, :up_rows, :] = gup_s[aligned(owner * up_rows, up_rows), :]
        ref[at, 0, up_rows:, :] = gdown_s[aligned(owner * down_rows, down_rows), :]

    @pl.when(step == members - 1)
    def combine():
        for k in range(count):
            spread = d_s[k]
            mixed = dot_tn(spread, eg_s[k])
            summed = dot_tn(spread, gs_s[k])
            exact = gg_s[k]
            rounded = exact.astype(bf16).astype(f32)
            rest = jnp.zeros((LANES - 2 * EXPERTS, TILE), f32)
            tail = jnp.concatenate([rounded, exact - rounded, rest], axis=0).T
            if start > 0:
                mixed += part_m[k].astype(f32)
                summed += part_g[k, :, :MODEL_WIDTH].astype(f32)
                tail += part_g[k, :, MODEL_WIDTH:].astype(f32)
            if last:
                ring_put(count, mix_refs, k, TILE, mixed)
                ring_put(count, ring_refs, k, TILE, summed)
                ring_put_tail(count, ring_refs, k, TILE, tail)
            else:
                mix_refs[0][k] = mixed.astype(bf16)
                ring_refs[0][k, :, :MODEL_WIDTH] = summed.astype(bf16)
                ring_refs[0][k, :, MODEL_WIDTH:] = tail.astype(bf16)


def backward_body(count, pieces, summed, meta, routes_ref, normed_ref, extra_ref, h_ref, c_ref, a_ref, wo_ref, q_ref, lse_ref, cos_ref, sin_ref, *refs):
    sums = refs[:summed]
    blocks = refs[summed : summed + len(pieces)]
    outs = refs[summed + len(pieces) :]
    gh_ref, go_ref, gpq_ref, gex_ref, gain_ref = outs[:5]
    ring_refs, ga_s = outs[5:-1], outs[-1]
    rows = q_ref.shape[0]
    place = meta[0]
    normed = normed_ref[...]
    total = ring_total(sums)
    normed_grad, tail = total[:, :MODEL_WIDTH], total[:, MODEL_WIDTH:]
    names = lanes_of((rows, LANES))
    named = routes_ref[...]
    picked = names == named[:, 0:1]
    for j in range(1, TOP):
        picked = jnp.logical_or(picked, names == named[:, j : j + 1])
    row_names = lax.broadcasted_iota(jnp.int32, (LANES, MODEL_WIDTH), 0)
    router = jnp.where(row_names < EXPERTS, extra_ref[...], 0.0).astype(bf16)
    gate = softmax_over(picked, dot_nt(normed, router), 1)
    gate_grad = jnp.where(picked, tail + pltpu.roll(tail, LANES - EXPERTS, 1), 0.0)
    inner = jnp.sum(gate * gate_grad, axis=1, keepdims=True)
    logit_grad = (gate * (gate_grad - inner)).astype(bf16)
    gex_ref[...] = dot_tn(normed, logit_grad)
    normed_grad += dot_nn(logit_grad, router)
    resid = h_ref[...]
    scale_inv = lax.rsqrt(jnp.mean(resid * resid, axis=-1, keepdims=True) + epsilon)
    hat = resid * scale_inv
    gain_ref[...] = jnp.broadcast_to(jnp.sum(normed_grad * hat, axis=0, keepdims=True), gain_ref.shape)
    scaled = normed_grad * extra_ref[EXPERTS + 1 : EXPERTS + 2, :]
    part = scale_inv * (scaled - hat * jnp.mean(scaled * hat, axis=-1, keepdims=True))
    resid_grad = c_ref[...].astype(f32) + part
    gh_ref[...] = resid_grad
    go = (res_scale * resid_grad).astype(bf16)
    go_ref[...] = go
    ga_s[...] = dot_nt(go, wo_ref[...]).astype(bf16)
    cosine, sine = cos_ref[...], sin_ref[...]
    low = lanes_of((rows, LANES)) < HEAD_SIZE

    def variant(seen):
        def group(g, carry):
            lanes = aligned(g * LANES, LANES)
            pair = query_pair(q_ref[:, lanes])
            upstream = ga_s[:, lanes].astype(f32)
            product = (upstream * a_ref[:, lanes].astype(f32)).T
            delta = jnp.concatenate(
                [
                    jnp.sum(product[:HEAD_SIZE], axis=0, keepdims=True),
                    jnp.sum(product[HEAD_SIZE:], axis=0, keepdims=True),
                ],
                axis=1,
            )
            logsum = lse_ref[pl.ds(g, 1), :]
            high_pair = jnp.concatenate(
                [jnp.where(low, 0.0, pltpu.roll(upstream, HEAD_SIZE, 1)), jnp.where(low, 0.0, upstream)], axis=0
            ).astype(bf16)
            query_grad = jnp.zeros((LANES, 2 * rows), f32)
            for k in range(seen):
                keys = block_lanes(pieces, blocks, k, lanes)
                weights = jnp.exp(causal_scores(keys, pair, k) - logsum)
                score_grad = (weights * (dot_nt(keys, high_pair) - delta)).astype(bf16)
                query_grad += dot_tn(keys, score_grad)
                back = dot_nn(score_grad, pair) + dot_nn(weights.astype(bf16), high_pair)
                put_lanes(k, lanes, back)
            query_grad = query_grad[:HEAD_SIZE] * att_scale
            tile = jnp.concatenate([query_grad[:, :rows], query_grad[:, rows:]], axis=0).T
            tile = tile.astype(bf16).astype(f32)
            gpq_ref[:, lanes] = rotate_tile_back(tile, cosine, sine).astype(bf16)
            return carry

        lax.fori_loop(0, KEY_VALUE_HEADS, group, 0)
        for k in range(seen, count):
            ring_put(count, ring_refs, k, rows, jnp.zeros((rows, MODEL_WIDTH), f32))

    def put_lanes(k, lanes, value):
        views = [r.at[..., lanes] for r in ring_refs]
        ring_put(count, views, k, rows, value)

    for seen in range(1, count + 1):
        pl.when(place == seen - 1)(functools.partial(variant, seen))


def store_sets(shards, meta, source, sets, columns):
    rows = MODEL_WIDTH // shards
    for r in range(shards):
        sets[r % 2][r // 2, :, columns] = source[aligned(meta[r] * rows, rows), :].astype(bf16)


def weights_body(count, shards, pieces, meta, a_ref, go_ref, gpq_ref, gex_ref, gain_ref, wq_ref, wkv_ref, extra_ref, cos_ref, sin_ref, *refs):
    blocks, parts = refs[: len(pieces)], refs[len(pieces) : -6]
    *sets, gp_s, normed_s, full_s, extra_s = refs[-6:]
    rows = gpq_ref.shape[0]
    low = lanes_of((rows, LANES)) < HEAD_SIZE
    for k in range(count):
        here = slice(k * rows, (k + 1) * rows)
        normed_s[here, :] = block_value(pieces, blocks, k)
        cosine, sine = cos_ref[k], sin_ref[k]
        part = ring_get(count, parts, k, rows).astype(f32)
        for j in range(MODEL_WIDTH // LANES):
            lanes = slice(j * LANES, (j + 1) * LANES)
            tile = part[:, lanes]
            gp_s[here, lanes] = jnp.where(low, rotate_tile_back(tile, cosine, sine), tile).astype(bf16)
    full_s[...] = dot_tn(normed_s[:rows, :], gpq_ref[...]).astype(bf16)
    store_sets(shards, meta, full_s, sets, slice(0, MODEL_WIDTH))
    full_s[...] = dot_tn(normed_s[...], gp_s[...]).astype(bf16)
    store_sets(shards, meta, full_s, sets, slice(MODEL_WIDTH, 2 * MODEL_WIDTH))
    full_s[...] = dot_tn(a_ref[...], go_ref[...]).astype(bf16)
    store_sets(shards, meta, full_s, sets, slice(2 * MODEL_WIDTH, 3 * MODEL_WIDTH))
    gain_grad = jnp.sum(dot_nt(gpq_ref[...], wq_ref[...]) * normed_s[:rows, :].astype(f32), axis=0, keepdims=True)
    for k in range(count):
        here = slice(k * rows, (k + 1) * rows)
        product = dot_nt(gp_s[here, :], wkv_ref[...]) * normed_s[here, :].astype(f32)
        gain_grad += jnp.sum(product, axis=0, keepdims=True)
    gain_grad = gain_grad / extra_ref[EXPERTS : EXPERTS + 1, :]
    row_names = lax.broadcasted_iota(jnp.int32, (LANES, MODEL_WIDTH), 0)
    gains = jnp.where(row_names == EXPERTS, gain_grad, jnp.where(row_names == EXPERTS + 1, gain_ref[0:1, :], 0.0))
    extra_s[...] = gex_ref[...] + gains.T
    store_sets(shards, meta, extra_s, sets, slice(3 * MODEL_WIDTH, 3 * MODEL_WIDTH + LANES))


def tokens_body(meta, x_ref, gpq_ref, wq_ref, wkv_ref, extra_ref, gh_ref, cos_ref, sin_ref, *refs):
    *sums, grad_ref, gpkv_s = refs
    total = ring_total(sums).astype(bf16).astype(f32)
    cosine, sine = cos_ref[...], sin_ref[...]
    low = lanes_of(cosine.shape) < HEAD_SIZE
    for j in range(MODEL_WIDTH // LANES):
        lanes = slice(j * LANES, (j + 1) * LANES)
        tile = total[:, lanes]
        gpkv_s[:, lanes] = jnp.where(low, rotate_tile_back(tile, cosine, sine), tile).astype(bf16)
    normed_grad = dot_nt(gpq_ref[...], wq_ref[...]) + dot_nt(gpkv_s[...], wkv_ref[...])
    source = x_ref[...].astype(f32)
    scale_inv = lax.rsqrt(jnp.mean(source * source, axis=-1, keepdims=True) + epsilon)
    hat = source * scale_inv
    scaled = normed_grad * extra_ref[EXPERTS : EXPERTS + 1, :]
    part = scale_inv * (scaled - hat * jnp.mean(scaled * hat, axis=-1, keepdims=True))
    grad_ref[...] = gh_ref[...] + part


def dense_update_body(count, rates, meta, *refs):
    quarters, refs = refs[:count], refs[count:]
    ins, outs, total_s = refs[:12], refs[12:28], refs[28]
    rows = quarters[0].shape[0]
    for k in range(count):
        at = lax.rem(meta[0] - k + count, count) * rows
        total_s[pl.ds(pl.multiple_of(at, rows), rows), :] = quarters[k][...].astype(f32)
    rest = total_s[:, 3 * MODEL_WIDTH :].T
    out = total_s[:, 2 * MODEL_WIDTH : 3 * MODEL_WIDTH]
    gradients = (rest[EXPERTS : EXPERTS + 2], total_s[:, : 2 * MODEL_WIDTH], out, rest[:EXPERTS])
    for i, (gradient, rate) in enumerate(zip(gradients, rates)):
        weight, first, second = [r[...] for r in ins[3 * i : 3 * i + 3]]
        for ref, value in zip(outs[4 * i : 4 * i + 4], (gradient, *adam_update(weight, gradient, first, second, rate))):
            ref[...] = value


def output_body(meta, h_ref, *refs):
    refs[-1][...] = (h_ref[...] + res_scale * ring_total(refs[:-1])).astype(bf16)


def experts_update_body(rates, rows, parts, rows_of, meta, *refs):
    gradient = rows_of(refs[:parts])
    ins, outs = refs[parts : parts + 6], refs[-8:]
    for i, rate in enumerate(rates):
        own = gradient[: rows[0]] if i == 0 else gradient[rows[0] :]
        weight, first, second = [r[0] for r in ins[3 * i : 3 * i + 3]]
        fresh, first, second = adam_update(weight, own, first, second, rate)
        for ref, value in zip(outs[4 * i : 4 * i + 4], (own, fresh, first, second)):
            ref[0] = value


def experts_update(start, share, arrays, rates, earlier, scalars, after=()):
    shares, share_specs, rows_of = share
    members = shares[0].shape[-3]
    rows = (arrays[0].shape[1], arrays[3].shape[1])

    def spec(a):
        return pl.BlockSpec((1,) + a.shape[1:], lambda e, m: (start + e, 0, 0))

    outs = [shape_of(a.shape, f32) for a in (arrays[0],) * 4 + (arrays[3],) * 4]
    in_specs = share_specs + [spec(a) for a in arrays]
    ins = shares + list(arrays)
    aliases = {}
    if earlier is not None:
        aliases = {1 + len(after) + len(ins) + i: i for i in range(8)}
        in_specs += [pl.BlockSpec(memory_space=pl.ANY)] * 8
        ins += list(earlier)
    return kernel_call(
        functools.partial(experts_update_body, rates, rows, len(shares), rows_of),
        outs,
        ins,
        scalars,
        grid=(members,),
        in_specs=in_specs,
        out_specs=[spec(a) for a in outs],
        micros=8,
        after=after,
        aliases=aliases,
    )


def angle_tables(rows, offsets):
    position = (offsets[:, None] + jnp.arange(rows)[None, :]).reshape(-1).astype(f32)
    frequency = 10000.0 ** (-(jnp.arange(HEAD_SIZE // 2).astype(f32) * 2.0 / HEAD_SIZE))
    angles = position[:, None] * frequency[None, :]
    cosine, sine = jnp.cos(angles), jnp.sin(angles)
    shape = (offsets.shape[0], rows, LANES)
    cosine = jnp.concatenate([cosine] * 4, axis=1).reshape(shape)
    return (cosine, jnp.concatenate([-sine, sine] * 2, axis=1).reshape(shape))


def shards_step(
    tokens,
    routes,
    cotangent,
    norm_gains,
    qkv_weight,
    out_weight,
    router_weight,
    expert_up,
    expert_down,
    mean_gains,
    square_gains,
    mean_qkv,
    square_qkv,
    mean_out,
    square_out,
    mean_router,
    square_router,
    mean_up,
    square_up,
    mean_down,
    square_down,
):
    rows = tokens.shape[1]
    count = lax.axis_size("seq")
    shards = lax.axis_size("fsdp")
    shard_rows = MODEL_WIDTH // shards
    local = EXPERTS // count
    early_experts = (5 * local + 4) // 8
    chunks = [(0, early_experts), (early_experts, local - early_experts)]
    place = lax.axis_index("seq").astype(jnp.int32)
    owners = (lax.axis_index("fsdp") ^ jnp.arange(shards)).astype(jnp.int32)
    owner_meta = jnp.concatenate([owners, place[None]])
    place_meta = place[None]
    x, c, own_routes = tokens[0], cotangent[0], routes[0]

    blank = jnp.zeros((shard_rows, LANES - EXPERTS - 2), f32)
    dense = jnp.concatenate([qkv_weight, out_weight, router_weight, norm_gains.T, blank], axis=1).astype(bf16)
    listed = jnp.zeros((rows, LANES), f32).at[:, :TOP].set(own_routes.astype(f32))
    dense_shards = Gathered(dense)
    told = lax.all_gather(jnp.concatenate([c, listed.astype(bf16)], axis=1), "seq", axis=0)
    dense_shards.forward()
    early = dense_shards.arrived()
    dense_pieces = dense_shards.pieces()
    expert_weights = []
    for start, members in chunks:
        mine = slice(start, start + members)
        packed = jnp.concatenate([expert_up[mine], expert_down[mine]], axis=1).astype(bf16)
        expert_weights.append(lax.all_gather(tie(packed, *early), "fsdp", axis=0))
    cosines, sines = angle_tables(rows, jnp.maximum(place - jnp.arange(count), 0) * rows)
    cosine, sine = cosines[0], sines[0]

    square = shape_of((MODEL_WIDTH, MODEL_WIDTH))
    wide = shape_of((rows, MODEL_WIDTH))
    wide_f = shape_of((rows, MODEL_WIDTH), f32)
    extra_shape = shape_of((LANES, MODEL_WIDTH), f32)
    unit = 2 * rows * MODEL_WIDTH * MODEL_WIDTH
    wq, wkv, wo, extra, normed_one, q, kv = kernel_call(
        functools.partial(qkv_body, dense_pieces),
        [square, square, square, extra_shape, wide, wide, wide],
        [x, cosine, sine] + [a for _, _, a in dense_pieces],
        owner_meta,
        scratch=[pltpu.VMEM((MODEL_WIDTH, LANES), f32)],
        micros=8,
    )
    kv_pieces = ring_gather(kv)
    attended, logsum, resid, normed_two = kernel_call(
        functools.partial(attend_body, count, kv_pieces),
        [wide, shape_of((KEY_VALUE_HEADS, 2 * rows), f32), wide_f, wide],
        [q, x, wo, extra] + [a for _, _, a in kv_pieces],
        place_meta,
        micros=12,
    )
    two_pieces = ring_gather(normed_two)

    slots = count * CAP
    packed_rows = (MODEL_WIDTH + FF) // shards
    part_g = part_m = None
    waited = (cosines, sines)
    normed_ring = Ringed(tie(normed_one, *[a for _, _, a in two_pieces[1:]]))
    for i, (start, members) in enumerate(chunks):
        last = i == len(chunks) - 1
        ins = [extra, expert_weights[i]] + [a for _, _, a in two_pieces] + [told]

        def still(a):
            return pl.BlockSpec(a.shape, functools.partial(lambda n, e, m: (0,) * n, a.ndim), pipeline_mode=pl.Buffered(1))

        all_spec = pl.BlockSpec((shards, 1, packed_rows, MODEL_WIDTH), lambda e, m: (0, e, 0, 0))
        set_spec = pl.BlockSpec((shards // 2, 1, packed_rows, MODEL_WIDTH), lambda e, m: (0, e, 0, 0))
        sets = [shape_of((shards // 2, members, packed_rows, MODEL_WIDTH))] * 2
        set_specs = [set_spec] * 2
        if not last:
            sets, set_specs = [shape_of((shards, members, packed_rows, MODEL_WIDTH))], [all_spec]
        in_specs = [still(extra), all_spec] + [still(a) for a in ins[2:]]
        if i > 0:
            ins += [part_g, part_m]
            in_specs += [still(part_g), still(part_m)]
        ring = ring_shapes if last else lambda n, r, w: [shape_of((n, r, w))]
        ring_count = len(ring(count, rows, WIDE))
        outs = sets + ring(count, rows, MODEL_WIDTH) + ring(count, rows, WIDE)
        out_specs = set_specs + [still(a) for a in outs[len(sets) :]]
        scratch = [
            pltpu.VMEM((MODEL_WIDTH, 2 * FF), bf16),
            pltpu.VMEM((FF, MODEL_WIDTH), bf16),
            pltpu.VMEM((slots, MODEL_WIDTH), bf16),
            pltpu.VMEM((slots, MODEL_WIDTH), bf16),
            pltpu.VMEM((slots, MODEL_WIDTH), bf16),
            pltpu.VMEM((slots, FF), bf16),
            pltpu.VMEM((slots, 2 * FF), bf16),
            pltpu.VMEM((count, members * CAP, rows), bf16),
            pltpu.VMEM((count, members * CAP, MODEL_WIDTH), bf16),
            pltpu.VMEM((count, members * CAP, MODEL_WIDTH), bf16),
            pltpu.VMEM((MODEL_WIDTH, 2 * FF), bf16),
            pltpu.VMEM((FF, MODEL_WIDTH), bf16),
            pltpu.VMEM((count, EXPERTS, rows), f32),
            pltpu.VMEM((count, EXPERTS, rows), f32),
            pltpu.VMEM((count, EXPERTS, rows), f32),
        ]
        results = kernel_call(
            functools.partial(experts_body, count, shards, two_pieces, start, members, last),
            outs,
            ins,
            owner_meta,
            scratch=scratch,
            grid=(members,),
            in_specs=in_specs,
            out_specs=out_specs,
            micros=8 * members,
            after=waited,
        )
        beside = normed_ring.forward() if last else normed_ring.near()
        results = list(results)
        first_part = len(sets)
        part_m, part_g = results[first_part], results[first_part + ring_count]
        mix_parts, ring_parts = results[first_part : first_part + ring_count], results[first_part + ring_count :]
        if not last:
            share = tie(results[0], *beside) if beside else results[0]
            share = lax.psum_scatter(share, "fsdp", scatter_dimension=0)

    two_ring = RingSum(ring_parts, *beside)
    late_sum = ScatteredExperts(tie(results[1], *beside, *two_ring.near()), results[0], place_meta)
    two_sums = two_ring.parts()
    sent = late_sum.first(*two_ring.sent)
    mixing = RingSum(mix_parts, *two_sums[3:], *sent)
    ring = ring_shapes(count, rows, MODEL_WIDTH)
    results = kernel_call(
        functools.partial(backward_body, count, kv_pieces, len(two_sums)),
        [wide_f, wide, wide, shape_of((MODEL_WIDTH, LANES), f32), shape_of((8, MODEL_WIDTH), f32)] + ring,
        [own_routes, normed_two, extra, resid, c, attended, wo, q, logsum, cosine, sine]
        + list(two_sums)
        + [a for _, _, a in kv_pieces],
        place_meta,
        scratch=[pltpu.VMEM((rows, MODEL_WIDTH), bf16)],
        micros=22,
    )
    resid_grad, go, gpq, router_grad, gain_grad = results[:5]
    mix_sums = mixing.parts()
    normed_pieces = normed_ring.pieces()
    dense_set = shape_of((shards // 2, shard_rows, 3 * MODEL_WIDTH + LANES))
    keep, send = kernel_call(
        functools.partial(weights_body, count, shards, normed_pieces),
        [dense_set] * 2,
        [attended, go, gpq, router_grad, gain_grad, wq, wkv, extra, cosines, sines]
        + [a for _, _, a in normed_pieces]
        + list(results[5:]),
        owner_meta,
        scratch=[
            pltpu.VMEM((count * rows, MODEL_WIDTH), bf16),
            pltpu.VMEM((count * rows, MODEL_WIDTH), bf16),
            pltpu.VMEM((MODEL_WIDTH, MODEL_WIDTH), bf16),
            pltpu.VMEM((MODEL_WIDTH, LANES), f32),
        ],
        after=mixing.near() + late_sum.arrived(),
        micros=12,
    )
    dense_sum = Scattered(place_meta)
    dense_sum.add(send, keep, *mix_sums[3:])
    rates = (learn_rates[4], learn_rates[5])
    experts = (expert_up, mean_up, square_up, expert_down, mean_down, square_down)
    sent = dense_sum.first()
    kv_ring = RingSum(results[5:], *mix_sums[3:])
    kv_sums = kv_ring.parts(*sent)
    spec = pl.BlockSpec((1,) + share.shape[1:], lambda e, m: (e, 0, 0))
    total = ([share], [spec], lambda refs: refs[0][0].astype(f32))
    dense_sum.second()
    own = dense_sum.total(*kv_sums[3:])
    updated = experts_update(chunks[0][0], total, experts, rates, None, place_meta, (own,))
    late_sum.second(own)
    quarters = own.reshape((count, shard_rows // count, own.shape[1]))
    quarters = lax.all_to_all(quarters, "seq", split_axis=0, concat_axis=0, tiled=True)
    (tokens_grad,) = kernel_call(
        tokens_body,
        [wide_f],
        [x, gpq, wq, wkv, extra, resid_grad, cosine, sine] + list(kv_sums),
        place_meta,
        scratch=[pltpu.VMEM((rows, MODEL_WIDTH), bf16)],
        after=(own,),
        micros=6,
    )
    (output,) = kernel_call(output_body, [wide], [resid] + mix_sums, place_meta, after=(own,), micros=3)
    quarter = jnp.sum(tie(quarters, tokens_grad, output, updated[0]).astype(f32), axis=0).astype(bf16)
    tokens_grad, output = tokens_grad[None], output[None]
    quarters = [quarter] + [shift_permute(quarter, "seq", k) for k in range(1, count)]
    updated = experts_update(chunks[1][0], late_sum.total(), experts, rates, updated, place_meta, (quarter,))
    dense_ins = [norm_gains, mean_gains, square_gains, qkv_weight, mean_qkv, square_qkv]
    dense_ins += [out_weight, mean_out, square_out, router_weight.T, mean_router.T, square_router.T]
    dense_outs = kernel_call(
        functools.partial(dense_update_body, count, learn_rates[:4]),
        [shape_of(a.shape, f32) for a in dense_ins[::3] for _ in range(4)],
        quarters + dense_ins,
        place_meta,
        scratch=[pltpu.VMEM((shard_rows, 3 * MODEL_WIDTH + LANES), f32)],
        after=(updated[0],),
        micros=5,
    )
    shard_gains, fresh_gains, momentum_gains, variance_gains = dense_outs[:4]
    shard_qkv, fresh_qkv, momentum_qkv, variance_qkv = dense_outs[4:8]
    shard_out, fresh_out, momentum_out, variance_out = dense_outs[8:12]
    shard_router, fresh_router, momentum_router, variance_router = [a.T for a in dense_outs[12:]]
    shard_up, fresh_up, momentum_up, variance_up = updated[:4]
    shard_down, fresh_down, momentum_down, variance_down = updated[4:]
    return (
        output,
        tokens_grad,
        shard_gains,
        shard_qkv,
        shard_out,
        shard_router,
        shard_up,
        shard_down,
        fresh_gains,
        fresh_qkv,
        fresh_out,
        fresh_router,
        fresh_up,
        fresh_down,
        momentum_gains,
        momentum_qkv,
        momentum_out,
        momentum_router,
        momentum_up,
        momentum_down,
        variance_gains,
        variance_qkv,
        variance_out,
        variance_router,
        variance_up,
        variance_down,
    )


def solution(mesh):
    block = P("fsdp", "seq", None)
    gains, dense, experts = P(None, "fsdp"), P("fsdp", None), P("seq", "fsdp", None)
    weights = (gains, dense, dense, dense, experts, experts)
    moments = tuple(s for spec in weights for s in (spec, spec))
    return jax.shard_map(
        shards_step,
        mesh=mesh,
        in_specs=(block, block, block) + weights + moments,
        out_specs=(block, block) + weights * 4,
        check_vma=False,
    )
```

```python
import functools

import jax
import jax.numpy as jnp
from jax import lax
from jax.experimental import pallas as pl
from jax.experimental.pallas import tpu as pltpu
from jax.sharding import PartitionSpec as P

MODEL_WIDTH = 1024
QUERY_HEADS = 16
KEY_VALUE_HEADS = 8
HEAD_SIZE = 64
EXPERTS = 32
FF = 512
TOP = 8
STEP = 3
CAP = 96
LANES = 128
TILE = 256

epsilon = 1e-06
res_scale = 0.22
att_scale = 0.015625
beta_one = 0.9
beta_two = 0.95
adam_eps = 1e-08
weight_decay = 0.1
learn_rates = (0.4, 0.04, 0.2, 0.01, 0.01, 0.05)

bf16 = jnp.bfloat16
f32 = jnp.float32
WIDE = MODEL_WIDTH + LANES


def adam_update(weight, gradient, first, second, rate):
    first_new = beta_one * first + (1.0 - beta_one) * gradient
    second_new = beta_two * second + (1.0 - beta_two) * gradient * gradient
    first_hat = first_new / (1.0 - beta_one**STEP)
    second_hat = second_new / (1.0 - beta_two**STEP)
    fresh = weight - rate * (first_hat / (jnp.sqrt(second_hat) + adam_eps) + weight_decay * weight)
    return (fresh, first_new, second_new)


def dot_nn(a, b):
    return lax.dot_general(a, b, (((1,), (0,)), ((), ())), preferred_element_type=f32)


def dot_nt(a, b):
    return lax.dot_general(a, b, (((1,), (1,)), ((), ())), preferred_element_type=f32)


def dot_tn(a, b):
    return lax.dot_general(a, b, (((0,), (0,)), ((), ())), preferred_element_type=f32)


def lanes_of(shape):
    return lax.broadcasted_iota(jnp.int32, shape, len(shape) - 1)


def aligned(index, size):
    if isinstance(index, int):
        return slice(index, index + size)
    return pl.ds(pl.multiple_of(index, size), size)


def kernel_call(body, outs, ins, scalars, scratch=(), grid=None, in_specs=None, out_specs=None, limit=60, after=(), micros=10, aliases=None, tables=()):
    in_specs = in_specs or [pl.BlockSpec(memory_space=pltpu.VMEM)] * len(ins)
    for a in tables:
        ins = list(ins) + [a]
        in_specs = in_specs + [pl.BlockSpec((1,) + a.shape[1:], lambda i, m: (0, 0, 0))]
    out_specs = out_specs or [pl.BlockSpec(memory_space=pltpu.VMEM)] * len(outs)
    in_specs = [pl.BlockSpec(memory_space=pl.ANY)] * len(after) + in_specs

    def ordered_body(meta, *refs):
        body(meta, *refs[len(after) :])

    return pl.pallas_call(
        ordered_body,
        out_shape=outs,
        grid_spec=pltpu.PrefetchScalarGridSpec(
            num_scalar_prefetch=1,
            grid=grid or (1,),
            in_specs=in_specs,
            out_specs=out_specs,
            scratch_shapes=list(scratch),
        ),
        compiler_params=pltpu.CompilerParams(vmem_limit_bytes=limit * 1024 * 1024),
        input_output_aliases=aliases or {},
        cost_estimate=pl.CostEstimate(flops=micros * 10**9, bytes_accessed=micros * 10**6, transcendentals=0),
    )(scalars, *after, *ins)


def tie(value, *earlier):
    anywhere = pl.BlockSpec(memory_space=pl.ANY)
    return pl.pallas_call(
        lambda *refs: None,
        out_shape=shape_of(value.shape, value.dtype),
        in_specs=[anywhere] * (1 + len(earlier)),
        out_specs=anywhere,
        input_output_aliases={0: 0},
    )(value, *earlier)


def shape_of(shape, kind=bf16):
    return jax.ShapeDtypeStruct(shape, kind)


def xor_permute(value, axis, mask):
    return lax.ppermute(value, axis, [(i, i ^ mask) for i in range(lax.axis_size(axis))])


def shift_permute(value, axis, step):
    size = lax.axis_size(axis)
    return lax.ppermute(value, axis, [(i, (i + step) % size) for i in range(size)])


class Gathered:
    def __init__(self, first, second):
        self.plain = lax.axis_size("fsdp") != 8
        self.first, self.second = first, second
        self.half = first.shape[0]
        if not self.plain:
            self.x_first = xor_permute(first, "fsdp", 2)
            self.y_second = xor_permute(second, "fsdp", 4)
            self.x_second = xor_permute(second, "fsdp", 2)
            self.y_first = xor_permute(first, "fsdp", 4)

    def forward(self, *earlier):
        if self.plain:
            return
        self.x_first = tie(self.x_first, *earlier)
        self.y_second = tie(self.y_second, *earlier)
        self.far_first = xor_permute(self.x_first, "fsdp", 4)
        self.far_second = xor_permute(self.y_second, "fsdp", 2)

    def arrived(self):
        return () if self.plain else (self.far_first, self.far_second)

    def pieces(self):
        count, half = lax.axis_size("fsdp"), self.half
        if self.plain:
            whole = lax.all_gather(jnp.concatenate([self.first, self.second]), "fsdp", axis=0)
            whole = jnp.take(whole, lax.axis_index("fsdp") ^ jnp.arange(count), axis=0)
            return [(r, 0, whole[r]) for r in range(count)]
        mine = [(0, 0, self.first), (0, half, self.second), (2, 0, self.x_first), (2, half, self.x_second)]
        mine += [(4, 0, self.y_first), (4, half, self.y_second), (6, 0, self.far_first), (6, half, self.far_second)]
        return mine + [(r + 1, row, xor_permute(a, "fsdp", 1)) for r, row, a in mine]


def pairs_body(groups, meta, *refs):
    sent_x, sent_y, rest = refs[2 * groups :]
    left = 0
    for keep, got in zip(refs[:groups], refs[groups : 2 * groups]):
        half, columns = keep.shape[1] // 2, keep.shape[2]
        lanes = slice(left, left + columns)
        left += columns

        def pair(i, part):
            piece = slice(part * half, (part + 1) * half)
            return (keep[i, piece, :].astype(f32) + got[i, piece, :].astype(f32)).astype(bf16)

        for ref, place, value in (
            (sent_x, 0, pair(3, 0)),
            (sent_x, 1, pair(1, 0)),
            (sent_y, 0, pair(3, 1)),
            (sent_y, 1, pair(2, 1)),
            (rest, 0, pair(0, 0)),
            (rest, 1, pair(0, 1)),
            (rest, 2, pair(1, 1)),
            (rest, 3, pair(2, 0)),
        ):
            ref[place, :, lanes] = value


def passed_body(meta, rest, over_x, over_y, then_x, then_y):
    then_x[...] = (rest[2].astype(f32) + over_y[0].astype(f32)).astype(bf16)
    then_y[...] = (rest[3].astype(f32) + over_x[0].astype(f32)).astype(bf16)


def summed_body(meta, rest, over_x, over_y, then_x, then_y, total):
    half = rest.shape[1]
    first = (rest[0].astype(f32) + over_x[1].astype(f32) + then_y[...].astype(f32)).astype(bf16)
    second = (rest[1].astype(f32) + over_y[1].astype(f32) + then_x[...].astype(f32)).astype(bf16)
    places, rows = total.shape[:2]
    for k in range(places):
        source, row = (first, k * rows) if k * rows < half else (second, k * rows - half)
        total[k] = source[row : row + rows]


class Scattered:
    def __init__(self, scalars):
        self.plain = lax.axis_size("fsdp") != 8
        self.scalars = scalars
        self.send, self.keep, self.got = [], [], []

    def add(self, send, keep, *earlier):
        self.send.append(send)
        self.keep.append(keep)
        if not self.plain:
            self.got.append(xor_permute(tie(send, *earlier) if earlier else send, "fsdp", 1))

    def first(self, *earlier):
        if self.plain:
            return ()
        rows, columns = self.keep[0].shape[1], sum(a.shape[2] for a in self.keep)
        two, four = shape_of((2, rows // 2, columns)), shape_of((4, rows // 2, columns))
        body = functools.partial(pairs_body, len(self.keep))
        sent_x, sent_y, self.rest = kernel_call(
            body, [two, two, four], self.keep + self.got, self.scalars, after=earlier, limit=24, micros=3
        )
        self.over_x = xor_permute(sent_x, "fsdp", 2)
        self.over_y = xor_permute(sent_y, "fsdp", 4)
        return (sent_x, sent_y)

    def second(self, *earlier):
        if self.plain:
            return ()
        one = shape_of(self.rest.shape[1:])
        ins = [self.rest, self.over_x, self.over_y]
        sent_x, sent_y = kernel_call(passed_body, [one, one], ins, self.scalars, after=earlier, limit=60, micros=2)
        self.then_x = xor_permute(sent_x, "fsdp", 2)
        self.then_y = xor_permute(sent_y, "fsdp", 4)
        return (sent_x, sent_y)

    def total(self, places, *earlier):
        if self.plain:
            count = lax.axis_size("fsdp")
            keep, send = jnp.concatenate(self.keep, axis=2), jnp.concatenate(self.send, axis=2)
            both = jnp.stack([keep, send], axis=1).reshape((count,) + keep.shape[1:])
            both = jnp.take(both, lax.axis_index("fsdp") ^ jnp.arange(count), axis=0)
            total = lax.psum_scatter(both, "fsdp", scatter_dimension=0)
            return total.reshape((places, -1, total.shape[1]))
        ins = [self.rest, self.over_x, self.over_y, self.then_x, self.then_y]
        outs = [shape_of((places, 2 * self.rest.shape[1] // places, self.rest.shape[2]))]
        return kernel_call(summed_body, outs, ins, self.scalars, after=earlier, limit=60, micros=2)[0]


def expert_pairs_body(meta, keep, got, sent_x, sent_y, rest):
    half = keep.shape[2] // 2

    def pair(i, part):
        piece = slice(part * half, (part + 1) * half)
        return (keep[i, 0, piece, :].astype(f32) + got[i, 0, piece, :].astype(f32)).astype(bf16)

    sent_x[0, 0], sent_x[1, 0] = pair(3, 0), pair(1, 0)
    sent_y[0, 0], sent_y[1, 0] = pair(3, 1), pair(2, 1)
    rest[0, 0], rest[1, 0], rest[2, 0], rest[3, 0] = pair(0, 0), pair(0, 1), pair(1, 1), pair(2, 0)


def expert_passed_body(meta, rest, over_x, over_y, then_x, then_y):
    then_x[0] = (rest[0, 0].astype(f32) + over_y[0, 0].astype(f32)).astype(bf16)
    then_y[0] = (rest[1, 0].astype(f32) + over_x[0, 0].astype(f32)).astype(bf16)


class ScatteredExperts:
    def __init__(self, send, keep, scalars):
        self.plain = lax.axis_size("fsdp") != 8
        self.send, self.keep, self.scalars = send, keep, scalars
        if not self.plain:
            self.got = xor_permute(send, "fsdp", 1)

    def first(self, *earlier):
        if self.plain:
            return ()
        sets, self.members, rows, columns = self.keep.shape
        half = rows // 2

        def group(n, start=0):
            return pl.BlockSpec((n, 1, half, columns), lambda e, m: (start, e, 0, 0))

        self.group = group
        self.single = pl.BlockSpec((1, half, columns), lambda e, m: (e, 0, 0))
        whole = pl.BlockSpec((sets, 1, rows, columns), lambda e, m: (0, e, 0, 0))
        shapes = [shape_of((n, self.members, half, columns)) for n in (2, 2, 4)]
        sent_x, sent_y, self.rest = kernel_call(
            expert_pairs_body,
            shapes,
            [self.keep, self.got],
            self.scalars,
            grid=(self.members,),
            in_specs=[whole, whole],
            out_specs=[group(2), group(2), group(4)],
            after=earlier,
            limit=60, micros=6,
        )
        self.sent = (sent_x, sent_y)
        return self.sent

    def depart(self, *earlier):
        if self.plain:
            return
        self.over_x = xor_permute(tie(self.sent[0], *earlier), "fsdp", 2)
        self.over_y = xor_permute(tie(self.sent[1], *earlier), "fsdp", 4)

    def arrived(self):
        return () if self.plain else (self.over_x, self.over_y)

    def second(self, *earlier):
        if self.plain:
            return ()
        one = shape_of(self.rest.shape[1:])
        sent_x, sent_y = kernel_call(
            expert_passed_body,
            [one, one],
            [self.rest, self.over_x, self.over_y],
            self.scalars,
            grid=(self.members,),
            in_specs=[self.group(2, 1), self.group(1), self.group(1)],
            out_specs=[self.single, self.single],
            after=earlier,
            limit=60, micros=4,
        )
        self.then_x = xor_permute(sent_x, "fsdp", 2)
        self.then_y = xor_permute(sent_y, "fsdp", 4)
        return (sent_x, sent_y)

    def total(self):
        if self.plain:
            count = lax.axis_size("fsdp")
            both = jnp.stack([self.keep, self.send], axis=1).reshape((count,) + self.keep.shape[1:])
            both = jnp.take(both, lax.axis_index("fsdp") ^ jnp.arange(count), axis=0)
            share = lax.psum_scatter(both, "fsdp", scatter_dimension=0)
            spec = pl.BlockSpec((1,) + share.shape[1:], lambda e, m: (e, 0, 0))
            return ([share], [spec], lambda refs: refs[0][0].astype(f32))
        arrays = [self.rest, self.over_x, self.over_y, self.then_x, self.then_y]
        specs = [self.group(2), self.group(1, 1), self.group(1, 1), self.single, self.single]

        def rows_of(refs):
            rest, over_x, over_y, then_x, then_y = refs
            first = rest[0, 0].astype(f32) + over_x[0, 0].astype(f32) + then_y[0].astype(f32)
            second = rest[1, 0].astype(f32) + over_y[0, 0].astype(f32) + then_x[0].astype(f32)
            return jnp.concatenate([first, second], axis=0)

        return (arrays, specs, rows_of)


class Ringed:
    def __init__(self, block):
        self.plain = lax.axis_size("seq") != 4
        self.block = block
        self.half = block.shape[0] // 2
        if not self.plain:
            self.below = shift_permute(block, "seq", 1)
            self.above = shift_permute(block, "seq", -1)

    def near(self):
        return () if self.plain else (self.below, self.above)

    def forward(self):
        if self.plain:
            return ()
        self.far_first = shift_permute(self.below[: self.half], "seq", 1)
        self.far_second = shift_permute(self.above[self.half :], "seq", -1)
        return (self.far_first, self.far_second)

    def pieces(self):
        count = lax.axis_size("seq")
        if self.plain:
            whole = lax.all_gather(self.block, "seq", axis=0)
            whole = jnp.take(whole, (lax.axis_index("seq") - jnp.arange(count)) % count, axis=0)
            return [(k, 0, whole[k]) for k in range(count)]
        pieces = [(0, 0, self.block), (1, 0, self.below), (3, 0, self.above)]
        return pieces + [(2, 0, self.far_first), (2, self.half, self.far_second)]


def ring_gather(block):
    ring = Ringed(block)
    ring.forward()
    return ring.pieces()


def ring_shapes(count, rows, columns):
    if count != 4:
        return [shape_of((count, rows, columns))]
    half = rows // 2
    return [shape_of((r, columns)) for r in (rows, rows, rows, half, half)]


def ring_put(count, refs, k, rows, value):
    half = rows // 2
    width = value.shape[1]
    value = value.astype(bf16)
    if count != 4:
        refs[0][k, :, :width] = value
        return
    own, down, up, keep_down, keep_up = refs
    places = {
        0: ((own, 0), (own, half)),
        1: ((keep_down, 0), (down, half)),
        2: ((down, 0), (up, 0)),
        3: ((up, half), (keep_up, 0)),
    }
    for part, (ref, row) in enumerate(places[k]):
        ref[row : row + half, :width] = value[part * half : (part + 1) * half]


def ring_put_tail(count, refs, k, rows, value):
    half = rows // 2
    value = value.astype(bf16)
    if count != 4:
        refs[0][k, :, MODEL_WIDTH:] = value
        return
    own, down, up, keep_down, keep_up = refs
    places = {
        0: ((own, 0), (own, half)),
        1: ((keep_down, 0), (down, half)),
        2: ((down, 0), (up, 0)),
        3: ((up, half), (keep_up, 0)),
    }
    for part, (ref, row) in enumerate(places[k]):
        ref[row : row + half, MODEL_WIDTH:] = value[part * half : (part + 1) * half]


def ring_get(count, refs, k, rows):
    if count != 4:
        return refs[0][k]
    half = rows // 2
    own, down, up, keep_down, keep_up = refs
    if k == 0:
        return own[...]
    first, second = {
        1: ((keep_down, 0), (down, half)),
        2: ((down, 0), (up, 0)),
        3: ((up, half), (keep_up, 0)),
    }[k]
    return jnp.concatenate([ref[row : row + half, :] for ref, row in (first, second)], axis=0)


class RingSum:
    def __init__(self, arrays, *earlier):
        self.plain = lax.axis_size("seq") != 4
        self.arrays = list(arrays)
        self.sent = ()
        if not self.plain:
            own, down, up, keep_down, keep_up = self.arrays
            if earlier:
                down, up = tie(down, *earlier), tie(up, *earlier)
            self.from_above = shift_permute(down, "seq", -1)
            self.from_below = shift_permute(up, "seq", 1)

    def near(self):
        return () if self.plain else (self.from_above, self.from_below)

    def parts(self, *earlier):
        if self.plain:
            count = lax.axis_size("seq")
            whole = jnp.take(self.arrays[0], (lax.axis_index("seq") - jnp.arange(count)) % count, axis=0)
            return [lax.psum_scatter(whole, "seq", scatter_dimension=0)]
        own, down, up, keep_down, keep_up = self.arrays
        half = keep_down.shape[0]
        if earlier:
            self.from_above = tie(self.from_above, *earlier)
            self.from_below = tie(self.from_below, *earlier)
        then_down = (keep_down.astype(f32) + self.from_above[:half].astype(f32)).astype(bf16)
        then_up = (keep_up.astype(f32) + self.from_below[:half].astype(f32)).astype(bf16)
        self.sent = (then_down, then_up)
        last_above = shift_permute(then_down, "seq", -1)
        last_below = shift_permute(then_up, "seq", 1)
        return [own, self.from_above, self.from_below, last_above, last_below]


def ring_total(refs):
    if len(refs) == 1:
        return refs[0][...].astype(f32)
    own, above, below, last_above, last_below = [r[...].astype(f32) for r in refs]
    half = own.shape[0] // 2
    first = own[:half] + below[half:] + last_above
    second = own[half:] + above[half:] + last_below
    return jnp.concatenate([first, second], axis=0)


def block_value(pieces, refs, k):
    found = [(row, ref) for (kk, row, _), ref in zip(pieces, refs) if kk == k]
    found.sort(key=lambda entry: entry[0])
    if len(found) == 1:
        return found[0][1][...]
    return jnp.concatenate([ref[...] for _, ref in found], axis=0)


def block_lanes(pieces, refs, k, lanes):
    found = [(row, ref) for (kk, row, _), ref in zip(pieces, refs) if kk == k]
    found.sort(key=lambda entry: entry[0])
    if len(found) == 1:
        return found[0][1][:, lanes]
    return jnp.concatenate([ref[:, lanes] for _, ref in found], axis=0)


def rotate_tile(tile, cosine, sine):
    first = lanes_of(tile.shape) % HEAD_SIZE < HEAD_SIZE // 2
    turned = jnp.where(first, pltpu.roll(tile, LANES - HEAD_SIZE // 2, 1), pltpu.roll(tile, HEAD_SIZE // 2, 1))
    return tile * cosine + turned * sine


def rotate_tile_back(tile, cosine, sine):
    return rotate_tile(tile, cosine, -sine)


def qkv_body(pieces, meta, x_ref, *refs):
    shards = refs[: len(pieces)]
    cos_ref, sin_ref, *refs = refs[len(pieces) :]
    wq_ref, wkv_ref, wo_ref, extra_ref, normed_ref, q_ref, kv_ref, columns = refs
    shard_rows = MODEL_WIDTH // max(r + 1 for r, _, _ in pieces)
    for (r, row, value), ref in zip(pieces, shards):
        rows = value.shape[0]
        place = pl.ds(pl.multiple_of(meta[r] * shard_rows + row, rows), rows)
        wq_ref[place, :] = ref[:, :MODEL_WIDTH]
        wkv_ref[place, :] = ref[:, MODEL_WIDTH : 2 * MODEL_WIDTH]
        wo_ref[place, :] = ref[:, 2 * MODEL_WIDTH : 3 * MODEL_WIDTH]
        columns[place, :] = ref[:, 3 * MODEL_WIDTH :].astype(f32)
    extra_ref[...] = columns[...].T
    source = x_ref[...].astype(f32)
    scale_inv = lax.rsqrt(jnp.mean(source * source, axis=-1, keepdims=True) + epsilon)
    normed = (source * scale_inv * extra_ref[EXPERTS : EXPERTS + 1, :]).astype(bf16)
    normed_ref[...] = normed
    cosine, sine = cos_ref[0], sin_ref[0]
    low = lanes_of(cosine.shape) < HEAD_SIZE
    for j in range(MODEL_WIDTH // TILE):
        block = dot_nn(normed, wq_ref[:, j * TILE : (j + 1) * TILE])
        for i in range(TILE // LANES):
            at = j * TILE + i * LANES
            tile = block[:, i * LANES : (i + 1) * LANES]
            q_ref[:, at : at + LANES] = rotate_tile(tile, cosine, sine).astype(bf16)
    for j in range(MODEL_WIDTH // TILE):
        block = dot_nn(normed, wkv_ref[:, j * TILE : (j + 1) * TILE])
        for i in range(TILE // LANES):
            at = j * TILE + i * LANES
            tile = block[:, i * LANES : (i + 1) * LANES]
            tile = jnp.where(low, rotate_tile(tile, cosine, sine), tile).astype(bf16)
            kv_ref[:, at : at + LANES] = tile


def causal_scores(keys, pair, k):
    scores = dot_nt(keys, pair)
    if k == 0:
        rows = keys.shape[0]
        query = lanes_of(scores.shape) % rows
        scores = jnp.where(query >= lax.broadcasted_iota(jnp.int32, scores.shape, 0), scores, -jnp.inf)
    return scores


def query_pair(tile):
    low = lanes_of(tile.shape) < HEAD_SIZE
    tile = tile.astype(f32) * att_scale
    even = jnp.where(low, tile, 0.0)
    odd = jnp.where(low, pltpu.roll(tile, HEAD_SIZE, 1), 0.0)
    return jnp.concatenate([even, odd], axis=0).astype(bf16)


def attend_body(count, pieces, meta, q_ref, x_ref, wo_ref, extra_ref, *refs):
    blocks = refs[: len(pieces)]
    a_ref, lse_ref, h_ref, normed_ref = refs[len(pieces) :]
    rows = q_ref.shape[0]
    place = meta[0]

    def variant(seen):
        def group(g, carry):
            lanes = aligned(g * LANES, LANES)
            pair = query_pair(q_ref[:, lanes])
            keys = [block_lanes(pieces, blocks, k, lanes) for k in range(seen)]
            scores = [causal_scores(keys[k], pair, k) for k in range(seen)]
            top = functools.reduce(jnp.maximum, [jnp.max(s, axis=0, keepdims=True) for s in scores])
            weights = [jnp.exp(s - top) for s in scores]
            total = functools.reduce(jnp.add, [jnp.sum(w, axis=0, keepdims=True) for w in weights])
            summed = functools.reduce(jnp.add, [dot_tn(t, w.astype(bf16)) for w, t in zip(weights, keys)])
            summed = summed[HEAD_SIZE:] * (1.0 / total)
            both = jnp.concatenate([summed[:, :rows], summed[:, rows:]], axis=0)
            a_ref[:, lanes] = both.T.astype(bf16)
            lse_ref[pl.ds(g, 1), :] = top + jnp.log(total)
            return carry

        lax.fori_loop(0, KEY_VALUE_HEADS, group, 0)

    for seen in range(1, count + 1):
        pl.when(place == seen - 1)(functools.partial(variant, seen))
    resid = x_ref[...].astype(f32) + res_scale * dot_nn(a_ref[...], wo_ref[...])
    h_ref[...] = resid
    scale_inv = lax.rsqrt(jnp.mean(resid * resid, axis=-1, keepdims=True) + epsilon)
    normed_ref[...] = (resid * scale_inv * extra_ref[EXPERTS + 1 : EXPERTS + 2, :]).astype(bf16)


def softmax_over(picked, logits, axis):
    top = jnp.max(jnp.where(picked, logits, -jnp.inf), axis=axis, keepdims=True)
    raised = jnp.where(picked, jnp.exp(jnp.minimum(logits - top, 0.0)), 0.0)
    return raised / jnp.sum(raised, axis=axis, keepdims=True)


def experts_body(count, shards, pieces, start, members, last, meta, extra_ref, *refs):
    refs = list(refs)

    def take(number):
        taken = refs[:number]
        del refs[:number]
        return taken

    up_w, down_w = take(2)
    blocks, (told,), listed = take(len(pieces)), take(1), take(count)
    if start > 0:
        (part_g, part_m) = take(2)
    keep_ref, send_ref = take(2) if last else (take(1) + [None])
    ring_count = len(ring_shapes(count, TILE, WIDE)) if last else 1
    mix_refs, ring_refs = take(ring_count), take(ring_count)
    x_s, c_s, ge_s, a_s, gu_s, d_s, eg_s, gs_s, gup_s, gdown_s, gate_s, rank_s, gg_s = refs
    step = pl.program_id(0)
    local = EXPERTS // count
    up_rows, down_rows = MODEL_WIDTH // shards, FF // shards
    slots = count * CAP
    place = meta[shards]
    expert = place * local + start + step

    def absolute(k):
        return lax.rem(place - k + count, count)

    @pl.when(step == 0)
    def routing():
        router = extra_ref[:EXPERTS, :].astype(bf16)
        later = (
            lax.broadcasted_iota(jnp.int32, (TILE, TILE), 0) < lax.broadcasted_iota(jnp.int32, (TILE, TILE), 1)
        )
        later = jnp.where(later, 1.0, 0.0).astype(bf16)
        names = lax.broadcasted_iota(jnp.int32, (EXPERTS, TILE), 0).astype(f32)
        for k in range(count):
            named = listed[k][...].astype(f32)
            picked = names == named[0:1, :]
            for j in range(1, TOP):
                picked = jnp.logical_or(picked, names == named[j : j + 1, :])
            logits = dot_nt(router, block_value(pieces, blocks, k))
            gate_s[k] = softmax_over(picked, logits, 0)
            before = dot_nn(jnp.where(picked, 1.0, 0.0).astype(bf16), later)
            rank_s[k] = jnp.where(picked, before, -1.0)
        gg_s[...] = jnp.zeros_like(gg_s)

    def up_columns(columns):
        return up_w[:, 0, :, columns].reshape(MODEL_WIDTH, TILE)

    def up_tile(j):
        here = slice(j * TILE // up_rows, (j + 1) * TILE // up_rows)
        return up_w[here, 0, :, :].reshape(TILE, 2 * FF)

    def down_columns(columns):
        return down_w[:, 0, :, columns].reshape(FF, TILE)

    def down_tile(j):
        here = slice(j * TILE // down_rows, (j + 1) * TILE // down_rows)
        return down_w[here, 0, :, :].reshape(TILE, MODEL_WIDTH)

    wanted = lax.broadcasted_iota(jnp.int32, (CAP, TILE), 0).astype(f32)
    held = aligned(step * CAP, CAP)
    gates = []
    for k in range(count):
        rank = rank_s[k, pl.ds(expert, 1), :]
        gate = gate_s[k, pl.ds(expert, 1), :]
        hit = wanted == rank
        chosen = jnp.where(hit, 1.0, 0.0).astype(bf16)
        d_s[k, held, :] = chosen
        here = slice(k * CAP, (k + 1) * CAP)
        x_s[here, :] = dot_nn(chosen, block_value(pieces, blocks, k)).astype(bf16)
        upstream = dot_nn(chosen, told[absolute(k)])
        own_gate = jnp.sum(jnp.where(hit, gate, 0.0), axis=1, keepdims=True)
        gates.append(own_gate)
        c_s[here, :] = upstream.astype(bf16)
        ge_s[here, :] = (own_gate * (res_scale * upstream)).astype(bf16)

    for j in range(FF // TILE):
        left, right = slice(j * TILE, (j + 1) * TILE), slice(FF + j * TILE, FF + (j + 1) * TILE)
        gate_part = dot_nn(x_s[...], up_columns(left))
        up_part = dot_nn(x_s[...], up_columns(right))
        hidden_grad = dot_nt(ge_s[...], down_tile(j))
        sigmoid_gate = jax.nn.sigmoid(gate_part)
        swish = gate_part * sigmoid_gate
        a_s[:, left] = (swish * up_part).astype(bf16)
        slope = sigmoid_gate * (1.0 + gate_part * (1.0 - sigmoid_gate))
        gu_s[:, left] = (hidden_grad * up_part * slope).astype(bf16)
        gu_s[:, right] = (hidden_grad * swish).astype(bf16)

    gate_grad = jnp.zeros((slots, 1), f32)
    for j in range(MODEL_WIDTH // TILE):
        columns = slice(j * TILE, (j + 1) * TILE)
        produced = dot_nn(a_s[...], down_columns(columns)).astype(bf16).astype(f32)
        gate_grad += jnp.sum(res_scale * c_s[:, columns].astype(f32) * produced, axis=1, keepdims=True)
        input_grad = dot_nt(gu_s[...], up_tile(j)).astype(bf16)
        for k in range(count):
            here = slice(k * CAP, (k + 1) * CAP)
            eg_s[k, held, columns] = (gates[k] * produced[here]).astype(bf16)
            gs_s[k, held, columns] = input_grad[here]
    for k in range(count):
        hit = wanted == rank_s[k, pl.ds(expert, 1), :]
        spread = jnp.where(hit, gate_grad[k * CAP : (k + 1) * CAP], 0.0)
        gg_s[k, pl.ds(expert, 1), :] = jnp.sum(spread, axis=0, keepdims=True)

    for j in range(FF // TILE):
        rows = slice(j * TILE, (j + 1) * TILE)
        tile = dot_tn(a_s[:, rows], ge_s[...]).astype(bf16)
        if last:
            gdown_s[rows, :] = tile
        else:
            here = slice(j * TILE // down_rows, (j + 1) * TILE // down_rows)
            keep_ref[here, 0, up_rows:, :] = tile.reshape(TILE // down_rows, down_rows, MODEL_WIDTH)
    for j in range(MODEL_WIDTH // TILE):
        rows = slice(j * TILE, (j + 1) * TILE)
        tile = dot_tn(x_s[:, rows], gu_s[...]).astype(bf16)
        if last:
            gup_s[rows, :] = tile
        else:
            here = slice(j * TILE // up_rows, (j + 1) * TILE // up_rows)
            keep_ref[here, 0, :up_rows, :] = tile.reshape(TILE // up_rows, up_rows, 2 * FF)
    if last:
        for r in range(shards):
            ref = send_ref if r % 2 else keep_ref
            ref[r // 2, 0, :up_rows, :] = gup_s[aligned(meta[r] * up_rows, up_rows), :]
            ref[r // 2, 0, up_rows:, :] = gdown_s[aligned(meta[r] * down_rows, down_rows), :]

    @pl.when(step == members - 1)
    def combine():
        for k in range(count):
            spread = d_s[k]
            mixed = dot_tn(spread, eg_s[k])
            summed = dot_tn(spread, gs_s[k])
            exact = gg_s[k]
            rounded = exact.astype(bf16).astype(f32)
            rest = jnp.zeros((LANES - 2 * EXPERTS, TILE), f32)
            tail = jnp.concatenate([rounded, exact - rounded, rest], axis=0).T
            if start > 0:
                mixed += part_m[k].astype(f32)
                summed += part_g[k, :, :MODEL_WIDTH].astype(f32)
                tail += part_g[k, :, MODEL_WIDTH:].astype(f32)
            if last:
                ring_put(count, mix_refs, k, TILE, mixed)
                ring_put(count, ring_refs, k, TILE, summed)
                ring_put_tail(count, ring_refs, k, TILE, tail)
            else:
                mix_refs[0][k] = mixed.astype(bf16)
                ring_refs[0][k, :, :MODEL_WIDTH] = summed.astype(bf16)
                ring_refs[0][k, :, MODEL_WIDTH:] = tail.astype(bf16)


def backward_body(count, pieces, summed, meta, routes_ref, normed_ref, extra_ref, h_ref, c_ref, a_ref, wo_ref, q_ref, lse_ref, *refs):
    sums = refs[:summed]
    blocks = refs[summed : summed + len(pieces)]
    cos_ref, sin_ref, *outs = refs[summed + len(pieces) :]
    gh_ref, go_ref, gpq_ref, gex_ref, gain_ref = outs[:5]
    ring_refs, ga_s = outs[5:-1], outs[-1]
    rows = q_ref.shape[0]
    place = meta[0]
    normed = normed_ref[...]
    total = ring_total(sums)
    normed_grad, tail = total[:, :MODEL_WIDTH], total[:, MODEL_WIDTH:]
    names = lanes_of((rows, LANES))
    named = routes_ref[...]
    picked = names == named[:, 0:1]
    for j in range(1, TOP):
        picked = jnp.logical_or(picked, names == named[:, j : j + 1])
    row_names = lax.broadcasted_iota(jnp.int32, (LANES, MODEL_WIDTH), 0)
    router = jnp.where(row_names < EXPERTS, extra_ref[...], 0.0).astype(bf16)
    gate = softmax_over(picked, dot_nt(normed, router), 1)
    gate_grad = jnp.where(picked, tail + pltpu.roll(tail, LANES - EXPERTS, 1), 0.0)
    inner = jnp.sum(gate * gate_grad, axis=1, keepdims=True)
    logit_grad = (gate * (gate_grad - inner)).astype(bf16)
    gex_ref[...] = dot_tn(normed, logit_grad)
    normed_grad += dot_nn(logit_grad, router)
    resid = h_ref[...]
    scale_inv = lax.rsqrt(jnp.mean(resid * resid, axis=-1, keepdims=True) + epsilon)
    hat = resid * scale_inv
    gain_ref[...] = jnp.broadcast_to(jnp.sum(normed_grad * hat, axis=0, keepdims=True), gain_ref.shape)
    scaled = normed_grad * extra_ref[EXPERTS + 1 : EXPERTS + 2, :]
    part = scale_inv * (scaled - hat * jnp.mean(scaled * hat, axis=-1, keepdims=True))
    resid_grad = c_ref[...].astype(f32) + part
    gh_ref[...] = resid_grad
    go = (res_scale * resid_grad).astype(bf16)
    go_ref[...] = go
    ga_s[...] = dot_nt(go, wo_ref[...]).astype(bf16)
    cosine, sine = cos_ref[0], sin_ref[0]
    low = lanes_of((rows, LANES)) < HEAD_SIZE

    def variant(seen):
        def group(g, carry):
            lanes = aligned(g * LANES, LANES)
            pair = query_pair(q_ref[:, lanes])
            upstream = ga_s[:, lanes].astype(f32)
            product = (upstream * a_ref[:, lanes].astype(f32)).T
            delta = jnp.concatenate(
                [
                    jnp.sum(product[:HEAD_SIZE], axis=0, keepdims=True),
                    jnp.sum(product[HEAD_SIZE:], axis=0, keepdims=True),
                ],
                axis=1,
            )
            logsum = lse_ref[pl.ds(g, 1), :]
            high_pair = jnp.concatenate(
                [jnp.where(low, 0.0, pltpu.roll(upstream, HEAD_SIZE, 1)), jnp.where(low, 0.0, upstream)], axis=0
            ).astype(bf16)
            query_grad = jnp.zeros((LANES, 2 * rows), f32)
            for k in range(seen):
                keys = block_lanes(pieces, blocks, k, lanes)
                weights = jnp.exp(causal_scores(keys, pair, k) - logsum)
                score_grad = (weights * (dot_nt(keys, high_pair) - delta)).astype(bf16)
                query_grad += dot_tn(keys, score_grad)
                back = dot_nn(score_grad, pair) + dot_nn(weights.astype(bf16), high_pair)
                put_lanes(k, lanes, back)
            query_grad = query_grad[:HEAD_SIZE] * att_scale
            tile = jnp.concatenate([query_grad[:, :rows], query_grad[:, rows:]], axis=0).T
            tile = tile.astype(bf16).astype(f32)
            gpq_ref[:, lanes] = rotate_tile_back(tile, cosine, sine).astype(bf16)
            return carry

        lax.fori_loop(0, KEY_VALUE_HEADS, group, 0)
        for k in range(seen, count):
            ring_put(count, ring_refs, k, rows, jnp.zeros((rows, MODEL_WIDTH), f32))

    def put_lanes(k, lanes, value):
        views = [r.at[..., lanes] for r in ring_refs]
        ring_put(count, views, k, rows, value)

    for seen in range(1, count + 1):
        pl.when(place == seen - 1)(functools.partial(variant, seen))


def store_sets(shards, meta, source, sets, columns):
    rows = MODEL_WIDTH // shards
    for r in range(shards):
        sets[r % 2][r // 2, :, columns] = source[aligned(meta[r] * rows, rows), :].astype(bf16)


def weights_body(count, shards, pieces, meta, a_ref, go_ref, gpq_ref, gex_ref, gain_ref, cos_ref, sin_ref, *refs):
    blocks, parts = refs[: len(pieces)], refs[len(pieces) : -6]
    *sets, gp_s, normed_s, full_s, extra_s = refs[-6:]
    rows = gpq_ref.shape[0]
    low = lanes_of((rows, LANES)) < HEAD_SIZE
    for k in range(count):
        here = slice(k * rows, (k + 1) * rows)
        normed_s[here, :] = block_value(pieces, blocks, k)
        cosine, sine = cos_ref[k], sin_ref[k]
        part = ring_get(count, parts, k, rows).astype(f32)
        for j in range(MODEL_WIDTH // LANES):
            lanes = slice(j * LANES, (j + 1) * LANES)
            tile = part[:, lanes]
            gp_s[here, lanes] = jnp.where(low, rotate_tile_back(tile, cosine, sine), tile).astype(bf16)
    full_s[...] = dot_tn(normed_s[:rows, :], gpq_ref[...]).astype(bf16)
    store_sets(shards, meta, full_s, sets, slice(0, MODEL_WIDTH))
    full_s[...] = dot_tn(normed_s[...], gp_s[...]).astype(bf16)
    store_sets(shards, meta, full_s, sets, slice(MODEL_WIDTH, 2 * MODEL_WIDTH))
    full_s[...] = dot_tn(a_ref[...], go_ref[...]).astype(bf16)
    store_sets(shards, meta, full_s, sets, slice(2 * MODEL_WIDTH, 3 * MODEL_WIDTH))
    row_names = lax.broadcasted_iota(jnp.int32, (LANES, MODEL_WIDTH), 0)
    gains = jnp.where(row_names == EXPERTS + 1, gain_ref[0:1, :], 0.0)
    extra_s[...] = gex_ref[...] + gains.T
    store_sets(shards, meta, extra_s, sets, slice(3 * MODEL_WIDTH, 3 * MODEL_WIDTH + LANES))


def tokens_body(meta, x_ref, gpq_ref, wq_ref, wkv_ref, extra_ref, gh_ref, *refs):
    *sums, cos_ref, sin_ref, grad_ref, gpkv_s = refs
    total = ring_total(sums).astype(bf16).astype(f32)
    cosine, sine = cos_ref[0], sin_ref[0]
    low = lanes_of(cosine.shape) < HEAD_SIZE
    for j in range(MODEL_WIDTH // LANES):
        lanes = slice(j * LANES, (j + 1) * LANES)
        tile = total[:, lanes]
        gpkv_s[:, lanes] = jnp.where(low, rotate_tile_back(tile, cosine, sine), tile).astype(bf16)
    normed_grad = dot_nt(gpq_ref[...], wq_ref[...]) + dot_nt(gpkv_s[...], wkv_ref[...])
    source = x_ref[...].astype(f32)
    scale_inv = lax.rsqrt(jnp.mean(source * source, axis=-1, keepdims=True) + epsilon)
    hat = source * scale_inv
    scaled = normed_grad * extra_ref[EXPERTS : EXPERTS + 1, :]
    part = scale_inv * (scaled - hat * jnp.mean(scaled * hat, axis=-1, keepdims=True))
    grad_ref[...] = gh_ref[...] + part


def dense_update_body(count, rates, meta, *refs):
    quarters, refs = refs[:count], refs[count:]
    ins, outs, rest_s, gain_s = refs[:12], refs[12:28], refs[28], refs[29]
    rows = quarters[0].shape[0]
    step = pl.program_id(0)

    def update(i, gradient):
        weight, first, second = [r[...] for r in ins[3 * i : 3 * i + 3]]
        values = (gradient, *adam_update(weight, gradient, first, second, rates[i]))
        for ref, value in zip(outs[4 * i : 4 * i + 4], values):
            ref[...] = value

    for k in range(count):

        @pl.when(step == k)
        def part(k=k):
            at = pl.ds(pl.multiple_of(lax.rem(meta[0] - k + count, count) * rows, rows), rows)
            gradient = quarters[k][...].astype(f32)
            qkv = gradient[:, : 2 * MODEL_WIDTH]
            product = jnp.sum(qkv * ins[3][...].astype(bf16).astype(f32), axis=1, keepdims=True)
            gain_s[at, :] = jnp.broadcast_to(product, (rows, LANES))
            rest_s[at, :] = gradient[:, 3 * MODEL_WIDTH :]
            update(1, qkv)
            update(2, gradient[:, 2 * MODEL_WIDTH : 3 * MODEL_WIDTH])

    @pl.when(step == count - 1)
    def small():
        rest = rest_s[...].T
        first = gain_s[...].T[0:1] / ins[0][0:1, :].astype(bf16).astype(f32)
        update(0, jnp.concatenate([first, rest[EXPERTS + 1 : EXPERTS + 2]], axis=0))
        update(3, rest[:EXPERTS])


def output_body(meta, h_ref, *refs):
    refs[-1][...] = (h_ref[...] + res_scale * ring_total(refs[:-1])).astype(bf16)


def experts_update_body(rates, rows, parts, rows_of, meta, *refs):
    gradient = rows_of(refs[:parts])
    ins, outs = refs[parts : parts + 6], refs[-8:]
    for i, rate in enumerate(rates):
        own = gradient[: rows[0]] if i == 0 else gradient[rows[0] :]
        weight, first, second = [r[0] for r in ins[3 * i : 3 * i + 3]]
        fresh, first, second = adam_update(weight, own, first, second, rate)
        for ref, value in zip(outs[4 * i : 4 * i + 4], (own, fresh, first, second)):
            ref[0] = value


def experts_update(start, share, arrays, rates, earlier, scalars, after=()):
    shares, share_specs, rows_of = share
    members = shares[0].shape[-3]
    rows = (arrays[0].shape[1], arrays[3].shape[1])

    def spec(a):
        return pl.BlockSpec((1,) + a.shape[1:], lambda e, m: (start + e, 0, 0))

    outs = [shape_of(a.shape, f32) for a in (arrays[0],) * 4 + (arrays[3],) * 4]
    in_specs = share_specs + [spec(a) for a in arrays]
    ins = shares + list(arrays)
    aliases = {}
    if earlier is not None:
        aliases = {1 + len(after) + len(ins) + i: i for i in range(8)}
        in_specs += [pl.BlockSpec(memory_space=pl.ANY)] * 8
        ins += list(earlier)
    return kernel_call(
        functools.partial(experts_update_body, rates, rows, len(shares), rows_of),
        outs,
        ins,
        scalars,
        grid=(members,),
        in_specs=in_specs,
        out_specs=[spec(a) for a in outs],
        limit=60, micros=8,
        after=after,
        aliases=aliases,
    )


def angle_tables(rows, offsets):
    position = (offsets[:, None] + jnp.arange(rows)[None, :]).reshape(-1).astype(f32)
    frequency = 10000.0 ** (-(jnp.arange(HEAD_SIZE // 2).astype(f32) * 2.0 / HEAD_SIZE))
    angles = position[:, None] * frequency[None, :]
    cosine, sine = jnp.cos(angles), jnp.sin(angles)
    shape = (offsets.shape[0], rows, LANES)
    cosine = jnp.concatenate([cosine] * 4, axis=1).reshape(shape)
    return (cosine, jnp.concatenate([-sine, sine] * 2, axis=1).reshape(shape))


def shards_step(
    tokens,
    routes,
    cotangent,
    norm_gains,
    qkv_weight,
    out_weight,
    router_weight,
    expert_up,
    expert_down,
    mean_gains,
    square_gains,
    mean_qkv,
    square_qkv,
    mean_out,
    square_out,
    mean_router,
    square_router,
    mean_up,
    square_up,
    mean_down,
    square_down,
):
    rows = tokens.shape[1]
    count = lax.axis_size("seq")
    shards = lax.axis_size("fsdp")
    shard_rows = MODEL_WIDTH // shards
    local = EXPERTS // count
    early_experts = 3 * local // 4
    chunks = [(0, early_experts), (early_experts, local - early_experts)]
    place = lax.axis_index("seq").astype(jnp.int32)
    owners = (lax.axis_index("fsdp") ^ jnp.arange(shards)).astype(jnp.int32)
    owner_meta = jnp.concatenate([owners, place[None]])
    place_meta = place[None]
    x, c, own_routes = tokens[0], cotangent[0], routes[0]

    def dense_part(piece):
        blank = jnp.zeros((shard_rows // 2, LANES - EXPERTS - 2), f32)
        parts = [qkv_weight[piece], out_weight[piece], router_weight[piece], norm_gains[:, piece].T, blank]
        return jnp.concatenate(parts, axis=1).astype(bf16)

    dense_shards = Gathered(dense_part(slice(0, shard_rows // 2)), dense_part(slice(shard_rows // 2, shard_rows)))
    told = lax.all_gather(c, "seq", axis=0)
    listed = jnp.concatenate([own_routes.T, jnp.zeros_like(own_routes.T)], axis=0).astype(f32).astype(bf16)
    routes_by_block = [listed]
    for k in range(1, count):
        routes_by_block.append(shift_permute(listed, "seq", k))
    cosines, sines = angle_tables(rows, jnp.maximum(place - jnp.arange(count), 0) * rows)
    dense_shards.forward(cosines, sines, *routes_by_block[1:])
    early = dense_shards.arrived()
    dense_pieces = dense_shards.pieces()
    expert_weights = []
    for start, members in chunks:
        mine = slice(start, start + members)
        packed = jnp.concatenate([expert_up[mine], expert_down[mine]], axis=1).astype(bf16)
        expert_weights.append(lax.all_gather(tie(packed, *early), "fsdp", axis=0))

    square = shape_of((MODEL_WIDTH, MODEL_WIDTH))
    wide = shape_of((rows, MODEL_WIDTH))
    wide_f = shape_of((rows, MODEL_WIDTH), f32)
    extra_shape = shape_of((LANES, MODEL_WIDTH), f32)
    unit = 2 * rows * MODEL_WIDTH * MODEL_WIDTH
    wq, wkv, wo, extra, normed_one, q, kv = kernel_call(
        functools.partial(qkv_body, dense_pieces),
        [square, square, square, extra_shape, wide, wide, wide],
        [x] + [a for _, _, a in dense_pieces],
        owner_meta,
        tables=(cosines, sines),
        scratch=[pltpu.VMEM((MODEL_WIDTH, LANES), f32)],
        limit=60, micros=8,
    )
    kv_pieces = ring_gather(kv)
    attended, logsum, resid, normed_two = kernel_call(
        functools.partial(attend_body, count, kv_pieces),
        [wide, shape_of((KEY_VALUE_HEADS, 2 * rows), f32), wide_f, wide],
        [q, x, wo, extra] + [a for _, _, a in kv_pieces],
        place_meta,
        limit=60, micros=12,
    )
    two_pieces = ring_gather(normed_two)

    slots = count * CAP
    packed_rows = (MODEL_WIDTH + FF) // shards
    part_g = part_m = None
    waited = (cosines, sines)
    normed_block = tie(normed_one, *[a for _, _, a in two_pieces[1:]])
    normed_blocks = tuple(shift_permute(normed_block, "seq", k) for k in range(1, count))
    normed_pieces = [(k, 0, a) for k, a in enumerate((normed_one,) + normed_blocks)]
    for i, (start, members) in enumerate(chunks):
        last = i == len(chunks) - 1
        ins = [extra, expert_weights[i], expert_weights[i]] + [a for _, _, a in two_pieces] + [told] + routes_by_block

        def still(a):
            return pl.BlockSpec(a.shape, functools.partial(lambda n, e, m: (0,) * n, a.ndim), pipeline_mode=pl.Buffered(1))

        all_spec = pl.BlockSpec((shards, 1, packed_rows, MODEL_WIDTH), lambda e, m: (0, e, 0, 0))
        set_spec = pl.BlockSpec((shards // 2, 1, packed_rows, MODEL_WIDTH), lambda e, m: (0, e, 0, 0))
        sets = [shape_of((shards // 2, members, packed_rows, MODEL_WIDTH))] * 2
        set_specs = [set_spec] * 2
        if not last:
            sets, set_specs = [shape_of((shards, members, packed_rows, MODEL_WIDTH))], [all_spec]
        up_spec = pl.BlockSpec((shards, 1, shard_rows, MODEL_WIDTH), lambda e, m: (0, e, 0, 0))
        place_down = MODEL_WIDTH // FF
        down_spec = pl.BlockSpec((shards, 1, FF // shards, MODEL_WIDTH), lambda e, m: (0, e, place_down, 0))
        in_specs = [still(extra), up_spec, down_spec] + [still(a) for a in ins[3:]]
        if i > 0:
            ins += [part_g, part_m]
            in_specs += [still(part_g), still(part_m)]
        ring = ring_shapes if last else lambda n, r, w: [shape_of((n, r, w))]
        ring_count = len(ring(count, rows, WIDE))
        outs = sets + ring(count, rows, MODEL_WIDTH) + ring(count, rows, WIDE)
        out_specs = set_specs + [still(a) for a in outs[len(sets) :]]
        scratch = [
            pltpu.VMEM((slots, MODEL_WIDTH), bf16),
            pltpu.VMEM((slots, MODEL_WIDTH), bf16),
            pltpu.VMEM((slots, MODEL_WIDTH), bf16),
            pltpu.VMEM((slots, FF), bf16),
            pltpu.VMEM((slots, 2 * FF), bf16),
            pltpu.VMEM((count, members * CAP, rows), bf16),
            pltpu.VMEM((count, members * CAP, MODEL_WIDTH), bf16),
            pltpu.VMEM((count, members * CAP, MODEL_WIDTH), bf16),
            pltpu.VMEM((MODEL_WIDTH, 2 * FF), bf16),
            pltpu.VMEM((FF, MODEL_WIDTH), bf16),
            pltpu.VMEM((count, EXPERTS, rows), f32),
            pltpu.VMEM((count, EXPERTS, rows), f32),
            pltpu.VMEM((count, EXPERTS, rows), f32),
        ]
        results = kernel_call(
            functools.partial(experts_body, count, shards, two_pieces, start, members, last),
            outs,
            ins,
            owner_meta,
            scratch=scratch,
            grid=(members,),
            in_specs=in_specs,
            out_specs=out_specs,
            micros=8 * members,
            after=waited,
        )
        results = list(results)
        first_part = len(sets)
        part_m, part_g = results[first_part], results[first_part + ring_count]
        mix_parts, ring_parts = results[first_part : first_part + ring_count], results[first_part + ring_count :]
        if not last:
            share = tie(results[0], *normed_blocks)
            share = lax.psum_scatter(share, "fsdp", scatter_dimension=0)

    two_ring = RingSum(ring_parts)
    late_sum = ScatteredExperts(tie(results[1], *two_ring.near()), results[0], place_meta)
    two_sums = two_ring.parts()
    sent = late_sum.first(*two_ring.sent)
    mixing = RingSum(mix_parts, *two_sums[3:], *sent)
    ring = ring_shapes(count, rows, MODEL_WIDTH)
    results = kernel_call(
        functools.partial(backward_body, count, kv_pieces, len(two_sums)),
        [wide_f, wide, wide, shape_of((MODEL_WIDTH, LANES), f32), shape_of((8, MODEL_WIDTH), f32)] + ring,
        [own_routes, normed_two, extra, resid, c, attended, wo, q, logsum]
        + list(two_sums)
        + [a for _, _, a in kv_pieces],
        place_meta,
        tables=(cosines, sines),
        scratch=[pltpu.VMEM((rows, MODEL_WIDTH), bf16)],
        limit=60, micros=22,
    )
    resid_grad, go, gpq, router_grad, gain_grad = results[:5]
    mix_sums = mixing.parts()
    dense_set = shape_of((shards // 2, shard_rows, 3 * MODEL_WIDTH + LANES))
    keep, send = kernel_call(
        functools.partial(weights_body, count, shards, normed_pieces),
        [dense_set] * 2,
        [attended, go, gpq, router_grad, gain_grad, cosines, sines]
        + [a for _, _, a in normed_pieces]
        + list(results[5:]),
        owner_meta,
        scratch=[
            pltpu.VMEM((count * rows, MODEL_WIDTH), bf16),
            pltpu.VMEM((count * rows, MODEL_WIDTH), bf16),
            pltpu.VMEM((MODEL_WIDTH, MODEL_WIDTH), bf16),
            pltpu.VMEM((MODEL_WIDTH, LANES), f32),
        ],
        after=mixing.near(),
        limit=60, micros=12,
    )
    dense_sum = Scattered(place_meta)
    dense_sum.add(send, keep, *mix_sums[3:])
    rates = (learn_rates[4], learn_rates[5])
    experts = (expert_up, mean_up, square_up, expert_down, mean_down, square_down)
    sent = dense_sum.first()
    kv_ring = RingSum(results[5:], *mix_sums[3:])
    spec = pl.BlockSpec((1,) + share.shape[1:], lambda e, m: (e, 0, 0))
    total = ([share], [spec], lambda refs: refs[0][0].astype(f32))
    updated = experts_update(chunks[0][0], total, experts, rates, None, place_meta, sent)
    kv_sums = kv_ring.parts(*dense_sum.second(updated[0]))
    own = dense_sum.total(count, *kv_ring.sent)
    late_sum.depart(own)
    quarters = lax.all_to_all(own, "seq", split_axis=0, concat_axis=0, tiled=True)
    (tokens_grad,) = kernel_call(
        tokens_body,
        [wide_f],
        [x, gpq, wq, wkv, extra, resid_grad] + list(kv_sums),
        place_meta,
        tables=(cosines, sines),
        scratch=[pltpu.VMEM((rows, MODEL_WIDTH), bf16)],
        after=(own,),
        limit=60, micros=6,
    )
    (output,) = kernel_call(output_body, [wide], [resid] + mix_sums, place_meta, after=(own,), limit=60, micros=3)
    quarter = jnp.sum(tie(quarters, tokens_grad, *late_sum.second(tokens_grad)).astype(f32), axis=0).astype(bf16)
    tokens_grad, output = tokens_grad[None], output[None]
    quarters = [quarter] + [shift_permute(quarter, "seq", k) for k in range(1, count)]
    updated = experts_update(chunks[1][0], late_sum.total(), experts, rates, updated, place_meta, (quarter,))
    dense_ins = [norm_gains, mean_gains, square_gains, qkv_weight, mean_qkv, square_qkv]
    dense_ins += [out_weight, mean_out, square_out, router_weight.T, mean_router.T, square_router.T]
    part_rows = shard_rows // count

    def whole_spec(a):
        return pl.BlockSpec(a.shape, lambda k, m: (0,) * a.ndim)

    def part_spec(a):
        return pl.BlockSpec((part_rows, a.shape[1]), lambda k, m: (lax.rem(m[0] - k + count, count), 0))

    specs = [whole_spec, part_spec, part_spec, whole_spec]
    dense_outs = kernel_call(
        functools.partial(dense_update_body, count, learn_rates[:4]),
        [shape_of(a.shape, f32) for a in dense_ins[::3] for _ in range(4)],
        quarters + dense_ins,
        place_meta,
        scratch=[pltpu.VMEM((shard_rows, LANES), f32), pltpu.VMEM((shard_rows, LANES), f32)],
        grid=(count,),
        in_specs=[whole_spec(a) for a in quarters] + [specs[i // 3](a) for i, a in enumerate(dense_ins)],
        out_specs=[specs[i](dense_ins[3 * i]) for i in range(4) for _ in range(4)],
        after=(updated[0],),
        limit=60, micros=5,
    )
    shard_gains, fresh_gains, momentum_gains, variance_gains = dense_outs[:4]
    shard_qkv, fresh_qkv, momentum_qkv, variance_qkv = dense_outs[4:8]
    shard_out, fresh_out, momentum_out, variance_out = dense_outs[8:12]
    shard_router, fresh_router, momentum_router, variance_router = [a.T for a in dense_outs[12:]]
    shard_up, fresh_up, momentum_up, variance_up = updated[:4]
    shard_down, fresh_down, momentum_down, variance_down = updated[4:]
    return (
        output,
        tokens_grad,
        shard_gains,
        shard_qkv,
        shard_out,
        shard_router,
        shard_up,
        shard_down,
        fresh_gains,
        fresh_qkv,
        fresh_out,
        fresh_router,
        fresh_up,
        fresh_down,
        momentum_gains,
        momentum_qkv,
        momentum_out,
        momentum_router,
        momentum_up,
        momentum_down,
        variance_gains,
        variance_qkv,
        variance_out,
        variance_router,
        variance_up,
        variance_down,
    )


def solution(mesh):
    block = P("fsdp", "seq", None)
    gains, dense, experts = P(None, "fsdp"), P("fsdp", None), P("seq", "fsdp", None)
    weights = (gains, dense, dense, dense, experts, experts)
    moments = tuple(s for spec in weights for s in (spec, spec))
    return jax.shard_map(
        shards_step,
        mesh=mesh,
        in_specs=(block, block, block) + weights + moments,
        out_specs=(block, block) + weights * 4,
        check_vma=False,
    )
```

```python
import functools

import jax
import jax.numpy as jnp
from jax import lax
from jax.experimental import pallas as pl
from jax.experimental.pallas import tpu as pltpu
from jax.sharding import PartitionSpec as P

MODEL_WIDTH = 1024
QUERY_HEADS = 16
KEY_VALUE_HEADS = 8
HEAD_SIZE = 64
EXPERTS = 32
FF = 512
TOP = 8
STEP = 3
CAP = 96
LANES = 128
TILE = 256

epsilon = 1e-06
res_scale = 0.22
att_scale = 0.015625
beta_one = 0.9
beta_two = 0.95
adam_eps = 1e-08
weight_decay = 0.1
learn_rates = (0.4, 0.04, 0.2, 0.01, 0.01, 0.05)

bf16 = jnp.bfloat16
f32 = jnp.float32
WIDE = MODEL_WIDTH + LANES


def adam_update(weight, gradient, first, second, rate):
    first_new = beta_one * first + (1.0 - beta_one) * gradient
    second_new = beta_two * second + (1.0 - beta_two) * gradient * gradient
    first_hat = first_new / (1.0 - beta_one**STEP)
    second_hat = second_new / (1.0 - beta_two**STEP)
    fresh = weight - rate * (first_hat / (jnp.sqrt(second_hat) + adam_eps) + weight_decay * weight)
    return (fresh, first_new, second_new)


def dot_nn(a, b):
    return lax.dot_general(a, b, (((1,), (0,)), ((), ())), preferred_element_type=f32)


def dot_nt(a, b):
    return lax.dot_general(a, b, (((1,), (1,)), ((), ())), preferred_element_type=f32)


def dot_tn(a, b):
    return lax.dot_general(a, b, (((0,), (0,)), ((), ())), preferred_element_type=f32)


def lanes_of(shape):
    return lax.broadcasted_iota(jnp.int32, shape, len(shape) - 1)


def aligned(index, size):
    if isinstance(index, int):
        return slice(index, index + size)
    return pl.ds(pl.multiple_of(index, size), size)


def kernel_call(body, outs, ins, scalars, scratch=(), grid=None, in_specs=None, out_specs=None, limit=60, after=(), micros=10, aliases=None, tables=()):
    in_specs = in_specs or [pl.BlockSpec(memory_space=pltpu.VMEM)] * len(ins)
    for a in tables:
        ins = list(ins) + [a]
        in_specs = in_specs + [pl.BlockSpec((1,) + a.shape[1:], lambda i, m: (0, 0, 0))]
    out_specs = out_specs or [pl.BlockSpec(memory_space=pltpu.VMEM)] * len(outs)
    in_specs = [pl.BlockSpec(memory_space=pl.ANY)] * len(after) + in_specs

    def ordered_body(meta, *refs):
        body(meta, *refs[len(after) :])

    return pl.pallas_call(
        ordered_body,
        out_shape=outs,
        grid_spec=pltpu.PrefetchScalarGridSpec(
            num_scalar_prefetch=1,
            grid=grid or (1,),
            in_specs=in_specs,
            out_specs=out_specs,
            scratch_shapes=list(scratch),
        ),
        compiler_params=pltpu.CompilerParams(vmem_limit_bytes=limit * 1024 * 1024),
        input_output_aliases=aliases or {},
        cost_estimate=pl.CostEstimate(flops=micros * 10**9, bytes_accessed=micros * 10**6, transcendentals=0),
    )(scalars, *after, *ins)


def tie(value, *earlier):
    anywhere = pl.BlockSpec(memory_space=pl.ANY)
    return pl.pallas_call(
        lambda *refs: None,
        out_shape=shape_of(value.shape, value.dtype),
        in_specs=[anywhere] * (1 + len(earlier)),
        out_specs=anywhere,
        input_output_aliases={0: 0},
    )(value, *earlier)


def shape_of(shape, kind=bf16):
    return jax.ShapeDtypeStruct(shape, kind)


def xor_permute(value, axis, mask):
    return lax.ppermute(value, axis, [(i, i ^ mask) for i in range(lax.axis_size(axis))])


def shift_permute(value, axis, step):
    size = lax.axis_size(axis)
    return lax.ppermute(value, axis, [(i, (i + step) % size) for i in range(size)])


class Gathered:
    def __init__(self, first, second):
        self.plain = lax.axis_size("fsdp") != 8
        self.first, self.second = first, second
        self.half = first.shape[0]
        if not self.plain:
            self.x_first = xor_permute(first, "fsdp", 2)
            self.y_second = xor_permute(second, "fsdp", 4)
            self.x_second = xor_permute(second, "fsdp", 2)
            self.y_first = xor_permute(first, "fsdp", 4)

    def forward(self, *earlier):
        if self.plain:
            return
        self.x_first = tie(self.x_first, *earlier)
        self.y_second = tie(self.y_second, *earlier)
        self.far_first = xor_permute(self.x_first, "fsdp", 4)
        self.far_second = xor_permute(self.y_second, "fsdp", 2)

    def arrived(self):
        return () if self.plain else (self.far_first, self.far_second)

    def pieces(self):
        count, half = lax.axis_size("fsdp"), self.half
        if self.plain:
            whole = lax.all_gather(jnp.concatenate([self.first, self.second]), "fsdp", axis=0)
            whole = jnp.take(whole, lax.axis_index("fsdp") ^ jnp.arange(count), axis=0)
            return [(r, 0, whole[r]) for r in range(count)]
        mine = [(0, 0, self.first), (0, half, self.second), (2, 0, self.x_first), (2, half, self.x_second)]
        mine += [(4, 0, self.y_first), (4, half, self.y_second), (6, 0, self.far_first), (6, half, self.far_second)]
        return mine + [(r + 1, row, xor_permute(a, "fsdp", 1)) for r, row, a in mine]


def pairs_body(groups, meta, *refs):
    sent_x, sent_y, rest = refs[2 * groups :]
    left = 0
    for keep, got in zip(refs[:groups], refs[groups : 2 * groups]):
        half, columns = keep.shape[1] // 2, keep.shape[2]
        lanes = slice(left, left + columns)
        left += columns

        def pair(i, part):
            piece = slice(part * half, (part + 1) * half)
            return (keep[i, piece, :].astype(f32) + got[i, piece, :].astype(f32)).astype(bf16)

        for ref, place, value in (
            (sent_x, 0, pair(3, 0)),
            (sent_x, 1, pair(1, 0)),
            (sent_y, 0, pair(3, 1)),
            (sent_y, 1, pair(2, 1)),
            (rest, 0, pair(0, 0)),
            (rest, 1, pair(0, 1)),
            (rest, 2, pair(1, 1)),
            (rest, 3, pair(2, 0)),
        ):
            ref[place, :, lanes] = value


class Scattered:
    def __init__(self, scalars):
        self.plain = lax.axis_size("fsdp") != 8
        self.scalars = scalars
        self.send, self.keep, self.got = [], [], []

    def add(self, send, keep, *earlier):
        self.send.append(send)
        self.keep.append(keep)
        if not self.plain:
            self.got.append(xor_permute(tie(send, *earlier) if earlier else send, "fsdp", 1))

    def first(self, *earlier):
        if self.plain:
            return ()
        rows, columns = self.keep[0].shape[1], sum(a.shape[2] for a in self.keep)
        two, four = shape_of((2, rows // 2, columns)), shape_of((4, rows // 2, columns))
        body = functools.partial(pairs_body, len(self.keep))
        sent_x, sent_y, self.rest = kernel_call(
            body, [two, two, four], self.keep + self.got, self.scalars, after=earlier, limit=24, micros=3
        )
        self.over_x = xor_permute(sent_x, "fsdp", 2)
        self.over_y = xor_permute(sent_y, "fsdp", 4)
        return (sent_x, sent_y)

    def second(self, *earlier):
        if self.plain:
            return ()
        if earlier:
            self.over_x, self.over_y = tie(self.over_x, *earlier), tie(self.over_y, *earlier)
        sent_x = (self.rest[2].astype(f32) + self.over_y[0].astype(f32)).astype(bf16)
        sent_y = (self.rest[3].astype(f32) + self.over_x[0].astype(f32)).astype(bf16)
        self.then_x = xor_permute(sent_x, "fsdp", 2)
        self.then_y = xor_permute(sent_y, "fsdp", 4)
        return (sent_x, sent_y)

    def total(self, places, *earlier):
        if self.plain:
            count = lax.axis_size("fsdp")
            keep, send = jnp.concatenate(self.keep, axis=2), jnp.concatenate(self.send, axis=2)
            both = jnp.stack([keep, send], axis=1).reshape((count,) + keep.shape[1:])
            both = jnp.take(both, lax.axis_index("fsdp") ^ jnp.arange(count), axis=0)
            total = lax.psum_scatter(both, "fsdp", scatter_dimension=0)
            return total.reshape((places, -1, total.shape[1]))
        if earlier:
            self.then_x = tie(self.then_x, *earlier)
        first = self.rest[0].astype(f32) + self.over_x[1].astype(f32) + self.then_y.astype(f32)
        second = self.rest[1].astype(f32) + self.over_y[1].astype(f32) + self.then_x.astype(f32)
        return jnp.concatenate([first, second]).astype(bf16).reshape((places, -1, first.shape[1]))


def expert_pairs_body(meta, keep, got, sent_x, sent_y, rest):
    half = keep.shape[2] // 2

    def pair(i, part):
        piece = slice(part * half, (part + 1) * half)
        return (keep[i, 0, piece, :].astype(f32) + got[i, 0, piece, :].astype(f32)).astype(bf16)

    sent_x[0, 0], sent_x[1, 0] = pair(3, 0), pair(1, 0)
    sent_y[0, 0], sent_y[1, 0] = pair(3, 1), pair(2, 1)
    rest[0, 0], rest[1, 0], rest[2, 0], rest[3, 0] = pair(0, 0), pair(0, 1), pair(1, 1), pair(2, 0)


def expert_passed_body(meta, rest, over_x, over_y, then_x, then_y):
    then_x[0] = (rest[0, 0].astype(f32) + over_y[0, 0].astype(f32)).astype(bf16)
    then_y[0] = (rest[1, 0].astype(f32) + over_x[0, 0].astype(f32)).astype(bf16)


class ScatteredExperts:
    def __init__(self, send, keep, scalars):
        self.plain = lax.axis_size("fsdp") != 8
        self.send, self.keep, self.scalars = send, keep, scalars
        if not self.plain:
            self.got = xor_permute(send, "fsdp", 1)

    def first(self, *earlier):
        if self.plain:
            return ()
        sets, self.members, rows, columns = self.keep.shape
        half = rows // 2

        def group(n, start=0):
            return pl.BlockSpec((n, 1, half, columns), lambda e, m: (start, e, 0, 0))

        self.group = group
        self.single = pl.BlockSpec((1, half, columns), lambda e, m: (e, 0, 0))
        whole = pl.BlockSpec((sets, 1, rows, columns), lambda e, m: (0, e, 0, 0))
        shapes = [shape_of((n, self.members, half, columns)) for n in (2, 2, 4)]
        sent_x, sent_y, self.rest = kernel_call(
            expert_pairs_body,
            shapes,
            [self.keep, self.got],
            self.scalars,
            grid=(self.members,),
            in_specs=[whole, whole],
            out_specs=[group(2), group(2), group(4)],
            after=earlier,
            limit=60, micros=6,
        )
        self.sent = (sent_x, sent_y)
        return self.sent

    def depart(self, *earlier):
        if self.plain:
            return
        self.over_x = xor_permute(tie(self.sent[0], *earlier), "fsdp", 2)
        self.over_y = xor_permute(tie(self.sent[1], *earlier), "fsdp", 4)

    def arrived(self):
        return () if self.plain else (self.over_x, self.over_y)

    def second(self, *earlier):
        if self.plain:
            return ()
        one = shape_of(self.rest.shape[1:])
        sent_x, sent_y = kernel_call(
            expert_passed_body,
            [one, one],
            [self.rest, self.over_x, self.over_y],
            self.scalars,
            grid=(self.members,),
            in_specs=[self.group(2, 1), self.group(1), self.group(1)],
            out_specs=[self.single, self.single],
            after=earlier,
            limit=60, micros=4,
        )
        self.then_x = xor_permute(sent_x, "fsdp", 2)
        self.then_y = xor_permute(sent_y, "fsdp", 4)
        return (sent_x, sent_y)

    def total(self):
        if self.plain:
            count = lax.axis_size("fsdp")
            both = jnp.stack([self.keep, self.send], axis=1).reshape((count,) + self.keep.shape[1:])
            both = jnp.take(both, lax.axis_index("fsdp") ^ jnp.arange(count), axis=0)
            share = lax.psum_scatter(both, "fsdp", scatter_dimension=0)
            spec = pl.BlockSpec((1,) + share.shape[1:], lambda e, m: (e, 0, 0))
            return ([share], [spec], lambda refs: refs[0][0].astype(f32))
        arrays = [self.rest, self.over_x, self.over_y, self.then_x, self.then_y]
        specs = [self.group(2), self.group(1, 1), self.group(1, 1), self.single, self.single]

        def rows_of(refs):
            rest, over_x, over_y, then_x, then_y = refs
            first = rest[0, 0].astype(f32) + over_x[0, 0].astype(f32) + then_y[0].astype(f32)
            second = rest[1, 0].astype(f32) + over_y[0, 0].astype(f32) + then_x[0].astype(f32)
            return jnp.concatenate([first, second], axis=0)

        return (arrays, specs, rows_of)


class Ringed:
    def __init__(self, block):
        self.plain = lax.axis_size("seq") != 4
        self.block = block
        self.half = block.shape[0] // 2
        if not self.plain:
            self.below = shift_permute(block, "seq", 1)
            self.above = shift_permute(block, "seq", -1)

    def near(self):
        return () if self.plain else (self.below, self.above)

    def forward(self):
        if self.plain:
            return ()
        self.far_first = shift_permute(self.below[: self.half], "seq", 1)
        self.far_second = shift_permute(self.above[self.half :], "seq", -1)
        return (self.far_first, self.far_second)

    def pieces(self):
        count = lax.axis_size("seq")
        if self.plain:
            whole = lax.all_gather(self.block, "seq", axis=0)
            whole = jnp.take(whole, (lax.axis_index("seq") - jnp.arange(count)) % count, axis=0)
            return [(k, 0, whole[k]) for k in range(count)]
        pieces = [(0, 0, self.block), (1, 0, self.below), (3, 0, self.above)]
        return pieces + [(2, 0, self.far_first), (2, self.half, self.far_second)]


def ring_gather(block):
    ring = Ringed(block)
    ring.forward()
    return ring.pieces()


def ring_shapes(count, rows, columns):
    if count != 4:
        return [shape_of((count, rows, columns))]
    half = rows // 2
    return [shape_of((r, columns)) for r in (rows, rows, rows, half, half)]


def ring_put(count, refs, k, rows, value):
    half = rows // 2
    width = value.shape[1]
    value = value.astype(bf16)
    if count != 4:
        refs[0][k, :, :width] = value
        return
    own, down, up, keep_down, keep_up = refs
    places = {
        0: ((own, 0), (own, half)),
        1: ((keep_down, 0), (down, half)),
        2: ((down, 0), (up, 0)),
        3: ((up, half), (keep_up, 0)),
    }
    for part, (ref, row) in enumerate(places[k]):
        ref[row : row + half, :width] = value[part * half : (part + 1) * half]


def ring_put_tail(count, refs, k, rows, value):
    half = rows // 2
    value = value.astype(bf16)
    if count != 4:
        refs[0][k, :, MODEL_WIDTH:] = value
        return
    own, down, up, keep_down, keep_up = refs
    places = {
        0: ((own, 0), (own, half)),
        1: ((keep_down, 0), (down, half)),
        2: ((down, 0), (up, 0)),
        3: ((up, half), (keep_up, 0)),
    }
    for part, (ref, row) in enumerate(places[k]):
        ref[row : row + half, MODEL_WIDTH:] = value[part * half : (part + 1) * half]


def ring_get(count, refs, k, rows):
    if count != 4:
        return refs[0][k]
    half = rows // 2
    own, down, up, keep_down, keep_up = refs
    if k == 0:
        return own[...]
    first, second = {
        1: ((keep_down, 0), (down, half)),
        2: ((down, 0), (up, 0)),
        3: ((up, half), (keep_up, 0)),
    }[k]
    return jnp.concatenate([ref[row : row + half, :] for ref, row in (first, second)], axis=0)


class RingSum:
    def __init__(self, arrays, *earlier):
        self.plain = lax.axis_size("seq") != 4
        self.arrays = list(arrays)
        self.sent = ()
        if not self.plain:
            own, down, up, keep_down, keep_up = self.arrays
            if earlier:
                down, up = tie(down, *earlier), tie(up, *earlier)
            self.from_above = shift_permute(down, "seq", -1)
            self.from_below = shift_permute(up, "seq", 1)

    def near(self):
        return () if self.plain else (self.from_above, self.from_below)

    def parts(self, *earlier):
        if self.plain:
            count = lax.axis_size("seq")
            whole = jnp.take(self.arrays[0], (lax.axis_index("seq") - jnp.arange(count)) % count, axis=0)
            return [lax.psum_scatter(whole, "seq", scatter_dimension=0)]
        own, down, up, keep_down, keep_up = self.arrays
        half = keep_down.shape[0]
        if earlier:
            self.from_above = tie(self.from_above, *earlier)
            self.from_below = tie(self.from_below, *earlier)
        then_down = (keep_down.astype(f32) + self.from_above[:half].astype(f32)).astype(bf16)
        then_up = (keep_up.astype(f32) + self.from_below[:half].astype(f32)).astype(bf16)
        self.sent = (then_down, then_up)
        last_above = shift_permute(then_down, "seq", -1)
        last_below = shift_permute(then_up, "seq", 1)
        return [own, self.from_above, self.from_below, last_above, last_below]


def ring_total(refs):
    if len(refs) == 1:
        return refs[0][...].astype(f32)
    own, above, below, last_above, last_below = [r[...].astype(f32) for r in refs]
    half = own.shape[0] // 2
    first = own[:half] + below[half:] + last_above
    second = own[half:] + above[half:] + last_below
    return jnp.concatenate([first, second], axis=0)


def block_value(pieces, refs, k):
    found = [(row, ref) for (kk, row, _), ref in zip(pieces, refs) if kk == k]
    found.sort(key=lambda entry: entry[0])
    if len(found) == 1:
        return found[0][1][...]
    return jnp.concatenate([ref[...] for _, ref in found], axis=0)


def block_lanes(pieces, refs, k, lanes):
    found = [(row, ref) for (kk, row, _), ref in zip(pieces, refs) if kk == k]
    found.sort(key=lambda entry: entry[0])
    if len(found) == 1:
        return found[0][1][:, lanes]
    return jnp.concatenate([ref[:, lanes] for _, ref in found], axis=0)


def rotate_tile(tile, cosine, sine):
    first = lanes_of(tile.shape) % HEAD_SIZE < HEAD_SIZE // 2
    turned = jnp.where(first, pltpu.roll(tile, LANES - HEAD_SIZE // 2, 1), pltpu.roll(tile, HEAD_SIZE // 2, 1))
    return tile * cosine + turned * sine


def rotate_tile_back(tile, cosine, sine):
    return rotate_tile(tile, cosine, -sine)


def qkv_body(pieces, meta, x_ref, *refs):
    shards = refs[: len(pieces)]
    cos_ref, sin_ref, *refs = refs[len(pieces) :]
    wq_ref, wkv_ref, wo_ref, extra_ref, normed_ref, q_ref, kv_ref, columns = refs
    shard_rows = MODEL_WIDTH // max(r + 1 for r, _, _ in pieces)
    for (r, row, value), ref in zip(pieces, shards):
        rows = value.shape[0]
        place = pl.ds(pl.multiple_of(meta[r] * shard_rows + row, rows), rows)
        wq_ref[place, :] = ref[:, :MODEL_WIDTH]
        wkv_ref[place, :] = ref[:, MODEL_WIDTH : 2 * MODEL_WIDTH]
        wo_ref[place, :] = ref[:, 2 * MODEL_WIDTH : 3 * MODEL_WIDTH]
        columns[place, :] = ref[:, 3 * MODEL_WIDTH :].astype(f32)
    extra_ref[...] = columns[...].T
    source = x_ref[...].astype(f32)
    scale_inv = lax.rsqrt(jnp.mean(source * source, axis=-1, keepdims=True) + epsilon)
    normed = (source * scale_inv * extra_ref[EXPERTS : EXPERTS + 1, :]).astype(bf16)
    normed_ref[...] = normed
    cosine, sine = cos_ref[0], sin_ref[0]
    low = lanes_of(cosine.shape) < HEAD_SIZE
    for j in range(MODEL_WIDTH // TILE):
        block = dot_nn(normed, wq_ref[:, j * TILE : (j + 1) * TILE])
        for i in range(TILE // LANES):
            at = j * TILE + i * LANES
            tile = block[:, i * LANES : (i + 1) * LANES]
            q_ref[:, at : at + LANES] = rotate_tile(tile, cosine, sine).astype(bf16)
    for j in range(MODEL_WIDTH // TILE):
        block = dot_nn(normed, wkv_ref[:, j * TILE : (j + 1) * TILE])
        for i in range(TILE // LANES):
            at = j * TILE + i * LANES
            tile = block[:, i * LANES : (i + 1) * LANES]
            tile = jnp.where(low, rotate_tile(tile, cosine, sine), tile).astype(bf16)
            kv_ref[:, at : at + LANES] = tile


def causal_scores(keys, pair, k):
    scores = dot_nt(keys, pair)
    if k == 0:
        rows = keys.shape[0]
        query = lanes_of(scores.shape) % rows
        scores = jnp.where(query >= lax.broadcasted_iota(jnp.int32, scores.shape, 0), scores, -jnp.inf)
    return scores


def query_pair(tile):
    low = lanes_of(tile.shape) < HEAD_SIZE
    tile = tile.astype(f32) * att_scale
    even = jnp.where(low, tile, 0.0)
    odd = jnp.where(low, pltpu.roll(tile, HEAD_SIZE, 1), 0.0)
    return jnp.concatenate([even, odd], axis=0).astype(bf16)


def attend_body(count, pieces, meta, q_ref, x_ref, wo_ref, extra_ref, *refs):
    blocks = refs[: len(pieces)]
    a_ref, lse_ref, h_ref, normed_ref = refs[len(pieces) :]
    rows = q_ref.shape[0]
    place = meta[0]

    def variant(seen):
        def group(g, carry):
            lanes = aligned(g * LANES, LANES)
            pair = query_pair(q_ref[:, lanes])
            keys = [block_lanes(pieces, blocks, k, lanes) for k in range(seen)]
            scores = [causal_scores(keys[k], pair, k) for k in range(seen)]
            top = functools.reduce(jnp.maximum, [jnp.max(s, axis=0, keepdims=True) for s in scores])
            weights = [jnp.exp(s - top) for s in scores]
            total = functools.reduce(jnp.add, [jnp.sum(w, axis=0, keepdims=True) for w in weights])
            summed = functools.reduce(jnp.add, [dot_tn(t, w.astype(bf16)) for w, t in zip(weights, keys)])
            summed = summed[HEAD_SIZE:] * (1.0 / total)
            both = jnp.concatenate([summed[:, :rows], summed[:, rows:]], axis=0)
            a_ref[:, lanes] = both.T.astype(bf16)
            lse_ref[pl.ds(g, 1), :] = top + jnp.log(total)
            return carry

        lax.fori_loop(0, KEY_VALUE_HEADS, group, 0)

    for seen in range(1, count + 1):
        pl.when(place == seen - 1)(functools.partial(variant, seen))
    resid = x_ref[...].astype(f32) + res_scale * dot_nn(a_ref[...], wo_ref[...])
    h_ref[...] = resid
    scale_inv = lax.rsqrt(jnp.mean(resid * resid, axis=-1, keepdims=True) + epsilon)
    normed_ref[...] = (resid * scale_inv * extra_ref[EXPERTS + 1 : EXPERTS + 2, :]).astype(bf16)


def softmax_over(picked, logits, axis):
    top = jnp.max(jnp.where(picked, logits, -jnp.inf), axis=axis, keepdims=True)
    raised = jnp.where(picked, jnp.exp(jnp.minimum(logits - top, 0.0)), 0.0)
    return raised / jnp.sum(raised, axis=axis, keepdims=True)


def experts_body(count, shards, pieces, start, members, last, meta, extra_ref, *refs):
    refs = list(refs)

    def take(number):
        taken = refs[:number]
        del refs[:number]
        return taken

    up_w, down_w = take(2)
    blocks, (told,), listed = take(len(pieces)), take(1), take(count)
    if start > 0:
        (part_g, part_m) = take(2)
    keep_ref, send_ref = take(2) if last else (take(1) + [None])
    ring_count = len(ring_shapes(count, TILE, WIDE)) if last else 1
    mix_refs, ring_refs = take(ring_count), take(ring_count)
    x_s, c_s, ge_s, a_s, gu_s, d_s, eg_s, gs_s, gup_s, gdown_s, gate_s, rank_s, gg_s = refs
    step = pl.program_id(0)
    local = EXPERTS // count
    up_rows, down_rows = MODEL_WIDTH // shards, FF // shards
    slots = count * CAP
    place = meta[shards]
    expert = place * local + start + step

    def absolute(k):
        return lax.rem(place - k + count, count)

    @pl.when(step == 0)
    def routing():
        router = extra_ref[:EXPERTS, :].astype(bf16)
        later = (
            lax.broadcasted_iota(jnp.int32, (TILE, TILE), 0) < lax.broadcasted_iota(jnp.int32, (TILE, TILE), 1)
        )
        later = jnp.where(later, 1.0, 0.0).astype(bf16)
        names = lax.broadcasted_iota(jnp.int32, (EXPERTS, TILE), 0).astype(f32)
        for k in range(count):
            named = listed[k][...].astype(f32)
            picked = names == named[0:1, :]
            for j in range(1, TOP):
                picked = jnp.logical_or(picked, names == named[j : j + 1, :])
            logits = dot_nt(router, block_value(pieces, blocks, k))
            gate_s[k] = softmax_over(picked, logits, 0)
            before = dot_nn(jnp.where(picked, 1.0, 0.0).astype(bf16), later)
            rank_s[k] = jnp.where(picked, before, -1.0)
        gg_s[...] = jnp.zeros_like(gg_s)

    def up_columns(columns):
        return up_w[:, 0, :, columns].reshape(MODEL_WIDTH, TILE)

    def up_tile(j):
        here = slice(j * TILE // up_rows, (j + 1) * TILE // up_rows)
        return up_w[here, 0, :, :].reshape(TILE, 2 * FF)

    def down_columns(columns):
        return down_w[:, 0, :, columns].reshape(FF, TILE)

    def down_tile(j):
        here = slice(j * TILE // down_rows, (j + 1) * TILE // down_rows)
        return down_w[here, 0, :, :].reshape(TILE, MODEL_WIDTH)

    wanted = lax.broadcasted_iota(jnp.int32, (CAP, TILE), 0).astype(f32)
    held = aligned(step * CAP, CAP)
    gates = []
    for k in range(count):
        rank = rank_s[k, pl.ds(expert, 1), :]
        gate = gate_s[k, pl.ds(expert, 1), :]
        hit = wanted == rank
        chosen = jnp.where(hit, 1.0, 0.0).astype(bf16)
        d_s[k, held, :] = chosen
        here = slice(k * CAP, (k + 1) * CAP)
        x_s[here, :] = dot_nn(chosen, block_value(pieces, blocks, k)).astype(bf16)
        upstream = dot_nn(chosen, told[absolute(k)])
        own_gate = jnp.sum(jnp.where(hit, gate, 0.0), axis=1, keepdims=True)
        gates.append(own_gate)
        c_s[here, :] = upstream.astype(bf16)
        ge_s[here, :] = (own_gate * (res_scale * upstream)).astype(bf16)

    for j in range(FF // TILE):
        left, right = slice(j * TILE, (j + 1) * TILE), slice(FF + j * TILE, FF + (j + 1) * TILE)
        gate_part = dot_nn(x_s[...], up_columns(left))
        up_part = dot_nn(x_s[...], up_columns(right))
        hidden_grad = dot_nt(ge_s[...], down_tile(j))
        sigmoid_gate = jax.nn.sigmoid(gate_part)
        swish = gate_part * sigmoid_gate
        a_s[:, left] = (swish * up_part).astype(bf16)
        slope = sigmoid_gate * (1.0 + gate_part * (1.0 - sigmoid_gate))
        gu_s[:, left] = (hidden_grad * up_part * slope).astype(bf16)
        gu_s[:, right] = (hidden_grad * swish).astype(bf16)

    gate_grad = jnp.zeros((slots, 1), f32)
    for j in range(MODEL_WIDTH // TILE):
        columns = slice(j * TILE, (j + 1) * TILE)
        produced = dot_nn(a_s[...], down_columns(columns)).astype(bf16).astype(f32)
        gate_grad += jnp.sum(res_scale * c_s[:, columns].astype(f32) * produced, axis=1, keepdims=True)
        input_grad = dot_nt(gu_s[...], up_tile(j)).astype(bf16)
        for k in range(count):
            here = slice(k * CAP, (k + 1) * CAP)
            eg_s[k, held, columns] = (gates[k] * produced[here]).astype(bf16)
            gs_s[k, held, columns] = input_grad[here]
    for k in range(count):
        hit = wanted == rank_s[k, pl.ds(expert, 1), :]
        spread = jnp.where(hit, gate_grad[k * CAP : (k + 1) * CAP], 0.0)
        gg_s[k, pl.ds(expert, 1), :] = jnp.sum(spread, axis=0, keepdims=True)

    for j in range(FF // TILE):
        rows = slice(j * TILE, (j + 1) * TILE)
        tile = dot_tn(a_s[:, rows], ge_s[...]).astype(bf16)
        if last:
            gdown_s[rows, :] = tile
        else:
            here = slice(j * TILE // down_rows, (j + 1) * TILE // down_rows)
            keep_ref[here, 0, up_rows:, :] = tile.reshape(TILE // down_rows, down_rows, MODEL_WIDTH)
    for j in range(MODEL_WIDTH // TILE):
        rows = slice(j * TILE, (j + 1) * TILE)
        tile = dot_tn(x_s[:, rows], gu_s[...]).astype(bf16)
        if last:
            gup_s[rows, :] = tile
        else:
            here = slice(j * TILE // up_rows, (j + 1) * TILE // up_rows)
            keep_ref[here, 0, :up_rows, :] = tile.reshape(TILE // up_rows, up_rows, 2 * FF)
    if last:
        for r in range(shards):
            ref = send_ref if r % 2 else keep_ref
            ref[r // 2, 0, :up_rows, :] = gup_s[aligned(meta[r] * up_rows, up_rows), :]
            ref[r // 2, 0, up_rows:, :] = gdown_s[aligned(meta[r] * down_rows, down_rows), :]

    @pl.when(step == members - 1)
    def combine():
        for k in range(count):
            spread = d_s[k]
            mixed = dot_tn(spread, eg_s[k])
            summed = dot_tn(spread, gs_s[k])
            exact = gg_s[k]
            rounded = exact.astype(bf16).astype(f32)
            rest = jnp.zeros((LANES - 2 * EXPERTS, TILE), f32)
            tail = jnp.concatenate([rounded, exact - rounded, rest], axis=0).T
            if start > 0:
                mixed += part_m[k].astype(f32)
                summed += part_g[k, :, :MODEL_WIDTH].astype(f32)
                tail += part_g[k, :, MODEL_WIDTH:].astype(f32)
            if last:
                ring_put(count, mix_refs, k, TILE, mixed)
                ring_put(count, ring_refs, k, TILE, summed)
                ring_put_tail(count, ring_refs, k, TILE, tail)
            else:
                mix_refs[0][k] = mixed.astype(bf16)
                ring_refs[0][k, :, :MODEL_WIDTH] = summed.astype(bf16)
                ring_refs[0][k, :, MODEL_WIDTH:] = tail.astype(bf16)


def backward_body(count, pieces, summed, meta, routes_ref, normed_ref, extra_ref, h_ref, c_ref, a_ref, wo_ref, q_ref, lse_ref, *refs):
    sums = refs[:summed]
    blocks = refs[summed : summed + len(pieces)]
    cos_ref, sin_ref, *outs = refs[summed + len(pieces) :]
    gh_ref, go_ref, gpq_ref, gex_ref, gain_ref = outs[:5]
    ring_refs, ga_s = outs[5:-1], outs[-1]
    rows = q_ref.shape[0]
    place = meta[0]
    normed = normed_ref[...]
    total = ring_total(sums)
    normed_grad, tail = total[:, :MODEL_WIDTH], total[:, MODEL_WIDTH:]
    names = lanes_of((rows, LANES))
    named = routes_ref[...]
    picked = names == named[:, 0:1]
    for j in range(1, TOP):
        picked = jnp.logical_or(picked, names == named[:, j : j + 1])
    row_names = lax.broadcasted_iota(jnp.int32, (LANES, MODEL_WIDTH), 0)
    router = jnp.where(row_names < EXPERTS, extra_ref[...], 0.0).astype(bf16)
    gate = softmax_over(picked, dot_nt(normed, router), 1)
    gate_grad = jnp.where(picked, tail + pltpu.roll(tail, LANES - EXPERTS, 1), 0.0)
    inner = jnp.sum(gate * gate_grad, axis=1, keepdims=True)
    logit_grad = (gate * (gate_grad - inner)).astype(bf16)
    gex_ref[...] = dot_tn(normed, logit_grad)
    normed_grad += dot_nn(logit_grad, router)
    resid = h_ref[...]
    scale_inv = lax.rsqrt(jnp.mean(resid * resid, axis=-1, keepdims=True) + epsilon)
    hat = resid * scale_inv
    gain_ref[...] = jnp.broadcast_to(jnp.sum(normed_grad * hat, axis=0, keepdims=True), gain_ref.shape)
    scaled = normed_grad * extra_ref[EXPERTS + 1 : EXPERTS + 2, :]
    part = scale_inv * (scaled - hat * jnp.mean(scaled * hat, axis=-1, keepdims=True))
    resid_grad = c_ref[...].astype(f32) + part
    gh_ref[...] = resid_grad
    go = (res_scale * resid_grad).astype(bf16)
    go_ref[...] = go
    ga_s[...] = dot_nt(go, wo_ref[...]).astype(bf16)
    cosine, sine = cos_ref[0], sin_ref[0]
    low = lanes_of((rows, LANES)) < HEAD_SIZE

    def variant(seen):
        def group(g, carry):
            lanes = aligned(g * LANES, LANES)
            pair = query_pair(q_ref[:, lanes])
            upstream = ga_s[:, lanes].astype(f32)
            product = (upstream * a_ref[:, lanes].astype(f32)).T
            delta = jnp.concatenate(
                [
                    jnp.sum(product[:HEAD_SIZE], axis=0, keepdims=True),
                    jnp.sum(product[HEAD_SIZE:], axis=0, keepdims=True),
                ],
                axis=1,
            )
            logsum = lse_ref[pl.ds(g, 1), :]
            high_pair = jnp.concatenate(
                [jnp.where(low, 0.0, pltpu.roll(upstream, HEAD_SIZE, 1)), jnp.where(low, 0.0, upstream)], axis=0
            ).astype(bf16)
            query_grad = jnp.zeros((LANES, 2 * rows), f32)
            for k in range(seen):
                keys = block_lanes(pieces, blocks, k, lanes)
                weights = jnp.exp(causal_scores(keys, pair, k) - logsum)
                score_grad = (weights * (dot_nt(keys, high_pair) - delta)).astype(bf16)
                query_grad += dot_tn(keys, score_grad)
                back = dot_nn(score_grad, pair) + dot_nn(weights.astype(bf16), high_pair)
                put_lanes(k, lanes, back)
            query_grad = query_grad[:HEAD_SIZE] * att_scale
            tile = jnp.concatenate([query_grad[:, :rows], query_grad[:, rows:]], axis=0).T
            tile = tile.astype(bf16).astype(f32)
            gpq_ref[:, lanes] = rotate_tile_back(tile, cosine, sine).astype(bf16)
            return carry

        lax.fori_loop(0, KEY_VALUE_HEADS, group, 0)
        for k in range(seen, count):
            ring_put(count, ring_refs, k, rows, jnp.zeros((rows, MODEL_WIDTH), f32))

    def put_lanes(k, lanes, value):
        views = [r.at[..., lanes] for r in ring_refs]
        ring_put(count, views, k, rows, value)

    for seen in range(1, count + 1):
        pl.when(place == seen - 1)(functools.partial(variant, seen))


def store_sets(shards, meta, source, sets, columns):
    rows = MODEL_WIDTH // shards
    for r in range(shards):
        sets[r % 2][r // 2, :, columns] = source[aligned(meta[r] * rows, rows), :].astype(bf16)


def weights_body(count, shards, pieces, meta, a_ref, go_ref, gpq_ref, gex_ref, gain_ref, cos_ref, sin_ref, *refs):
    blocks, parts = refs[: len(pieces)], refs[len(pieces) : -6]
    *sets, gp_s, normed_s, full_s, extra_s = refs[-6:]
    rows = gpq_ref.shape[0]
    low = lanes_of((rows, LANES)) < HEAD_SIZE
    for k in range(count):
        here = slice(k * rows, (k + 1) * rows)
        normed_s[here, :] = block_value(pieces, blocks, k)
        cosine, sine = cos_ref[k], sin_ref[k]
        part = ring_get(count, parts, k, rows).astype(f32)
        for j in range(MODEL_WIDTH // LANES):
            lanes = slice(j * LANES, (j + 1) * LANES)
            tile = part[:, lanes]
            gp_s[here, lanes] = jnp.where(low, rotate_tile_back(tile, cosine, sine), tile).astype(bf16)
    full_s[...] = dot_tn(normed_s[:rows, :], gpq_ref[...]).astype(bf16)
    store_sets(shards, meta, full_s, sets, slice(0, MODEL_WIDTH))
    full_s[...] = dot_tn(normed_s[...], gp_s[...]).astype(bf16)
    store_sets(shards, meta, full_s, sets, slice(MODEL_WIDTH, 2 * MODEL_WIDTH))
    full_s[...] = dot_tn(a_ref[...], go_ref[...]).astype(bf16)
    store_sets(shards, meta, full_s, sets, slice(2 * MODEL_WIDTH, 3 * MODEL_WIDTH))
    row_names = lax.broadcasted_iota(jnp.int32, (LANES, MODEL_WIDTH), 0)
    gains = jnp.where(row_names == EXPERTS + 1, gain_ref[0:1, :], 0.0)
    extra_s[...] = gex_ref[...] + gains.T
    store_sets(shards, meta, extra_s, sets, slice(3 * MODEL_WIDTH, 3 * MODEL_WIDTH + LANES))


def tokens_body(meta, x_ref, gpq_ref, wq_ref, wkv_ref, extra_ref, gh_ref, *refs):
    *sums, cos_ref, sin_ref, grad_ref, gpkv_s = refs
    total = ring_total(sums).astype(bf16).astype(f32)
    cosine, sine = cos_ref[0], sin_ref[0]
    low = lanes_of(cosine.shape) < HEAD_SIZE
    for j in range(MODEL_WIDTH // LANES):
        lanes = slice(j * LANES, (j + 1) * LANES)
        tile = total[:, lanes]
        gpkv_s[:, lanes] = jnp.where(low, rotate_tile_back(tile, cosine, sine), tile).astype(bf16)
    normed_grad = dot_nt(gpq_ref[...], wq_ref[...]) + dot_nt(gpkv_s[...], wkv_ref[...])
    source = x_ref[...].astype(f32)
    scale_inv = lax.rsqrt(jnp.mean(source * source, axis=-1, keepdims=True) + epsilon)
    hat = source * scale_inv
    scaled = normed_grad * extra_ref[EXPERTS : EXPERTS + 1, :]
    part = scale_inv * (scaled - hat * jnp.mean(scaled * hat, axis=-1, keepdims=True))
    grad_ref[...] = gh_ref[...] + part


def dense_update_body(count, rates, meta, *refs):
    quarters, refs = refs[:count], refs[count:]
    ins, outs, rest_s, gain_s = refs[:12], refs[12:28], refs[28], refs[29]
    rows = quarters[0].shape[0]
    step = pl.program_id(0)

    def update(i, gradient):
        weight, first, second = [r[...] for r in ins[3 * i : 3 * i + 3]]
        values = (gradient, *adam_update(weight, gradient, first, second, rates[i]))
        for ref, value in zip(outs[4 * i : 4 * i + 4], values):
            ref[...] = value

    for k in range(count):

        @pl.when(step == k)
        def part(k=k):
            at = pl.ds(pl.multiple_of(lax.rem(meta[0] - k + count, count) * rows, rows), rows)
            gradient = quarters[k][...].astype(f32)
            qkv = gradient[:, : 2 * MODEL_WIDTH]
            product = jnp.sum(qkv * ins[3][...].astype(bf16).astype(f32), axis=1, keepdims=True)
            gain_s[at, :] = jnp.broadcast_to(product, (rows, LANES))
            rest_s[at, :] = gradient[:, 3 * MODEL_WIDTH :]
            update(1, qkv)
            update(2, gradient[:, 2 * MODEL_WIDTH : 3 * MODEL_WIDTH])

    @pl.when(step == count - 1)
    def small():
        rest = rest_s[...].T
        first = gain_s[...].T[0:1] / ins[0][0:1, :].astype(bf16).astype(f32)
        update(0, jnp.concatenate([first, rest[EXPERTS + 1 : EXPERTS + 2]], axis=0))
        update(3, rest[:EXPERTS])


def output_body(meta, h_ref, *refs):
    refs[-1][...] = (h_ref[...] + res_scale * ring_total(refs[:-1])).astype(bf16)


def experts_update_body(rates, rows, parts, rows_of, meta, *refs):
    gradient = rows_of(refs[:parts])
    ins, outs = refs[parts : parts + 6], refs[-8:]
    for i, rate in enumerate(rates):
        own = gradient[: rows[0]] if i == 0 else gradient[rows[0] :]
        weight, first, second = [r[0] for r in ins[3 * i : 3 * i + 3]]
        fresh, first, second = adam_update(weight, own, first, second, rate)
        for ref, value in zip(outs[4 * i : 4 * i + 4], (own, fresh, first, second)):
            ref[0] = value


def experts_update(start, share, arrays, rates, earlier, scalars, after=()):
    shares, share_specs, rows_of = share
    members = shares[0].shape[-3]
    rows = (arrays[0].shape[1], arrays[3].shape[1])

    def spec(a):
        return pl.BlockSpec((1,) + a.shape[1:], lambda e, m: (start + e, 0, 0))

    outs = [shape_of(a.shape, f32) for a in (arrays[0],) * 4 + (arrays[3],) * 4]
    in_specs = share_specs + [spec(a) for a in arrays]
    ins = shares + list(arrays)
    aliases = {}
    if earlier is not None:
        aliases = {1 + len(after) + len(ins) + i: i for i in range(8)}
        in_specs += [pl.BlockSpec(memory_space=pl.ANY)] * 8
        ins += list(earlier)
    return kernel_call(
        functools.partial(experts_update_body, rates, rows, len(shares), rows_of),
        outs,
        ins,
        scalars,
        grid=(members,),
        in_specs=in_specs,
        out_specs=[spec(a) for a in outs],
        limit=60, micros=8,
        after=after,
        aliases=aliases,
    )


def angle_tables(rows, offsets):
    position = (offsets[:, None] + jnp.arange(rows)[None, :]).reshape(-1).astype(f32)
    frequency = 10000.0 ** (-(jnp.arange(HEAD_SIZE // 2).astype(f32) * 2.0 / HEAD_SIZE))
    angles = position[:, None] * frequency[None, :]
    cosine, sine = jnp.cos(angles), jnp.sin(angles)
    shape = (offsets.shape[0], rows, LANES)
    cosine = jnp.concatenate([cosine] * 4, axis=1).reshape(shape)
    return (cosine, jnp.concatenate([-sine, sine] * 2, axis=1).reshape(shape))


def shards_step(
    tokens,
    routes,
    cotangent,
    norm_gains,
    qkv_weight,
    out_weight,
    router_weight,
    expert_up,
    expert_down,
    mean_gains,
    square_gains,
    mean_qkv,
    square_qkv,
    mean_out,
    square_out,
    mean_router,
    square_router,
    mean_up,
    square_up,
    mean_down,
    square_down,
):
    rows = tokens.shape[1]
    count = lax.axis_size("seq")
    shards = lax.axis_size("fsdp")
    shard_rows = MODEL_WIDTH // shards
    local = EXPERTS // count
    early_experts = 3 * local // 4
    chunks = [(0, early_experts), (early_experts, local - early_experts)]
    place = lax.axis_index("seq").astype(jnp.int32)
    owners = (lax.axis_index("fsdp") ^ jnp.arange(shards)).astype(jnp.int32)
    owner_meta = jnp.concatenate([owners, place[None]])
    place_meta = place[None]
    x, c, own_routes = tokens[0], cotangent[0], routes[0]

    def dense_part(piece):
        blank = jnp.zeros((shard_rows // 2, LANES - EXPERTS - 2), f32)
        parts = [qkv_weight[piece], out_weight[piece], router_weight[piece], norm_gains[:, piece].T, blank]
        return jnp.concatenate(parts, axis=1).astype(bf16)

    dense_shards = Gathered(dense_part(slice(0, shard_rows // 2)), dense_part(slice(shard_rows // 2, shard_rows)))
    told = lax.all_gather(c, "seq", axis=0)
    listed = jnp.concatenate([own_routes.T, jnp.zeros_like(own_routes.T)], axis=0).astype(f32).astype(bf16)
    routes_by_block = [listed]
    for k in range(1, count):
        routes_by_block.append(shift_permute(listed, "seq", k))
    cosines, sines = angle_tables(rows, jnp.maximum(place - jnp.arange(count), 0) * rows)
    dense_shards.forward(cosines, sines, *routes_by_block[1:])
    early = dense_shards.arrived()
    dense_pieces = dense_shards.pieces()
    expert_weights = []
    for start, members in chunks:
        mine = slice(start, start + members)
        packed = jnp.concatenate([expert_up[mine], expert_down[mine]], axis=1).astype(bf16)
        expert_weights.append(lax.all_gather(tie(packed, *early), "fsdp", axis=0))

    square = shape_of((MODEL_WIDTH, MODEL_WIDTH))
    wide = shape_of((rows, MODEL_WIDTH))
    wide_f = shape_of((rows, MODEL_WIDTH), f32)
    extra_shape = shape_of((LANES, MODEL_WIDTH), f32)
    unit = 2 * rows * MODEL_WIDTH * MODEL_WIDTH
    wq, wkv, wo, extra, normed_one, q, kv = kernel_call(
        functools.partial(qkv_body, dense_pieces),
        [square, square, square, extra_shape, wide, wide, wide],
        [x] + [a for _, _, a in dense_pieces],
        owner_meta,
        tables=(cosines, sines),
        scratch=[pltpu.VMEM((MODEL_WIDTH, LANES), f32)],
        limit=60, micros=8,
    )
    kv_pieces = ring_gather(kv)
    attended, logsum, resid, normed_two = kernel_call(
        functools.partial(attend_body, count, kv_pieces),
        [wide, shape_of((KEY_VALUE_HEADS, 2 * rows), f32), wide_f, wide],
        [q, x, wo, extra] + [a for _, _, a in kv_pieces],
        place_meta,
        limit=60, micros=12,
    )
    two_pieces = ring_gather(normed_two)

    slots = count * CAP
    packed_rows = (MODEL_WIDTH + FF) // shards
    part_g = part_m = None
    waited = (cosines, sines)
    normed_block = tie(normed_one, *[a for _, _, a in two_pieces[1:]])
    normed_blocks = tuple(shift_permute(normed_block, "seq", k) for k in range(1, count))
    normed_pieces = [(k, 0, a) for k, a in enumerate((normed_one,) + normed_blocks)]
    for i, (start, members) in enumerate(chunks):
        last = i == len(chunks) - 1
        ins = [extra, expert_weights[i], expert_weights[i]] + [a for _, _, a in two_pieces] + [told] + routes_by_block

        def still(a):
            return pl.BlockSpec(a.shape, functools.partial(lambda n, e, m: (0,) * n, a.ndim), pipeline_mode=pl.Buffered(1))

        all_spec = pl.BlockSpec((shards, 1, packed_rows, MODEL_WIDTH), lambda e, m: (0, e, 0, 0))
        set_spec = pl.BlockSpec((shards // 2, 1, packed_rows, MODEL_WIDTH), lambda e, m: (0, e, 0, 0))
        sets = [shape_of((shards // 2, members, packed_rows, MODEL_WIDTH))] * 2
        set_specs = [set_spec] * 2
        if not last:
            sets, set_specs = [shape_of((shards, members, packed_rows, MODEL_WIDTH))], [all_spec]
        up_spec = pl.BlockSpec((shards, 1, shard_rows, MODEL_WIDTH), lambda e, m: (0, e, 0, 0))
        place_down = MODEL_WIDTH // FF
        down_spec = pl.BlockSpec((shards, 1, FF // shards, MODEL_WIDTH), lambda e, m: (0, e, place_down, 0))
        in_specs = [still(extra), up_spec, down_spec] + [still(a) for a in ins[3:]]
        if i > 0:
            ins += [part_g, part_m]
            in_specs += [still(part_g), still(part_m)]
        ring = ring_shapes if last else lambda n, r, w: [shape_of((n, r, w))]
        ring_count = len(ring(count, rows, WIDE))
        outs = sets + ring(count, rows, MODEL_WIDTH) + ring(count, rows, WIDE)
        out_specs = set_specs + [still(a) for a in outs[len(sets) :]]
        scratch = [
            pltpu.VMEM((slots, MODEL_WIDTH), bf16),
            pltpu.VMEM((slots, MODEL_WIDTH), bf16),
            pltpu.VMEM((slots, MODEL_WIDTH), bf16),
            pltpu.VMEM((slots, FF), bf16),
            pltpu.VMEM((slots, 2 * FF), bf16),
            pltpu.VMEM((count, members * CAP, rows), bf16),
            pltpu.VMEM((count, members * CAP, MODEL_WIDTH), bf16),
            pltpu.VMEM((count, members * CAP, MODEL_WIDTH), bf16),
            pltpu.VMEM((MODEL_WIDTH, 2 * FF), bf16),
            pltpu.VMEM((FF, MODEL_WIDTH), bf16),
            pltpu.VMEM((count, EXPERTS, rows), f32),
            pltpu.VMEM((count, EXPERTS, rows), f32),
            pltpu.VMEM((count, EXPERTS, rows), f32),
        ]
        results = kernel_call(
            functools.partial(experts_body, count, shards, two_pieces, start, members, last),
            outs,
            ins,
            owner_meta,
            scratch=scratch,
            grid=(members,),
            in_specs=in_specs,
            out_specs=out_specs,
            micros=8 * members,
            after=waited,
        )
        results = list(results)
        first_part = len(sets)
        part_m, part_g = results[first_part], results[first_part + ring_count]
        mix_parts, ring_parts = results[first_part : first_part + ring_count], results[first_part + ring_count :]
        if not last:
            share = tie(results[0], *normed_blocks)
            share = lax.psum_scatter(share, "fsdp", scatter_dimension=0)

    two_ring = RingSum(ring_parts)
    late_sum = ScatteredExperts(tie(results[1], *two_ring.near()), results[0], place_meta)
    two_sums = two_ring.parts()
    sent = late_sum.first(*two_ring.sent)
    mixing = RingSum(mix_parts, *two_sums[3:], *sent)
    ring = ring_shapes(count, rows, MODEL_WIDTH)
    results = kernel_call(
        functools.partial(backward_body, count, kv_pieces, len(two_sums)),
        [wide_f, wide, wide, shape_of((MODEL_WIDTH, LANES), f32), shape_of((8, MODEL_WIDTH), f32)] + ring,
        [own_routes, normed_two, extra, resid, c, attended, wo, q, logsum]
        + list(two_sums)
        + [a for _, _, a in kv_pieces],
        place_meta,
        tables=(cosines, sines),
        scratch=[pltpu.VMEM((rows, MODEL_WIDTH), bf16)],
        limit=60, micros=22,
    )
    resid_grad, go, gpq, router_grad, gain_grad = results[:5]
    mix_sums = mixing.parts()
    dense_set = shape_of((shards // 2, shard_rows, 3 * MODEL_WIDTH + LANES))
    keep, send = kernel_call(
        functools.partial(weights_body, count, shards, normed_pieces),
        [dense_set] * 2,
        [attended, go, gpq, router_grad, gain_grad, cosines, sines]
        + [a for _, _, a in normed_pieces]
        + list(results[5:]),
        owner_meta,
        scratch=[
            pltpu.VMEM((count * rows, MODEL_WIDTH), bf16),
            pltpu.VMEM((count * rows, MODEL_WIDTH), bf16),
            pltpu.VMEM((MODEL_WIDTH, MODEL_WIDTH), bf16),
            pltpu.VMEM((MODEL_WIDTH, LANES), f32),
        ],
        after=mixing.near(),
        limit=60, micros=12,
    )
    dense_sum = Scattered(place_meta)
    dense_sum.add(send, keep, *mix_sums[3:])
    rates = (learn_rates[4], learn_rates[5])
    experts = (expert_up, mean_up, square_up, expert_down, mean_down, square_down)
    sent = dense_sum.first()
    kv_ring = RingSum(results[5:], *mix_sums[3:])
    spec = pl.BlockSpec((1,) + share.shape[1:], lambda e, m: (e, 0, 0))
    total = ([share], [spec], lambda refs: refs[0][0].astype(f32))
    updated = experts_update(chunks[0][0], total, experts, rates, None, place_meta, sent)
    kv_sums = kv_ring.parts(*dense_sum.second(updated[0]))
    own = dense_sum.total(count, *kv_ring.sent)
    late_sum.depart(own)
    quarters = lax.all_to_all(own, "seq", split_axis=0, concat_axis=0, tiled=True)
    (tokens_grad,) = kernel_call(
        tokens_body,
        [wide_f],
        [x, gpq, wq, wkv, extra, resid_grad] + list(kv_sums),
        place_meta,
        tables=(cosines, sines),
        scratch=[pltpu.VMEM((rows, MODEL_WIDTH), bf16)],
        after=(own,),
        limit=60, micros=6,
    )
    quarter = jnp.sum(tie(quarters, tokens_grad, *late_sum.second(tokens_grad)).astype(f32), axis=0).astype(bf16)
    (output,) = kernel_call(output_body, [wide], [resid] + mix_sums, place_meta, after=(quarter,), micros=3)
    tokens_grad, output = tokens_grad[None], output[None]
    quarters = [quarter] + [shift_permute(quarter, "seq", k) for k in range(1, count)]
    updated = experts_update(chunks[1][0], late_sum.total(), experts, rates, updated, place_meta, (quarter,))
    dense_ins = [norm_gains, mean_gains, square_gains, qkv_weight, mean_qkv, square_qkv]
    dense_ins += [out_weight, mean_out, square_out, router_weight.T, mean_router.T, square_router.T]
    part_rows = shard_rows // count

    def whole_spec(a):
        return pl.BlockSpec(a.shape, lambda k, m: (0,) * a.ndim)

    def part_spec(a):
        return pl.BlockSpec((part_rows, a.shape[1]), lambda k, m: (lax.rem(m[0] - k + count, count), 0))

    specs = [whole_spec, part_spec, part_spec, whole_spec]
    dense_outs = kernel_call(
        functools.partial(dense_update_body, count, learn_rates[:4]),
        [shape_of(a.shape, f32) for a in dense_ins[::3] for _ in range(4)],
        quarters + dense_ins,
        place_meta,
        scratch=[pltpu.VMEM((shard_rows, LANES), f32), pltpu.VMEM((shard_rows, LANES), f32)],
        grid=(count,),
        in_specs=[whole_spec(a) for a in quarters] + [specs[i // 3](a) for i, a in enumerate(dense_ins)],
        out_specs=[specs[i](dense_ins[3 * i]) for i in range(4) for _ in range(4)],
        after=(updated[0],),
        limit=60, micros=5,
    )
    shard_gains, fresh_gains, momentum_gains, variance_gains = dense_outs[:4]
    shard_qkv, fresh_qkv, momentum_qkv, variance_qkv = dense_outs[4:8]
    shard_out, fresh_out, momentum_out, variance_out = dense_outs[8:12]
    shard_router, fresh_router, momentum_router, variance_router = [a.T for a in dense_outs[12:]]
    shard_up, fresh_up, momentum_up, variance_up = updated[:4]
    shard_down, fresh_down, momentum_down, variance_down = updated[4:]
    return (
        output,
        tokens_grad,
        shard_gains,
        shard_qkv,
        shard_out,
        shard_router,
        shard_up,
        shard_down,
        fresh_gains,
        fresh_qkv,
        fresh_out,
        fresh_router,
        fresh_up,
        fresh_down,
        momentum_gains,
        momentum_qkv,
        momentum_out,
        momentum_router,
        momentum_up,
        momentum_down,
        variance_gains,
        variance_qkv,
        variance_out,
        variance_router,
        variance_up,
        variance_down,
    )


def solution(mesh):
    block = P("fsdp", "seq", None)
    gains, dense, experts = P(None, "fsdp"), P("fsdp", None), P("seq", "fsdp", None)
    weights = (gains, dense, dense, dense, experts, experts)
    moments = tuple(s for spec in weights for s in (spec, spec))
    return jax.shard_map(
        shards_step,
        mesh=mesh,
        in_specs=(block, block, block) + weights + moments,
        out_specs=(block, block) + weights * 4,
        check_vma=False,
    )
```

```python
import functools

import jax
import jax.numpy as jnp
from jax import lax
from jax.experimental import pallas as pl
from jax.experimental.pallas import tpu as pltpu
from jax.sharding import PartitionSpec as P

MODEL_WIDTH = 1024
QUERY_HEADS = 16
KEY_VALUE_HEADS = 8
HEAD_SIZE = 64
EXPERTS = 32
FF = 512
TOP = 8
STEP = 3
CAP = 96
LANES = 128
TILE = 256

epsilon = 1e-06
res_scale = 0.22
att_scale = 0.015625
beta_one = 0.9
beta_two = 0.95
adam_eps = 1e-08
weight_decay = 0.1
learn_rates = (0.4, 0.04, 0.2, 0.01, 0.01, 0.05)

bf16 = jnp.bfloat16
f32 = jnp.float32
WIDE = MODEL_WIDTH + LANES


def adam_update(weight, gradient, first, second, rate):
    first_new = beta_one * first + (1.0 - beta_one) * gradient
    second_new = beta_two * second + (1.0 - beta_two) * gradient * gradient
    first_hat = first_new * (1.0 / (1.0 - beta_one**STEP))
    second_hat = second_new * (1.0 / (1.0 - beta_two**STEP))
    fresh = weight - rate * (first_hat / (jnp.sqrt(second_hat) + adam_eps) + weight_decay * weight)
    return (fresh, first_new, second_new)


def dot_nn(a, b):
    return lax.dot_general(a, b, (((1,), (0,)), ((), ())), preferred_element_type=f32)


def dot_nt(a, b):
    return lax.dot_general(a, b, (((1,), (1,)), ((), ())), preferred_element_type=f32)


def dot_tn(a, b):
    return lax.dot_general(a, b, (((0,), (0,)), ((), ())), preferred_element_type=f32)


def lanes_of(shape):
    return lax.broadcasted_iota(jnp.int32, shape, len(shape) - 1)


def aligned(index, size):
    if isinstance(index, int):
        return slice(index, index + size)
    return pl.ds(pl.multiple_of(index, size), size)


def kernel_call(body, outs, ins, scalars, scratch=(), grid=None, in_specs=None, out_specs=None, limit=60, after=(), micros=10, aliases=None, tables=()):
    in_specs = in_specs or [pl.BlockSpec(memory_space=pltpu.VMEM)] * len(ins)
    for a in tables:
        ins = list(ins) + [a]
        in_specs = in_specs + [pl.BlockSpec((1,) + a.shape[1:], lambda i, m: (0, 0, 0))]
    out_specs = out_specs or [pl.BlockSpec(memory_space=pltpu.VMEM)] * len(outs)
    in_specs = [pl.BlockSpec(memory_space=pl.ANY)] * len(after) + in_specs

    def ordered_body(meta, *refs):
        body(meta, *refs[len(after) :])

    return pl.pallas_call(
        ordered_body,
        out_shape=outs,
        grid_spec=pltpu.PrefetchScalarGridSpec(
            num_scalar_prefetch=1,
            grid=grid or (1,),
            in_specs=in_specs,
            out_specs=out_specs,
            scratch_shapes=list(scratch),
        ),
        compiler_params=pltpu.CompilerParams(vmem_limit_bytes=limit * 1024 * 1024),
        input_output_aliases=aliases or {},
        cost_estimate=pl.CostEstimate(flops=micros * 10**9, bytes_accessed=micros * 10**6, transcendentals=0),
    )(scalars, *after, *ins)


def streamed_call(body, outs, ins, scalars, scratch=(), after=(), micros=10, sends=32):
    shapes = [a.shape for a in ins]
    count, made = len(ins), len(outs)
    anywhere = pl.BlockSpec(memory_space=pl.ANY)

    def kernel(meta, *refs):
        refs = refs[len(after) :]
        source, target, refs = refs[:count], refs[count : count + made], refs[count + made :]
        held, rest = refs[:count], refs[count:-2]
        arrive, leave = refs[-2:]
        inbound = [pltpu.make_async_copy(a, b, arrive.at[i]) for i, (a, b) in enumerate(zip(source, held))]
        for copy in inbound:
            copy.start()
        waited, outbound = set(), []

        def need(*wanted):
            for ref in wanted:
                i = next(i for i, b in enumerate(held) if b is ref)
                if i not in waited:
                    waited.add(i)
                    inbound[i].wait()

        def send(ref, place, columns=None):
            to = target[place] if columns is None else target[place].at[:, :, columns]
            copy = pltpu.make_async_copy(ref, to, leave.at[len(outbound)])
            copy.start()
            outbound.append(copy)

        body(meta, need, send, *held, *rest)
        need(*held)
        for copy in outbound:
            copy.wait()

    return pl.pallas_call(
        kernel,
        out_shape=outs,
        grid_spec=pltpu.PrefetchScalarGridSpec(
            num_scalar_prefetch=1,
            grid=(1,),
            in_specs=[anywhere] * (len(after) + count),
            out_specs=[anywhere] * made,
            scratch_shapes=[pltpu.VMEM(shape, a.dtype) for shape, a in zip(shapes, ins)]
            + list(scratch)
            + [pltpu.SemaphoreType.DMA((count,)), pltpu.SemaphoreType.DMA((sends,))],
        ),
        compiler_params=pltpu.CompilerParams(vmem_limit_bytes=60 * 1024 * 1024),
        cost_estimate=pl.CostEstimate(flops=micros * 10**9, bytes_accessed=micros * 10**6, transcendentals=0),
    )(scalars, *after, *ins)


def tie(value, *earlier):
    anywhere = pl.BlockSpec(memory_space=pl.ANY)
    return pl.pallas_call(
        lambda *refs: None,
        out_shape=shape_of(value.shape, value.dtype),
        in_specs=[anywhere] * (1 + len(earlier)),
        out_specs=anywhere,
        input_output_aliases={0: 0},
    )(value, *earlier)


def shape_of(shape, kind=bf16):
    return jax.ShapeDtypeStruct(shape, kind)


def xor_permute(value, axis, mask):
    return lax.ppermute(value, axis, [(i, i ^ mask) for i in range(lax.axis_size(axis))])


def shift_permute(value, axis, step):
    size = lax.axis_size(axis)
    return lax.ppermute(value, axis, [(i, (i + step) % size) for i in range(size)])


class Gathered:
    def __init__(self, first, second):
        self.plain = lax.axis_size("fsdp") != 8
        self.first, self.second = first, second
        self.half = first.shape[0]
        if not self.plain:
            self.x_first = xor_permute(first, "fsdp", 2)
            self.y_second = xor_permute(second, "fsdp", 4)
            self.x_second = xor_permute(second, "fsdp", 2)
            self.y_first = xor_permute(first, "fsdp", 4)

    def forward(self, *earlier):
        if self.plain:
            return
        self.x_first = tie(self.x_first, *earlier)
        self.y_second = tie(self.y_second, *earlier)
        self.far_first = xor_permute(self.x_first, "fsdp", 4)
        self.far_second = xor_permute(self.y_second, "fsdp", 2)

    def arrived(self):
        return () if self.plain else (self.far_first, self.far_second)

    def pieces(self):
        count, half = lax.axis_size("fsdp"), self.half
        if self.plain:
            whole = lax.all_gather(jnp.concatenate([self.first, self.second]), "fsdp", axis=0)
            whole = jnp.take(whole, lax.axis_index("fsdp") ^ jnp.arange(count), axis=0)
            return [(r, 0, whole[r]) for r in range(count)]
        mine = [(0, 0, self.first), (0, half, self.second), (2, 0, self.x_first), (2, half, self.x_second)]
        mine += [(4, 0, self.y_first), (4, half, self.y_second), (6, 0, self.far_first), (6, half, self.far_second)]
        return mine + [(r + 1, row, xor_permute(a, "fsdp", 1)) for r, row, a in mine]


def pairs_body(groups, meta, *refs):
    sent_x, sent_y, rest = refs[2 * groups :]
    left = 0
    for keep, got in zip(refs[:groups], refs[groups : 2 * groups]):
        half, columns = keep.shape[1] // 2, keep.shape[2]
        lanes = slice(left, left + columns)
        left += columns

        def pair(i, part):
            piece = slice(part * half, (part + 1) * half)
            return (keep[i, piece, :].astype(f32) + got[i, piece, :].astype(f32)).astype(bf16)

        for ref, place, value in (
            (sent_x, 0, pair(3, 0)),
            (sent_x, 1, pair(1, 0)),
            (sent_y, 0, pair(3, 1)),
            (sent_y, 1, pair(2, 1)),
            (rest, 0, pair(0, 0)),
            (rest, 1, pair(0, 1)),
            (rest, 2, pair(1, 1)),
            (rest, 3, pair(2, 0)),
        ):
            ref[place, :, lanes] = value


def passed_body(meta, rest, over_x, over_y, then_x, then_y):
    then_x[...] = (rest[2].astype(f32) + over_y[0].astype(f32)).astype(bf16)
    then_y[...] = (rest[3].astype(f32) + over_x[0].astype(f32)).astype(bf16)


def summed_body(meta, rest, over_x, over_y, then_x, then_y, total):
    half = rest.shape[1]
    first = (rest[0].astype(f32) + over_x[1].astype(f32) + then_y[...].astype(f32)).astype(bf16)
    second = (rest[1].astype(f32) + over_y[1].astype(f32) + then_x[...].astype(f32)).astype(bf16)
    places, rows = total.shape[:2]
    for k in range(places):
        source, row = (first, k * rows) if k * rows < half else (second, k * rows - half)
        total[k] = source[row : row + rows]


class Scattered:
    def __init__(self, scalars):
        self.plain = lax.axis_size("fsdp") != 8
        self.scalars = scalars
        self.send, self.keep, self.got = [], [], []

    def add(self, send, keep, *earlier):
        self.send.append(send)
        self.keep.append(keep)
        if not self.plain:
            self.got.append(xor_permute(tie(send, *earlier) if earlier else send, "fsdp", 1))

    def first(self, *earlier):
        if self.plain:
            return ()
        rows, columns = self.keep[0].shape[1], sum(a.shape[2] for a in self.keep)
        two, four = shape_of((2, rows // 2, columns)), shape_of((4, rows // 2, columns))
        body = functools.partial(pairs_body, len(self.keep))
        sent_x, sent_y, self.rest = kernel_call(
            body, [two, two, four], self.keep + self.got, self.scalars, after=earlier, limit=24, micros=3
        )
        self.over_x = xor_permute(sent_x, "fsdp", 2)
        self.over_y = xor_permute(sent_y, "fsdp", 4)
        return (sent_x, sent_y)

    def second(self, *earlier):
        if self.plain:
            return ()
        if earlier:
            self.over_x, self.over_y = tie(self.over_x, *earlier), tie(self.over_y, *earlier)
        sent_x = (self.rest[2].astype(f32) + self.over_y[0].astype(f32)).astype(bf16)
        sent_y = (self.rest[3].astype(f32) + self.over_x[0].astype(f32)).astype(bf16)
        self.then_x = xor_permute(sent_x, "fsdp", 2)
        self.then_y = xor_permute(sent_y, "fsdp", 4)
        return (sent_x, sent_y)

    def total(self, places, *earlier):
        if self.plain:
            count = lax.axis_size("fsdp")
            keep, send = jnp.concatenate(self.keep, axis=2), jnp.concatenate(self.send, axis=2)
            both = jnp.stack([keep, send], axis=1).reshape((count,) + keep.shape[1:])
            both = jnp.take(both, lax.axis_index("fsdp") ^ jnp.arange(count), axis=0)
            total = lax.psum_scatter(both, "fsdp", scatter_dimension=0)
            return total.reshape((places, -1, total.shape[1]))
        if earlier:
            self.then_x = tie(self.then_x, *earlier)
        first = self.rest[0].astype(f32) + self.over_x[1].astype(f32) + self.then_y.astype(f32)
        second = self.rest[1].astype(f32) + self.over_y[1].astype(f32) + self.then_x.astype(f32)
        return jnp.concatenate([first, second]).astype(bf16).reshape((places, -1, first.shape[1]))


def expert_pairs_body(meta, keep, got, sent_x, sent_y, rest):
    half = keep.shape[2] // 2

    def pair(i, part):
        piece = slice(part * half, (part + 1) * half)
        return (keep[i, 0, piece, :].astype(f32) + got[i, 0, piece, :].astype(f32)).astype(bf16)

    sent_x[0, 0], sent_x[1, 0] = pair(3, 0), pair(1, 0)
    sent_y[0, 0], sent_y[1, 0] = pair(3, 1), pair(2, 1)
    rest[0, 0], rest[1, 0], rest[2, 0], rest[3, 0] = pair(0, 0), pair(0, 1), pair(1, 1), pair(2, 0)


def expert_passed_body(meta, rest, over_x, over_y, then_x, then_y):
    then_x[0] = (rest[0, 0].astype(f32) + over_y[0, 0].astype(f32)).astype(bf16)
    then_y[0] = (rest[1, 0].astype(f32) + over_x[0, 0].astype(f32)).astype(bf16)


class ScatteredExperts:
    def __init__(self, send, keep, scalars):
        self.plain = lax.axis_size("fsdp") != 8
        self.send, self.keep, self.scalars = send, keep, scalars
        if not self.plain:
            self.got = xor_permute(send, "fsdp", 1)

    def first(self, *earlier):
        if self.plain:
            return ()
        sets, self.members, rows, columns = self.keep.shape
        half = rows // 2

        def group(n, start=0):
            return pl.BlockSpec((n, 1, half, columns), lambda e, m: (start, e, 0, 0))

        self.group = group
        self.single = pl.BlockSpec((1, half, columns), lambda e, m: (e, 0, 0))
        whole = pl.BlockSpec((sets, 1, rows, columns), lambda e, m: (0, e, 0, 0))
        shapes = [shape_of((n, self.members, half, columns)) for n in (2, 2, 4)]
        sent_x, sent_y, self.rest = kernel_call(
            expert_pairs_body,
            shapes,
            [self.keep, self.got],
            self.scalars,
            grid=(self.members,),
            in_specs=[whole, whole],
            out_specs=[group(2), group(2), group(4)],
            after=earlier,
            limit=60, micros=6,
        )
        self.sent = (sent_x, sent_y)
        return self.sent

    def depart(self, *earlier):
        if self.plain:
            return
        self.over_x = xor_permute(tie(self.sent[0], *earlier), "fsdp", 2)
        self.over_y = xor_permute(tie(self.sent[1], *earlier), "fsdp", 4)

    def arrived(self):
        return () if self.plain else (self.over_x, self.over_y)

    def second(self, *earlier):
        if self.plain:
            return ()
        one = shape_of(self.rest.shape[1:])
        sent_x, sent_y = kernel_call(
            expert_passed_body,
            [one, one],
            [self.rest, self.over_x, self.over_y],
            self.scalars,
            grid=(self.members,),
            in_specs=[self.group(2, 1), self.group(1), self.group(1)],
            out_specs=[self.single, self.single],
            after=earlier,
            limit=60, micros=4,
        )
        self.then_x = xor_permute(sent_x, "fsdp", 2)
        self.then_y = xor_permute(sent_y, "fsdp", 4)
        return (sent_x, sent_y)

    def total(self):
        if self.plain:
            count = lax.axis_size("fsdp")
            both = jnp.stack([self.keep, self.send], axis=1).reshape((count,) + self.keep.shape[1:])
            both = jnp.take(both, lax.axis_index("fsdp") ^ jnp.arange(count), axis=0)
            share = lax.psum_scatter(both, "fsdp", scatter_dimension=0)
            spec = pl.BlockSpec((1,) + share.shape[1:], lambda e, m: (e, 0, 0))
            return ([share], [spec], lambda refs: refs[0][0].astype(f32))
        arrays = [self.rest, self.over_x, self.over_y, self.then_x, self.then_y]
        specs = [self.group(2), self.group(1, 1), self.group(1, 1), self.single, self.single]

        def rows_of(refs):
            rest, over_x, over_y, then_x, then_y = refs
            first = rest[0, 0].astype(f32) + over_x[0, 0].astype(f32) + then_y[0].astype(f32)
            second = rest[1, 0].astype(f32) + over_y[0, 0].astype(f32) + then_x[0].astype(f32)
            return jnp.concatenate([first, second], axis=0)

        return (arrays, specs, rows_of)


class Ringed:
    def __init__(self, block):
        self.plain = lax.axis_size("seq") != 4
        self.block = block
        self.half = block.shape[0] // 2
        if not self.plain:
            self.below = shift_permute(block, "seq", 1)
            self.above = shift_permute(block, "seq", -1)

    def near(self):
        return () if self.plain else (self.below, self.above)

    def forward(self):
        if self.plain:
            return ()
        self.far_first = shift_permute(self.below[: self.half], "seq", 1)
        self.far_second = shift_permute(self.above[self.half :], "seq", -1)
        return (self.far_first, self.far_second)

    def pieces(self):
        count = lax.axis_size("seq")
        if self.plain:
            whole = lax.all_gather(self.block, "seq", axis=0)
            whole = jnp.take(whole, (lax.axis_index("seq") - jnp.arange(count)) % count, axis=0)
            return [(k, 0, whole[k]) for k in range(count)]
        pieces = [(0, 0, self.block), (1, 0, self.below), (3, 0, self.above)]
        return pieces + [(2, 0, self.far_first), (2, self.half, self.far_second)]


def ring_gather(block):
    ring = Ringed(block)
    ring.forward()
    return ring.pieces()


def ring_shapes(count, rows, columns):
    if count != 4:
        return [shape_of((count, rows, columns))]
    half = rows // 2
    return [shape_of((r, columns)) for r in (rows, rows, rows, half, half)]


def ring_put(count, refs, k, rows, value):
    half = rows // 2
    width = value.shape[1]
    value = value.astype(bf16)
    if count != 4:
        refs[0][k, :, :width] = value
        return
    own, down, up, keep_down, keep_up = refs
    places = {
        0: ((own, 0), (own, half)),
        1: ((keep_down, 0), (down, half)),
        2: ((down, 0), (up, 0)),
        3: ((up, half), (keep_up, 0)),
    }
    for part, (ref, row) in enumerate(places[k]):
        ref[row : row + half, :width] = value[part * half : (part + 1) * half]


def ring_put_tail(count, refs, k, rows, value):
    half = rows // 2
    value = value.astype(bf16)
    if count != 4:
        refs[0][k, :, MODEL_WIDTH:] = value
        return
    own, down, up, keep_down, keep_up = refs
    places = {
        0: ((own, 0), (own, half)),
        1: ((keep_down, 0), (down, half)),
        2: ((down, 0), (up, 0)),
        3: ((up, half), (keep_up, 0)),
    }
    for part, (ref, row) in enumerate(places[k]):
        ref[row : row + half, MODEL_WIDTH:] = value[part * half : (part + 1) * half]


def ring_get(count, refs, k, rows):
    if count != 4:
        return refs[0][k]
    half = rows // 2
    own, down, up, keep_down, keep_up = refs
    if k == 0:
        return own[...]
    first, second = {
        1: ((keep_down, 0), (down, half)),
        2: ((down, 0), (up, 0)),
        3: ((up, half), (keep_up, 0)),
    }[k]
    return jnp.concatenate([ref[row : row + half, :] for ref, row in (first, second)], axis=0)


class RingSum:
    def __init__(self, arrays, *earlier):
        self.plain = lax.axis_size("seq") != 4
        self.arrays = list(arrays)
        self.sent = ()
        if not self.plain:
            own, down, up, keep_down, keep_up = self.arrays
            if earlier:
                down, up = tie(down, *earlier), tie(up, *earlier)
            self.from_above = shift_permute(down, "seq", -1)
            self.from_below = shift_permute(up, "seq", 1)

    def near(self):
        return () if self.plain else (self.from_above, self.from_below)

    def parts(self, *earlier):
        if self.plain:
            count = lax.axis_size("seq")
            whole = jnp.take(self.arrays[0], (lax.axis_index("seq") - jnp.arange(count)) % count, axis=0)
            return [lax.psum_scatter(whole, "seq", scatter_dimension=0)]
        own, down, up, keep_down, keep_up = self.arrays
        half = keep_down.shape[0]
        if earlier:
            self.from_above = tie(self.from_above, *earlier)
            self.from_below = tie(self.from_below, *earlier)
        then_down = (keep_down.astype(f32) + self.from_above[:half].astype(f32)).astype(bf16)
        then_up = (keep_up.astype(f32) + self.from_below[:half].astype(f32)).astype(bf16)
        self.sent = (then_down, then_up)
        last_above = shift_permute(then_down, "seq", -1)
        last_below = shift_permute(then_up, "seq", 1)
        return [own, self.from_above, self.from_below, last_above, last_below]


def ring_total(refs):
    if len(refs) == 1:
        return refs[0][...].astype(f32)
    own, above, below, last_above, last_below = [r[...].astype(f32) for r in refs]
    half = own.shape[0] // 2
    first = own[:half] + below[half:] + last_above
    second = own[half:] + above[half:] + last_below
    return jnp.concatenate([first, second], axis=0)


def block_value(pieces, refs, k):
    found = [(row, ref) for (kk, row, _), ref in zip(pieces, refs) if kk == k]
    found.sort(key=lambda entry: entry[0])
    if len(found) == 1:
        return found[0][1][...]
    return jnp.concatenate([ref[...] for _, ref in found], axis=0)


def block_lanes(pieces, refs, k, lanes):
    found = [(row, ref) for (kk, row, _), ref in zip(pieces, refs) if kk == k]
    found.sort(key=lambda entry: entry[0])
    if len(found) == 1:
        return found[0][1][:, lanes]
    return jnp.concatenate([ref[:, lanes] for _, ref in found], axis=0)


def rotate_tile(tile, cosine, sine):
    first = lanes_of(tile.shape) % HEAD_SIZE < HEAD_SIZE // 2
    turned = jnp.where(first, pltpu.roll(tile, LANES - HEAD_SIZE // 2, 1), pltpu.roll(tile, HEAD_SIZE // 2, 1))
    return tile * cosine + turned * sine


def rotate_tile_back(tile, cosine, sine):
    return rotate_tile(tile, cosine, -sine)


def qkv_body(pieces, meta, x_ref, *refs):
    shards = refs[: len(pieces)]
    cos_ref, sin_ref, *refs = refs[len(pieces) :]
    wq_ref, wkv_ref, wo_ref, extra_ref, normed_ref, q_ref, kv_ref, columns = refs
    shard_rows = MODEL_WIDTH // max(r + 1 for r, _, _ in pieces)
    for (r, row, value), ref in zip(pieces, shards):
        rows = value.shape[0]
        place = pl.ds(pl.multiple_of(meta[r] * shard_rows + row, rows), rows)
        wq_ref[place, :] = ref[:, :MODEL_WIDTH]
        wkv_ref[place, :] = ref[:, MODEL_WIDTH : 2 * MODEL_WIDTH]
        wo_ref[place, :] = ref[:, 2 * MODEL_WIDTH : 3 * MODEL_WIDTH]
        columns[place, :] = ref[:, 3 * MODEL_WIDTH :].astype(f32)
    extra_ref[...] = columns[...].T
    source = x_ref[...].astype(f32)
    scale_inv = lax.rsqrt(jnp.mean(source * source, axis=-1, keepdims=True) + epsilon)
    normed = (source * scale_inv * extra_ref[EXPERTS : EXPERTS + 1, :]).astype(bf16)
    normed_ref[...] = normed
    cosine, sine = cos_ref[0], sin_ref[0]
    low = lanes_of(cosine.shape) < HEAD_SIZE
    for j in range(MODEL_WIDTH // TILE):
        block = dot_nn(normed, wq_ref[:, j * TILE : (j + 1) * TILE])
        for i in range(TILE // LANES):
            at = j * TILE + i * LANES
            tile = block[:, i * LANES : (i + 1) * LANES]
            q_ref[:, at : at + LANES] = rotate_tile(tile, cosine, sine).astype(bf16)
    for j in range(MODEL_WIDTH // TILE):
        block = dot_nn(normed, wkv_ref[:, j * TILE : (j + 1) * TILE])
        for i in range(TILE // LANES):
            at = j * TILE + i * LANES
            tile = block[:, i * LANES : (i + 1) * LANES]
            tile = jnp.where(low, rotate_tile(tile, cosine, sine), tile).astype(bf16)
            kv_ref[:, at : at + LANES] = tile


def causal_scores(keys, pair, k):
    scores = dot_nt(keys, pair)
    if k == 0:
        rows = keys.shape[0]
        query = lanes_of(scores.shape) % rows
        scores = jnp.where(query >= lax.broadcasted_iota(jnp.int32, scores.shape, 0), scores, -jnp.inf)
    return scores


def query_pair(tile):
    low = lanes_of(tile.shape) < HEAD_SIZE
    tile = tile.astype(f32) * att_scale
    even = jnp.where(low, tile, 0.0)
    odd = jnp.where(low, pltpu.roll(tile, HEAD_SIZE, 1), 0.0)
    return jnp.concatenate([even, odd], axis=0).astype(bf16)


def attend_body(count, pieces, meta, q_ref, x_ref, wo_ref, extra_ref, *refs):
    blocks = refs[: len(pieces)]
    a_ref, lse_ref, h_ref, normed_ref = refs[len(pieces) :]
    rows = q_ref.shape[0]
    place = meta[0]

    def variant(seen):
        def group(g, carry):
            lanes = aligned(g * LANES, LANES)
            pair = query_pair(q_ref[:, lanes])
            keys = [block_lanes(pieces, blocks, k, lanes) for k in range(seen)]
            scores = [causal_scores(keys[k], pair, k) for k in range(seen)]
            top = functools.reduce(jnp.maximum, [jnp.max(s, axis=0, keepdims=True) for s in scores])
            weights = [jnp.exp(s - top) for s in scores]
            total = functools.reduce(jnp.add, [jnp.sum(w, axis=0, keepdims=True) for w in weights])
            summed = functools.reduce(jnp.add, [dot_tn(t, w.astype(bf16)) for w, t in zip(weights, keys)])
            summed = summed[HEAD_SIZE:] * (1.0 / total)
            both = jnp.concatenate([summed[:, :rows], summed[:, rows:]], axis=0)
            a_ref[:, lanes] = both.T.astype(bf16)
            lse_ref[pl.ds(g, 1), :] = top + jnp.log(total)
            return carry

        lax.fori_loop(0, KEY_VALUE_HEADS, group, 0)

    for seen in range(1, count + 1):
        pl.when(place == seen - 1)(functools.partial(variant, seen))
    resid = x_ref[...].astype(f32) + res_scale * dot_nn(a_ref[...], wo_ref[...])
    h_ref[...] = resid
    scale_inv = lax.rsqrt(jnp.mean(resid * resid, axis=-1, keepdims=True) + epsilon)
    normed_ref[...] = (resid * scale_inv * extra_ref[EXPERTS + 1 : EXPERTS + 2, :]).astype(bf16)


def softmax_over(picked, logits, axis):
    top = jnp.max(jnp.where(picked, logits, -jnp.inf), axis=axis, keepdims=True)
    raised = jnp.where(picked, jnp.exp(jnp.minimum(logits - top, 0.0)), 0.0)
    return raised / jnp.sum(raised, axis=axis, keepdims=True)


def experts_body(count, shards, pieces, start, members, last, meta, extra_ref, *refs):
    refs = list(refs)

    def take(number):
        taken = refs[:number]
        del refs[:number]
        return taken

    up_w, down_w = take(2)
    blocks, (told,), listed = take(len(pieces)), take(1), take(count)
    if start > 0:
        (part_g, part_m) = take(2)
    keep_ref, send_ref = take(2) if last else (take(1) + [None])
    ring_count = len(ring_shapes(count, TILE, WIDE)) if last else 1
    mix_refs, ring_refs = take(ring_count), take(ring_count)
    x_s, c_s, ge_s, a_s, gu_s, d_s, eg_s, gs_s, gup_s, gdown_s, gate_s, rank_s, gg_s = refs
    step = pl.program_id(0)
    local = EXPERTS // count
    up_rows, down_rows = MODEL_WIDTH // shards, FF // shards
    slots = count * CAP
    place = meta[shards]
    expert = place * local + start + step

    def absolute(k):
        return lax.rem(place - k + count, count)

    @pl.when(step == 0)
    def routing():
        router = extra_ref[:EXPERTS, :].astype(bf16)
        later = (
            lax.broadcasted_iota(jnp.int32, (TILE, TILE), 0) < lax.broadcasted_iota(jnp.int32, (TILE, TILE), 1)
        )
        later = jnp.where(later, 1.0, 0.0).astype(bf16)
        names = lax.broadcasted_iota(jnp.int32, (EXPERTS, TILE), 0).astype(f32)
        for k in range(count):
            named = listed[k][...].astype(f32)
            picked = names == named[0:1, :]
            for j in range(1, TOP):
                picked = jnp.logical_or(picked, names == named[j : j + 1, :])
            logits = dot_nt(router, block_value(pieces, blocks, k))
            gate_s[k] = softmax_over(picked, logits, 0)
            before = dot_nn(jnp.where(picked, 1.0, 0.0).astype(bf16), later)
            rank_s[k] = jnp.where(picked, before, -1.0)
        gg_s[...] = jnp.zeros_like(gg_s)

    def up_columns(columns):
        return up_w[:, 0, :, columns].reshape(MODEL_WIDTH, TILE)

    def up_tile(j):
        here = slice(j * TILE // up_rows, (j + 1) * TILE // up_rows)
        return up_w[here, 0, :, :].reshape(TILE, 2 * FF)

    def down_columns(columns):
        return down_w[:, 0, :, columns].reshape(FF, TILE)

    def down_tile(j):
        here = slice(j * TILE // down_rows, (j + 1) * TILE // down_rows)
        return down_w[here, 0, :, :].reshape(TILE, MODEL_WIDTH)

    wanted = lax.broadcasted_iota(jnp.int32, (CAP, TILE), 0).astype(f32)
    held = aligned(step * CAP, CAP)
    gates = []
    for k in range(count):
        rank = rank_s[k, pl.ds(expert, 1), :]
        gate = gate_s[k, pl.ds(expert, 1), :]
        hit = wanted == rank
        chosen = jnp.where(hit, 1.0, 0.0).astype(bf16)
        d_s[k, held, :] = chosen
        here = slice(k * CAP, (k + 1) * CAP)
        x_s[here, :] = dot_nn(chosen, block_value(pieces, blocks, k)).astype(bf16)
        upstream = dot_nn(chosen, told[absolute(k)])
        own_gate = jnp.sum(jnp.where(hit, gate, 0.0), axis=1, keepdims=True)
        gates.append(own_gate)
        c_s[here, :] = upstream.astype(bf16)
        ge_s[here, :] = (own_gate * (res_scale * upstream)).astype(bf16)

    for j in range(FF // TILE):
        left, right = slice(j * TILE, (j + 1) * TILE), slice(FF + j * TILE, FF + (j + 1) * TILE)
        gate_part = dot_nn(x_s[...], up_columns(left))
        up_part = dot_nn(x_s[...], up_columns(right))
        hidden_grad = dot_nt(ge_s[...], down_tile(j))
        sigmoid_gate = jax.nn.sigmoid(gate_part)
        swish = gate_part * sigmoid_gate
        a_s[:, left] = (swish * up_part).astype(bf16)
        slope = sigmoid_gate * (1.0 + gate_part * (1.0 - sigmoid_gate))
        gu_s[:, left] = (hidden_grad * up_part * slope).astype(bf16)
        gu_s[:, right] = (hidden_grad * swish).astype(bf16)

    gate_grad = jnp.zeros((slots, 1), f32)
    for j in range(MODEL_WIDTH // TILE):
        columns = slice(j * TILE, (j + 1) * TILE)
        produced = dot_nn(a_s[...], down_columns(columns)).astype(bf16).astype(f32)
        gate_grad += jnp.sum(res_scale * c_s[:, columns].astype(f32) * produced, axis=1, keepdims=True)
        input_grad = dot_nt(gu_s[...], up_tile(j)).astype(bf16)
        for k in range(count):
            here = slice(k * CAP, (k + 1) * CAP)
            eg_s[k, held, columns] = (gates[k] * produced[here]).astype(bf16)
            gs_s[k, held, columns] = input_grad[here]
    for k in range(count):
        hit = wanted == rank_s[k, pl.ds(expert, 1), :]
        spread = jnp.where(hit, gate_grad[k * CAP : (k + 1) * CAP], 0.0)
        gg_s[k, pl.ds(expert, 1), :] = jnp.sum(spread, axis=0, keepdims=True)

    for j in range(FF // TILE):
        rows = slice(j * TILE, (j + 1) * TILE)
        tile = dot_tn(a_s[:, rows], ge_s[...]).astype(bf16)
        if last:
            gdown_s[rows, :] = tile
        else:
            here = slice(j * TILE // down_rows, (j + 1) * TILE // down_rows)
            keep_ref[here, 0, up_rows:, :] = tile.reshape(TILE // down_rows, down_rows, MODEL_WIDTH)
    for j in range(MODEL_WIDTH // TILE):
        rows = slice(j * TILE, (j + 1) * TILE)
        tile = dot_tn(x_s[:, rows], gu_s[...]).astype(bf16)
        if last:
            gup_s[rows, :] = tile
        else:
            here = slice(j * TILE // up_rows, (j + 1) * TILE // up_rows)
            keep_ref[here, 0, :up_rows, :] = tile.reshape(TILE // up_rows, up_rows, 2 * FF)
    if last:
        for r in range(shards):
            ref = send_ref if r % 2 else keep_ref
            ref[r // 2, 0, :up_rows, :] = gup_s[aligned(meta[r] * up_rows, up_rows), :]
            ref[r // 2, 0, up_rows:, :] = gdown_s[aligned(meta[r] * down_rows, down_rows), :]

    @pl.when(step == members - 1)
    def combine():
        for k in range(count):
            spread = d_s[k]
            mixed = dot_tn(spread, eg_s[k])
            summed = dot_tn(spread, gs_s[k])
            exact = gg_s[k]
            rounded = exact.astype(bf16).astype(f32)
            rest = jnp.zeros((LANES - 2 * EXPERTS, TILE), f32)
            tail = jnp.concatenate([rounded, exact - rounded, rest], axis=0).T
            if start > 0:
                mixed += part_m[k].astype(f32)
                summed += part_g[k, :, :MODEL_WIDTH].astype(f32)
                tail += part_g[k, :, MODEL_WIDTH:].astype(f32)
            if last:
                ring_put(count, mix_refs, k, TILE, mixed)
                ring_put(count, ring_refs, k, TILE, summed)
                ring_put_tail(count, ring_refs, k, TILE, tail)
            else:
                mix_refs[0][k] = mixed.astype(bf16)
                ring_refs[0][k, :, :MODEL_WIDTH] = summed.astype(bf16)
                ring_refs[0][k, :, MODEL_WIDTH:] = tail.astype(bf16)


def backward_body(count, pieces, summed, meta, routes_ref, normed_ref, extra_ref, h_ref, c_ref, a_ref, wo_ref, q_ref, lse_ref, *refs):
    sums = refs[:summed]
    blocks = refs[summed : summed + len(pieces)]
    cos_ref, sin_ref, *outs = refs[summed + len(pieces) :]
    gh_ref, go_ref, gpq_ref, gex_ref, gain_ref = outs[:5]
    ring_refs, ga_s = outs[5:-1], outs[-1]
    rows = q_ref.shape[0]
    place = meta[0]
    normed = normed_ref[...]
    total = ring_total(sums)
    normed_grad, tail = total[:, :MODEL_WIDTH], total[:, MODEL_WIDTH:]
    names = lanes_of((rows, LANES))
    named = routes_ref[...]
    picked = names == named[:, 0:1]
    for j in range(1, TOP):
        picked = jnp.logical_or(picked, names == named[:, j : j + 1])
    row_names = lax.broadcasted_iota(jnp.int32, (LANES, MODEL_WIDTH), 0)
    router = jnp.where(row_names < EXPERTS, extra_ref[...], 0.0).astype(bf16)
    gate = softmax_over(picked, dot_nt(normed, router), 1)
    gate_grad = jnp.where(picked, tail + pltpu.roll(tail, LANES - EXPERTS, 1), 0.0)
    inner = jnp.sum(gate * gate_grad, axis=1, keepdims=True)
    logit_grad = (gate * (gate_grad - inner)).astype(bf16)
    gex_ref[...] = dot_tn(normed, logit_grad)
    normed_grad += dot_nn(logit_grad, router)
    resid = h_ref[...]
    scale_inv = lax.rsqrt(jnp.mean(resid * resid, axis=-1, keepdims=True) + epsilon)
    hat = resid * scale_inv
    gain_ref[...] = jnp.broadcast_to(jnp.sum(normed_grad * hat, axis=0, keepdims=True), gain_ref.shape)
    scaled = normed_grad * extra_ref[EXPERTS + 1 : EXPERTS + 2, :]
    part = scale_inv * (scaled - hat * jnp.mean(scaled * hat, axis=-1, keepdims=True))
    resid_grad = c_ref[...].astype(f32) + part
    gh_ref[...] = resid_grad
    go = (res_scale * resid_grad).astype(bf16)
    go_ref[...] = go
    ga_s[...] = dot_nt(go, wo_ref[...]).astype(bf16)
    cosine, sine = cos_ref[0], sin_ref[0]
    low = lanes_of((rows, LANES)) < HEAD_SIZE

    def variant(seen):
        def group(g, carry):
            lanes = aligned(g * LANES, LANES)
            pair = query_pair(q_ref[:, lanes])
            upstream = ga_s[:, lanes].astype(f32)
            product = (upstream * a_ref[:, lanes].astype(f32)).T
            delta = jnp.concatenate(
                [
                    jnp.sum(product[:HEAD_SIZE], axis=0, keepdims=True),
                    jnp.sum(product[HEAD_SIZE:], axis=0, keepdims=True),
                ],
                axis=1,
            )
            logsum = lse_ref[pl.ds(g, 1), :]
            high_pair = jnp.concatenate(
                [jnp.where(low, 0.0, pltpu.roll(upstream, HEAD_SIZE, 1)), jnp.where(low, 0.0, upstream)], axis=0
            ).astype(bf16)
            query_grad = jnp.zeros((LANES, 2 * rows), f32)
            for k in range(seen):
                keys = block_lanes(pieces, blocks, k, lanes)
                weights = jnp.exp(causal_scores(keys, pair, k) - logsum)
                score_grad = (weights * (dot_nt(keys, high_pair) - delta)).astype(bf16)
                query_grad += dot_tn(keys, score_grad)
                back = dot_nn(score_grad, pair) + dot_nn(weights.astype(bf16), high_pair)
                put_lanes(k, lanes, back)
            query_grad = query_grad[:HEAD_SIZE] * att_scale
            tile = jnp.concatenate([query_grad[:, :rows], query_grad[:, rows:]], axis=0).T
            tile = tile.astype(bf16).astype(f32)
            gpq_ref[:, lanes] = rotate_tile_back(tile, cosine, sine).astype(bf16)
            return carry

        lax.fori_loop(0, KEY_VALUE_HEADS, group, 0)
        for k in range(seen, count):
            ring_put(count, ring_refs, k, rows, jnp.zeros((rows, MODEL_WIDTH), f32))

    def put_lanes(k, lanes, value):
        views = [r.at[..., lanes] for r in ring_refs]
        ring_put(count, views, k, rows, value)

    for seen in range(1, count + 1):
        pl.when(place == seen - 1)(functools.partial(variant, seen))


def store_sets(shards, meta, source, sets, columns):
    rows = MODEL_WIDTH // shards
    for r in range(shards):
        sets[r % 2][r // 2, :, columns] = source[aligned(meta[r] * rows, rows), :].astype(bf16)


def weights_body(count, shards, pieces, meta, a_ref, go_ref, gpq_ref, gex_ref, gain_ref, cos_ref, sin_ref, *refs):
    blocks, parts = refs[: len(pieces)], refs[len(pieces) : -6]
    *sets, gp_s, normed_s, full_s, extra_s = refs[-6:]
    rows = gpq_ref.shape[0]
    low = lanes_of((rows, LANES)) < HEAD_SIZE
    for k in range(count):
        here = slice(k * rows, (k + 1) * rows)
        normed_s[here, :] = block_value(pieces, blocks, k)
        cosine, sine = cos_ref[k], sin_ref[k]
        part = ring_get(count, parts, k, rows).astype(f32)
        for j in range(MODEL_WIDTH // LANES):
            lanes = slice(j * LANES, (j + 1) * LANES)
            tile = part[:, lanes]
            gp_s[here, lanes] = jnp.where(low, rotate_tile_back(tile, cosine, sine), tile).astype(bf16)
    full_s[...] = dot_tn(normed_s[:rows, :], gpq_ref[...]).astype(bf16)
    store_sets(shards, meta, full_s, sets, slice(0, MODEL_WIDTH))
    full_s[...] = dot_tn(normed_s[...], gp_s[...]).astype(bf16)
    store_sets(shards, meta, full_s, sets, slice(MODEL_WIDTH, 2 * MODEL_WIDTH))
    full_s[...] = dot_tn(a_ref[...], go_ref[...]).astype(bf16)
    store_sets(shards, meta, full_s, sets, slice(2 * MODEL_WIDTH, 3 * MODEL_WIDTH))
    row_names = lax.broadcasted_iota(jnp.int32, (LANES, MODEL_WIDTH), 0)
    gains = jnp.where(row_names == EXPERTS + 1, gain_ref[0:1, :], 0.0)
    extra_s[...] = gex_ref[...] + gains.T
    store_sets(shards, meta, extra_s, sets, slice(3 * MODEL_WIDTH, 3 * MODEL_WIDTH + LANES))


def tokens_body(meta, x_ref, gpq_ref, wq_ref, wkv_ref, extra_ref, gh_ref, *refs):
    *sums, cos_ref, sin_ref, grad_ref, gpkv_s = refs
    total = ring_total(sums).astype(bf16).astype(f32)
    cosine, sine = cos_ref[0], sin_ref[0]
    low = lanes_of(cosine.shape) < HEAD_SIZE
    for j in range(MODEL_WIDTH // LANES):
        lanes = slice(j * LANES, (j + 1) * LANES)
        tile = total[:, lanes]
        gpkv_s[:, lanes] = jnp.where(low, rotate_tile_back(tile, cosine, sine), tile).astype(bf16)
    normed_grad = dot_nt(gpq_ref[...], wq_ref[...]) + dot_nt(gpkv_s[...], wkv_ref[...])
    source = x_ref[...].astype(f32)
    scale_inv = lax.rsqrt(jnp.mean(source * source, axis=-1, keepdims=True) + epsilon)
    hat = source * scale_inv
    scaled = normed_grad * extra_ref[EXPERTS : EXPERTS + 1, :]
    part = scale_inv * (scaled - hat * jnp.mean(scaled * hat, axis=-1, keepdims=True))
    grad_ref[...] = gh_ref[...] + part


def dense_update_body(count, rates, meta, need, send, *refs):
    quarters, refs = refs[:count], refs[count:]
    ins, outs, total_s = refs[:12], refs[12:28], refs[28]
    rows = quarters[0].shape[0]

    def update(i, gradient):
        weight, first, second = [r[...] for r in ins[3 * i : 3 * i + 3]]
        values = (gradient, *adam_update(weight, gradient, first, second, rates[i]))
        for at, (ref, value) in enumerate(zip(outs[4 * i : 4 * i + 4], values)):
            ref[...] = value
            send(ref, 4 * i + at)

    need(*quarters)
    for k in range(count):
        at = pl.ds(pl.multiple_of(lax.rem(meta[0] - k + count, count) * rows, rows), rows)
        total_s[at, :] = quarters[k][...].astype(f32)
    need(*ins[3:6])
    qkv = total_s[:, : 2 * MODEL_WIDTH]
    update(1, qkv)
    product = jnp.sum(qkv * ins[3][...].astype(bf16).astype(f32), axis=1, keepdims=True)
    need(*ins[6:9])
    update(2, total_s[:, 2 * MODEL_WIDTH : 3 * MODEL_WIDTH])
    need(*ins[:3], *ins[9:])
    rest = total_s[:, 3 * MODEL_WIDTH :].T
    first = jnp.broadcast_to(product, (product.shape[0], LANES)).T[0:1] / ins[0][0:1, :].astype(bf16).astype(f32)
    update(0, jnp.concatenate([first, rest[EXPERTS + 1 : EXPERTS + 2]], axis=0))
    update(3, rest[:EXPERTS])


def output_body(meta, h_ref, *refs):
    refs[-1][...] = (h_ref[...] + res_scale * ring_total(refs[:-1])).astype(bf16)


def experts_update_body(rates, rows, parts, rows_of, meta, *refs):
    gradient = rows_of(refs[:parts])
    ins, outs = refs[parts : parts + 6], refs[-8:]
    for i, rate in enumerate(rates):
        own = gradient[: rows[0]] if i == 0 else gradient[rows[0] :]
        weight, first, second = [r[0] for r in ins[3 * i : 3 * i + 3]]
        fresh, first, second = adam_update(weight, own, first, second, rate)
        for ref, value in zip(outs[4 * i : 4 * i + 4], (own, fresh, first, second)):
            ref[0] = value


def experts_update(start, share, arrays, rates, earlier, scalars, after=()):
    shares, share_specs, rows_of = share
    members = shares[0].shape[-3]
    rows = (arrays[0].shape[1], arrays[3].shape[1])

    def spec(a):
        return pl.BlockSpec((1,) + a.shape[1:], lambda e, m: (start + e, 0, 0))

    outs = [shape_of(a.shape, f32) for a in (arrays[0],) * 4 + (arrays[3],) * 4]
    in_specs = share_specs + [spec(a) for a in arrays]
    ins = shares + list(arrays)
    aliases = {}
    if earlier is not None:
        aliases = {1 + len(after) + len(ins) + i: i for i in range(8)}
        in_specs += [pl.BlockSpec(memory_space=pl.ANY)] * 8
        ins += list(earlier)
    return kernel_call(
        functools.partial(experts_update_body, rates, rows, len(shares), rows_of),
        outs,
        ins,
        scalars,
        grid=(members,),
        in_specs=in_specs,
        out_specs=[spec(a) for a in outs],
        limit=60, micros=8,
        after=after,
        aliases=aliases,
    )


def angle_tables(rows, offsets):
    position = (offsets[:, None] + jnp.arange(rows)[None, :]).reshape(-1).astype(f32)
    frequency = 10000.0 ** (-(jnp.arange(HEAD_SIZE // 2).astype(f32) * 2.0 / HEAD_SIZE))
    angles = position[:, None] * frequency[None, :]
    cosine, sine = jnp.cos(angles), jnp.sin(angles)
    shape = (offsets.shape[0], rows, LANES)
    cosine = jnp.concatenate([cosine] * 4, axis=1).reshape(shape)
    return (cosine, jnp.concatenate([-sine, sine] * 2, axis=1).reshape(shape))


def shards_step(
    tokens,
    routes,
    cotangent,
    norm_gains,
    qkv_weight,
    out_weight,
    router_weight,
    expert_up,
    expert_down,
    mean_gains,
    square_gains,
    mean_qkv,
    square_qkv,
    mean_out,
    square_out,
    mean_router,
    square_router,
    mean_up,
    square_up,
    mean_down,
    square_down,
):
    rows = tokens.shape[1]
    count = lax.axis_size("seq")
    shards = lax.axis_size("fsdp")
    shard_rows = MODEL_WIDTH // shards
    local = EXPERTS // count
    early_experts = 3 * local // 4
    chunks = [(0, early_experts), (early_experts, local - early_experts)]
    place = lax.axis_index("seq").astype(jnp.int32)
    owners = (lax.axis_index("fsdp") ^ jnp.arange(shards)).astype(jnp.int32)
    owner_meta = jnp.concatenate([owners, place[None]])
    place_meta = place[None]
    x, c, own_routes = tokens[0], cotangent[0], routes[0]

    def dense_part(piece):
        blank = jnp.zeros((shard_rows // 2, LANES - EXPERTS - 2), f32)
        parts = [qkv_weight[piece], out_weight[piece], router_weight[piece], norm_gains[:, piece].T, blank]
        return jnp.concatenate(parts, axis=1).astype(bf16)

    dense_shards = Gathered(dense_part(slice(0, shard_rows // 2)), dense_part(slice(shard_rows // 2, shard_rows)))
    told = lax.all_gather(c, "seq", axis=0)
    listed = jnp.concatenate([own_routes.T, jnp.zeros_like(own_routes.T)], axis=0).astype(f32).astype(bf16)
    routes_by_block = [listed]
    for k in range(1, count):
        routes_by_block.append(shift_permute(listed, "seq", k))
    cosines, sines = angle_tables(rows, jnp.maximum(place - jnp.arange(count), 0) * rows)
    dense_shards.forward(cosines, sines, *routes_by_block[1:])
    early = dense_shards.arrived()
    dense_pieces = dense_shards.pieces()
    expert_weights = []
    for start, members in chunks:
        mine = slice(start, start + members)
        packed = jnp.concatenate([expert_up[mine], expert_down[mine]], axis=1).astype(bf16)
        expert_weights.append(lax.all_gather(tie(packed, *early), "fsdp", axis=0))

    square = shape_of((MODEL_WIDTH, MODEL_WIDTH))
    wide = shape_of((rows, MODEL_WIDTH))
    wide_f = shape_of((rows, MODEL_WIDTH), f32)
    extra_shape = shape_of((LANES, MODEL_WIDTH), f32)
    unit = 2 * rows * MODEL_WIDTH * MODEL_WIDTH
    wq, wkv, wo, extra, normed_one, q, kv = kernel_call(
        functools.partial(qkv_body, dense_pieces),
        [square, square, square, extra_shape, wide, wide, wide],
        [x] + [a for _, _, a in dense_pieces],
        owner_meta,
        tables=(cosines, sines),
        scratch=[pltpu.VMEM((MODEL_WIDTH, LANES), f32)],
        limit=60, micros=8,
    )
    kv_pieces = ring_gather(kv)
    attended, logsum, resid, normed_two = kernel_call(
        functools.partial(attend_body, count, kv_pieces),
        [wide, shape_of((KEY_VALUE_HEADS, 2 * rows), f32), wide_f, wide],
        [q, x, wo, extra] + [a for _, _, a in kv_pieces],
        place_meta,
        limit=60, micros=12,
    )
    two_pieces = ring_gather(normed_two)

    slots = count * CAP
    packed_rows = (MODEL_WIDTH + FF) // shards
    part_g = part_m = None
    waited = (cosines, sines)
    normed_block = tie(normed_one, *[a for _, _, a in two_pieces[1:]])
    normed_blocks = tuple(shift_permute(normed_block, "seq", k) for k in range(1, count))
    normed_pieces = [(k, 0, a) for k, a in enumerate((normed_one,) + normed_blocks)]
    for i, (start, members) in enumerate(chunks):
        last = i == len(chunks) - 1
        ins = [extra, expert_weights[i], expert_weights[i]] + [a for _, _, a in two_pieces] + [told] + routes_by_block

        def still(a):
            return pl.BlockSpec(a.shape, functools.partial(lambda n, e, m: (0,) * n, a.ndim), pipeline_mode=pl.Buffered(1))

        all_spec = pl.BlockSpec((shards, 1, packed_rows, MODEL_WIDTH), lambda e, m: (0, e, 0, 0))
        set_spec = pl.BlockSpec((shards // 2, 1, packed_rows, MODEL_WIDTH), lambda e, m: (0, e, 0, 0))
        sets = [shape_of((shards // 2, members, packed_rows, MODEL_WIDTH))] * 2
        set_specs = [set_spec] * 2
        if not last:
            sets, set_specs = [shape_of((shards, members, packed_rows, MODEL_WIDTH))], [all_spec]
        up_spec = pl.BlockSpec((shards, 1, shard_rows, MODEL_WIDTH), lambda e, m: (0, e, 0, 0))
        place_down = MODEL_WIDTH // FF
        down_spec = pl.BlockSpec((shards, 1, FF // shards, MODEL_WIDTH), lambda e, m: (0, e, place_down, 0))
        in_specs = [still(extra), up_spec, down_spec] + [still(a) for a in ins[3:]]
        if i > 0:
            ins += [part_g, part_m]
            in_specs += [still(part_g), still(part_m)]
        ring = ring_shapes if last else lambda n, r, w: [shape_of((n, r, w))]
        ring_count = len(ring(count, rows, WIDE))
        outs = sets + ring(count, rows, MODEL_WIDTH) + ring(count, rows, WIDE)
        out_specs = set_specs + [still(a) for a in outs[len(sets) :]]
        scratch = [
            pltpu.VMEM((slots, MODEL_WIDTH), bf16),
            pltpu.VMEM((slots, MODEL_WIDTH), bf16),
            pltpu.VMEM((slots, MODEL_WIDTH), bf16),
            pltpu.VMEM((slots, FF), bf16),
            pltpu.VMEM((slots, 2 * FF), bf16),
            pltpu.VMEM((count, members * CAP, rows), bf16),
            pltpu.VMEM((count, members * CAP, MODEL_WIDTH), bf16),
            pltpu.VMEM((count, members * CAP, MODEL_WIDTH), bf16),
            pltpu.VMEM((MODEL_WIDTH, 2 * FF), bf16),
            pltpu.VMEM((FF, MODEL_WIDTH), bf16),
            pltpu.VMEM((count, EXPERTS, rows), f32),
            pltpu.VMEM((count, EXPERTS, rows), f32),
            pltpu.VMEM((count, EXPERTS, rows), f32),
        ]
        results = kernel_call(
            functools.partial(experts_body, count, shards, two_pieces, start, members, last),
            outs,
            ins,
            owner_meta,
            scratch=scratch,
            grid=(members,),
            in_specs=in_specs,
            out_specs=out_specs,
            micros=8 * members,
            after=waited,
        )
        results = list(results)
        first_part = len(sets)
        part_m, part_g = results[first_part], results[first_part + ring_count]
        mix_parts, ring_parts = results[first_part : first_part + ring_count], results[first_part + ring_count :]
        if not last:
            share = tie(results[0], *normed_blocks)
            share = lax.psum_scatter(share, "fsdp", scatter_dimension=0)

    two_ring = RingSum(ring_parts)
    late_sum = ScatteredExperts(tie(results[1], *two_ring.near()), results[0], place_meta)
    two_sums = two_ring.parts()
    sent = late_sum.first(*two_ring.sent)
    mixing = RingSum(mix_parts, *two_sums[3:], *sent)
    ring = ring_shapes(count, rows, MODEL_WIDTH)
    results = kernel_call(
        functools.partial(backward_body, count, kv_pieces, len(two_sums)),
        [wide_f, wide, wide, shape_of((MODEL_WIDTH, LANES), f32), shape_of((8, MODEL_WIDTH), f32)] + ring,
        [own_routes, normed_two, extra, resid, c, attended, wo, q, logsum]
        + list(two_sums)
        + [a for _, _, a in kv_pieces],
        place_meta,
        tables=(cosines, sines),
        scratch=[pltpu.VMEM((rows, MODEL_WIDTH), bf16)],
        limit=60, micros=22,
    )
    resid_grad, go, gpq, router_grad, gain_grad = results[:5]
    mix_sums = mixing.parts()
    dense_set = shape_of((shards // 2, shard_rows, 3 * MODEL_WIDTH + LANES))
    keep, send = kernel_call(
        functools.partial(weights_body, count, shards, normed_pieces),
        [dense_set] * 2,
        [attended, go, gpq, router_grad, gain_grad, cosines, sines]
        + [a for _, _, a in normed_pieces]
        + list(results[5:]),
        owner_meta,
        scratch=[
            pltpu.VMEM((count * rows, MODEL_WIDTH), bf16),
            pltpu.VMEM((count * rows, MODEL_WIDTH), bf16),
            pltpu.VMEM((MODEL_WIDTH, MODEL_WIDTH), bf16),
            pltpu.VMEM((MODEL_WIDTH, LANES), f32),
        ],
        after=mixing.near(),
        limit=60, micros=12,
    )
    dense_sum = Scattered(place_meta)
    dense_sum.add(send, keep, *mix_sums[3:])
    rates = (learn_rates[4], learn_rates[5])
    experts = (expert_up, mean_up, square_up, expert_down, mean_down, square_down)
    sent = dense_sum.first()
    kv_ring = RingSum(results[5:], *mix_sums[3:])
    spec = pl.BlockSpec((1,) + share.shape[1:], lambda e, m: (e, 0, 0))
    total = ([share], [spec], lambda refs: refs[0][0].astype(f32))
    updated = experts_update(chunks[0][0], total, experts, rates, None, place_meta, sent)
    kv_sums = kv_ring.parts(*dense_sum.second(updated[0]))
    own = dense_sum.total(count, *kv_ring.sent)
    late_sum.depart(own)
    quarters = lax.all_to_all(own, "seq", split_axis=0, concat_axis=0, tiled=True)
    (tokens_grad,) = kernel_call(
        tokens_body,
        [wide_f],
        [x, gpq, wq, wkv, extra, resid_grad] + list(kv_sums),
        place_meta,
        tables=(cosines, sines),
        scratch=[pltpu.VMEM((rows, MODEL_WIDTH), bf16)],
        after=(own,),
        limit=60, micros=6,
    )
    quarter = jnp.sum(tie(quarters, tokens_grad, *late_sum.second(tokens_grad)).astype(f32), axis=0).astype(bf16)
    (output,) = kernel_call(output_body, [wide], [resid] + mix_sums, place_meta, after=(quarter,), micros=3)
    tokens_grad, output = tokens_grad[None], output[None]
    quarters = [quarter] + [shift_permute(quarter, "seq", k) for k in range(1, count)]
    updated = experts_update(chunks[1][0], late_sum.total(), experts, rates, updated, place_meta, (quarter,))
    dense_ins = [norm_gains, mean_gains, square_gains, qkv_weight, mean_qkv, square_qkv]
    dense_ins += [out_weight, mean_out, square_out, router_weight.T, mean_router.T, square_router.T]
    dense_shapes = [shape_of(a.shape, f32) for a in dense_ins[::3] for _ in range(4)]
    dense_outs = streamed_call(
        functools.partial(dense_update_body, count, learn_rates[:4]),
        dense_shapes,
        quarters + dense_ins,
        place_meta,
        scratch=[pltpu.VMEM(a.shape, f32) for a in dense_shapes]
        + [pltpu.VMEM((shard_rows, 3 * MODEL_WIDTH + LANES), f32)],
        after=(updated[0],),
        micros=5,
    )
    shard_gains, fresh_gains, momentum_gains, variance_gains = dense_outs[:4]
    shard_qkv, fresh_qkv, momentum_qkv, variance_qkv = dense_outs[4:8]
    shard_out, fresh_out, momentum_out, variance_out = dense_outs[8:12]
    shard_router, fresh_router, momentum_router, variance_router = [a.T for a in dense_outs[12:]]
    shard_up, fresh_up, momentum_up, variance_up = updated[:4]
    shard_down, fresh_down, momentum_down, variance_down = updated[4:]
    return (
        output,
        tokens_grad,
        shard_gains,
        shard_qkv,
        shard_out,
        shard_router,
        shard_up,
        shard_down,
        fresh_gains,
        fresh_qkv,
        fresh_out,
        fresh_router,
        fresh_up,
        fresh_down,
        momentum_gains,
        momentum_qkv,
        momentum_out,
        momentum_router,
        momentum_up,
        momentum_down,
        variance_gains,
        variance_qkv,
        variance_out,
        variance_router,
        variance_up,
        variance_down,
    )


def solution(mesh):
    block = P("fsdp", "seq", None)
    gains, dense, experts = P(None, "fsdp"), P("fsdp", None), P("seq", "fsdp", None)
    weights = (gains, dense, dense, dense, experts, experts)
    moments = tuple(s for spec in weights for s in (spec, spec))
    return jax.shard_map(
        shards_step,
        mesh=mesh,
        in_specs=(block, block, block) + weights + moments,
        out_specs=(block, block) + weights * 4,
        check_vma=False,
    )
```
